32 devices in a mesh: seq: 8 (over z, x), dp: 4 (over y, core).
Axes of the slice: x: 2, y: 2, z: 4, core: 2. Of those that a mesh axis runs over, the one named last changes fastest.
Arguments:
- frames_in: bfloat16 [32, 512, 1024], P('dp', 'seq'), parts along dimension 0, may hold values from -6 to 6
- noise: bfloat16 [32, 512, 1024], P('dp', 'seq'), parts along dimension 0, may hold values from -6 to 6
- lengths: int32 [32], P('dp'), parts along dimension 0, may hold values from 128 to 512, as said below
- span_starts: int32 [32, 16], P('dp'), parts along dimension 0, may hold values from 0 to 502
- w_in1: bfloat16 [1024, 4096], P('seq'), may hold values from -0.1875 to 0.1875
- w_out1: bfloat16 [4096, 1024], P('seq'), may hold values from -0.09375 to 0.09375
- w_qkv: bfloat16 [1024, 3072], P('seq'), may hold values from -0.1875 to 0.1875
- w_attn: bfloat16 [1024, 1024], P('seq'), may hold values from -0.75 to 0.75
- w_point1: bfloat16 [1024, 2048], P('seq'), may hold values from -0.1875 to 0.1875
- w_point2: bfloat16 [1024, 1024], P('seq'), may hold values from -0.5 to 0.5
- w_in2: bfloat16 [1024, 4096], P('seq'), may hold values from -0.1875 to 0.1875
- w_out2: bfloat16 [4096, 1024], P('seq'), may hold values from -0.09375 to 0.09375
- norm_params: float32 [6, 2, 1024], replicated
- kernel: float32 [5, 1024], replicated, may hold values from -2.5 to 2.5
- slopes: float32 [8], replicated, may hold values from 0.3 to 3
- cotangent: bfloat16 [32, 512, 1024], P('dp', 'seq'), parts along dimension 0, may hold values from -6 to 6
Outputs:
- block_out: bfloat16 [32, 512, 1024], P('dp', 'seq'), parts along dimension 0
- grad_frames: float32 [32, 512, 1024], P('dp', 'seq'), parts along dimension 0
- grad_in1: float32 [4096, 4096], P(('dp', 'seq')), parts along dimension 0
- grad_out1: float32 [16384, 1024], P(('dp', 'seq')), parts along dimension 0
- grad_qkv: float32 [4096, 3072], P(('dp', 'seq')), parts along dimension 0
- grad_attn: float32 [4096, 1024], P(('dp', 'seq')), parts along dimension 0
- grad_point1: float32 [4096, 2048], P(('dp', 'seq')), parts along dimension 0
- grad_point2: float32 [4096, 1024], P(('dp', 'seq')), parts along dimension 0
- grad_in2: float32 [4096, 4096], P(('dp', 'seq')), parts along dimension 0
- grad_out2: float32 [16384, 1024], P(('dp', 'seq')), parts along dimension 0
- grad_norms: float32 [24, 2, 1024], P('dp'), parts along dimension 0
- grad_kernel: float32 [20, 1024], P('dp'), parts along dimension 0
- grad_slopes: float32 [32], P('dp'), parts along dimension 0
The draws below stay inside these ranges and needn't reach their ends.
There are 4 independent parts, one for each index of `dp`. The reference program is written for one: setup_inputs(seed, part) draws one part's arguments, and reference() takes and returns one part's arrays. A program takes and returns all parts, laid end to end along the dimension named above; an argument that names none is the same for every part. Nothing has to cross between parts.
Inputs may be any that keep to these rules, and one draw needn't show every extreme that they name: `lengths`: every utterance keeps at least 128 frames, and one utterance of each group keeps all 512. `span_starts`: each span covers 10 frames from its start; spans may intersect.
All inputs are finite; a program needn't handle non-finite values.
Results may differ from the reference program's by a relative error of at most 0.034.
Values may be sent and summed in bfloat16 or wider, within the bound.
A program may use at most 512 MiB of HBM per device.

```python
import math
import jax
import jax.numpy as jnp
from jax import lax

D = 1024
FF = 4096
HEADS = 8
HEAD_DIM = 128
TAPS = 5
SPAN = 10
NORMS = 6
UTTS = 8
LEN = 512
NSPAN = 16


def draw_lengths(key, part):
    key = jax.random.fold_in(key, 11)
    first_key, second_key = jax.random.split(key)
    spread = jax.random.randint(first_key, (UTTS,), LEN // 4, LEN + 1)
    chosen = jax.random.randint(second_key, (), 0, UTTS)
    return jnp.where(jnp.arange(UTTS) == chosen, LEN, spread).astype(jnp.int32)


def draw_norm_params(key, part):
    key = jax.random.fold_in(key, 23)
    first_key, second_key = jax.random.split(key)
    gain_part = 1.0 + 0.2 * jnp.clip(jax.random.normal(first_key, (NORMS, 1, D), jnp.float32), -2.0, 2.0)
    shift_part = 0.3 * jax.random.normal(second_key, (NORMS, 1, D), jnp.float32)
    return jnp.concatenate([gain_part, shift_part], axis=1)


def place_ends(drawn, rng, low, largest):
    longest = drawn.shape.index(max(drawn.shape))
    spots = []
    for shift in (0, 1):
        where = [jax.random.randint(jax.random.fold_in(rng, axis), (), 0, length) for axis, length in enumerate(drawn.shape)]
        where[longest] = (where[longest] + shift) % drawn.shape[longest]
        spots.append(tuple(where))
    return drawn.at[spots[0]].set(low).at[spots[1]].set(largest)


def block_levels(own_key, extent, cuts, least, high):
    def one(dim, blocks):
        heights = jax.random.uniform(jax.random.fold_in(jax.random.fold_in(own_key, 6), dim), (blocks,), jnp.float32, least / len(cuts), high / len(cuts))
        return jnp.repeat(jnp.exp(heights), extent[dim] // blocks).reshape((-1,) + (1,) * (len(extent) - dim - 1))

    gain = one(*cuts[0])
    for cut in cuts[1:]:
        gain = gain * one(*cut)
    return gain


def bell_draw(rng, extent, deviation, reach, cuts=(), kind=jnp.bfloat16):
    values = jax.random.normal(rng, extent, jnp.float32) * deviation
    if len(cuts) > 0:
        values = block_levels(rng, extent, cuts, -0.22, 0.18) * values
    return jnp.clip(values, min=-reach, max=reach).astype(kind)


def setup_inputs(seed: int = 0, part: int = 0) -> dict:
    seeds = jax.random.split(jax.random.key(seed), 17)
    part_splits = jax.random.split(jax.random.fold_in(seeds[16], part), 17)
    return {
        "frames_in": bell_draw(part_splits[0], (UTTS, LEN, D), 1.0, 6.0, ((1, 8),)),
        "noise": bell_draw(part_splits[1], (UTTS, LEN, D), 1.0, 6.0, ((1, 8),)),
        "lengths": draw_lengths(jax.random.fold_in(jax.random.fold_in(seeds[16], part), 71), part),
        "span_starts": place_ends(jax.random.randint(part_splits[3], (UTTS, NSPAN), 0, LEN - SPAN + 1), jax.random.fold_in(part_splits[3], 1), 0, LEN - SPAN).astype(jnp.int32),
        "w_in1": bell_draw(seeds[4], (D, FF), D ** -0.5, 0.1875, ((0, 8),)),
        "w_out1": bell_draw(seeds[5], (FF, D), FF ** -0.5, 0.09375, ((0, 8),)),
        "w_qkv": bell_draw(seeds[6], (D, 3 * D), D ** -0.5, 0.1875, ((0, 8),)),
        "w_attn": bell_draw(seeds[7], (D, D), (D // 16) ** -0.5, 0.75, ((0, 8),)),
        "w_point1": bell_draw(seeds[8], (D, 2 * D), D ** -0.5, 0.1875, ((0, 8),)),
        "w_point2": bell_draw(seeds[9], (D, D), (D // 8) ** -0.5, 0.5, ((0, 8),)),
        "w_in2": bell_draw(seeds[10], (D, FF), D ** -0.5, 0.1875, ((0, 8),)),
        "w_out2": bell_draw(seeds[11], (FF, D), FF ** -0.5, 0.09375, ((0, 8),)),
        "norm_params": draw_norm_params(jax.random.fold_in(seeds[16], 71), part),
        "kernel": bell_draw(seeds[13], (TAPS, D), TAPS ** -0.5, 2.5, (), jnp.float32),
        "slopes": jnp.clip(jnp.exp(jax.random.uniform(seeds[14], (HEADS,), jnp.float32, math.log(0.3), math.log(3.0))), 0.3, 3.0),
        "cotangent": bell_draw(part_splits[15], (UTTS, LEN, D), 1.0, 6.0, ((1, 8),)),
    }


@jax.custom_vjp
def low(v):
    return lax.optimization_barrier(v.astype(jnp.bfloat16)).astype(jnp.float32)

@jax.custom_vjp
def low_back(v):
    return v

def low_keep(v):
    return (low(v), None)

def low_pass(kept, grad):
    return (grad,)

def back_keep(v):
    return (v, None)

def back_low(kept, grad):
    return (low(grad),)
low.defvjp(low_keep, low_pass)
low_back.defvjp(back_keep, back_low)
EPSILON = 1e-05
NEGATIVE = -1e+30
HIGHEST = lax.Precision.HIGHEST

def layer_norm(inputs, gain_vec, shift_vec):
    average = lax.optimization_barrier(jnp.mean(inputs, axis=-1, keepdims=True))
    centred = inputs - average
    variance = lax.optimization_barrier(jnp.mean(centred * centred, axis=-1, keepdims=True))
    return centred * lax.rsqrt(variance + EPSILON) * gain_vec + shift_vec

def project(inputs, matrix):
    return low_back(jnp.einsum('...i,ij->...j', inputs, matrix, precision=HIGHEST))

def feed_forward(inputs, gain_vec, shift_vec, w_first, w_second):
    hidden = project(low(layer_norm(inputs, gain_vec, shift_vec)), w_first)
    return project(low(jax.nn.silu(hidden)), w_second)

def attention_block(query_blk, keys, values, query_pos, key_pos, key_live, slopes):
    scores = low_back(jnp.einsum('qhd,khd->hqk', query_blk, keys, precision=HIGHEST) * HEAD_DIM ** (-0.5))
    distance = jnp.abs(query_pos[:, None] - key_pos[None, :]).astype(jnp.float32) / LEN
    scores = scores - slopes[:, None, None] * distance[None]
    scores = jnp.where(key_live[None, None, :], scores, NEGATIVE)
    row_max = lax.optimization_barrier(jnp.max(scores, axis=-1, keepdims=True))
    expd = jnp.exp(scores - row_max)
    probab = low(expd / lax.optimization_barrier(jnp.sum(expd, axis=-1, keepdims=True)))
    return jnp.einsum('hqk,khd->qhd', probab, values, precision=HIGHEST)

def attend_all(queries, keys, values, lengths, slopes):
    block_rows = min(512, LEN)
    block_count = LEN // block_rows
    positions = jnp.arange(LEN, dtype=jnp.int32)
    checked = jax.checkpoint(attention_block)

    def per_utterance(bundle):
        utt_query, utt_key, utt_value, utt_length = bundle
        key_live = positions < utt_length
        query_blocks = utt_query.reshape(block_count, block_rows, HEADS, HEAD_DIM)
        pos_blocks = positions.reshape(block_count, block_rows)
        result = lax.map(lambda block_pair: checked(block_pair[0], utt_key, utt_value, block_pair[1], positions, key_live, slopes), (query_blocks, pos_blocks))
        return result.reshape(LEN, HEADS, HEAD_DIM)
    return lax.map(per_utterance, (queries, keys, values, lengths))

def reference(frames_in, noise, lengths, span_starts, w_in1, w_out1, w_qkv, w_attn, w_point1, w_point2, w_in2, w_out2, norm_params, kernel, slopes, cotangent):
    frame_pos = jnp.arange(LEN, dtype=jnp.int32)
    live_mask = frame_pos[None, :] < lengths[:, None]
    live_rows = live_mask.astype(jnp.float32)[..., None]
    span_begin = span_starts[:, :, None]
    masked = jnp.any((span_begin <= frame_pos[None, None, :]) & (frame_pos[None, None, :] < span_begin + SPAN), axis=1)
    start_in = jnp.where(masked[..., None], noise.astype(jnp.float32), frames_in.astype(jnp.float32))
    matrices = tuple((matrix.astype(jnp.float32) for matrix in (w_in1, w_out1, w_qkv, w_attn, w_point1, w_point2, w_in2, w_out2)))
    half_taps = TAPS // 2

    def forward(inputs, m_in1, m_out1, m_qkv, m_attn, m_point1, m_point2, m_in2, m_out2, norms, taps_vec, slope_vec):
        ffn_one = feed_forward(inputs, norms[0, 0], norms[0, 1], m_in1, m_out1)
        resid_one = inputs + 0.5 * ffn_one
        packed = low(project(low(layer_norm(resid_one, norms[1, 0], norms[1, 1])), m_qkv))
        packed = packed.reshape(UTTS, LEN, 3, HEADS, HEAD_DIM)
        heads_out = attend_all(packed[:, :, 0], packed[:, :, 1], packed[:, :, 2], lengths, slope_vec)
        heads_out = low(low_back(heads_out)).reshape(UTTS, LEN, D)
        attended = project(heads_out, m_attn)
        resid_two = resid_one + attended
        joined = project(low(layer_norm(resid_two, norms[2, 0], norms[2, 1])), m_point1)
        gated = low(joined[..., :D] * jax.nn.sigmoid(joined[..., D:]) * live_rows)
        padded = jnp.pad(gated, ((0, 0), (half_taps, half_taps), (0, 0)))
        depth = taps_vec[0] * padded[:, 0:LEN]
        for position in range(1, TAPS):
            depth = depth + taps_vec[position] * padded[:, position:position + LEN]
        depth = low_back(depth)
        activ = low(jax.nn.silu(layer_norm(depth, norms[3, 0], norms[3, 1])))
        convolved = project(activ, m_point2)
        resid_three = resid_two + convolved
        ffn_two = feed_forward(resid_three, norms[4, 0], norms[4, 1], m_in2, m_out2)
        resid_four = resid_three + 0.5 * ffn_two
        return layer_norm(resid_four, norms[5, 0], norms[5, 1])
    result, back_fn = jax.vjp(forward, start_in, *matrices, norm_params, kernel, slopes)
    grads = back_fn(cotangent.astype(jnp.float32))
    grad_frames = jnp.where(masked[..., None], 0.0, grads[0])
    return (result.astype(jnp.bfloat16), grad_frames, grads[1], grads[2], grads[3], grads[4], grads[5], grads[6], grads[7], grads[8], grads[9], grads[10], grads[11])
```

```python
import functools

import jax
import jax.numpy as jnp
from jax import lax
from jax.experimental import pallas as pl
from jax.experimental.pallas import tpu as pltpu
from jax.sharding import PartitionSpec as P

MESH = pl.DeviceIdType.MESH
BF16 = jnp.bfloat16
F32 = jnp.float32
ANY = pl.BlockSpec(memory_space=pl.ANY)

SPAN = 10


EPSILON = 1e-05
NEGATIVE = -1e30


def padded_2(shard, sides, width):
    for axis, dim in sides:
        peers, length = (lax.axis_size(axis), shard.shape[dim])
        up = [(i, (i + 1) % peers) for i in range(peers - 1)]
        down = [(j, i) for i, j in up]
        last = lax.slice_in_dim(shard, length - width, length, axis=dim)
        initial = lax.slice_in_dim(shard, 0, width, axis=dim)
        before = lax.ppermute(last, axis, up)
        after = lax.ppermute(initial, axis, down)
        shard = jnp.concatenate([before, shard, after], axis=dim)
    return shard


def layer_norm(inputs, gain_vec, shift_vec):
    average = jnp.mean(inputs, axis=-1, keepdims=True)
    centred = inputs - average
    variance = jnp.mean(centred * centred, axis=-1, keepdims=True)
    return centred * lax.rsqrt(variance + EPSILON) * gain_vec + shift_vec


def swish_norm(inputs, gain_vec, shift_vec):
    return jax.nn.silu(layer_norm(inputs, gain_vec, shift_vec))


def glu_gate(joined, live_rows):
    half_width = joined.shape[-1] // 2
    return joined[..., :half_width] * jax.nn.sigmoid(joined[..., half_width:]) * live_rows


def matmul(left_side, right_side):
    return jnp.dot(left_side, right_side, preferred_element_type=jnp.float32)


def matmul_right_t(left_side, right_side):
    return lax.dot_general(
        left_side, right_side, (((1,), (1,)), ((), ())), preferred_element_type=jnp.float32
    )


def matmul_left_t(left_side, right_side):
    return lax.dot_general(
        left_side, right_side, (((0,), (0,)), ((), ())), preferred_element_type=jnp.float32
    )


def block_scores(queries, keys, query_pos, key_pos, key_live, slopes, seq_length):
    factor = queries.shape[-1] ** (-0.5)
    scores = (
        jnp.einsum("uqhd,ukhd->uhqk", queries, keys, preferred_element_type=jnp.float32) * factor
    )
    distance = jnp.abs(query_pos[:, None] - key_pos[None, :]).astype(jnp.float32) / seq_length
    scores = scores - slopes[None, :, None, None] * distance[None, None]
    return (jnp.where(key_live[:, None, None, :], scores, NEGATIVE), distance)


def per_device_any(
    frames_in,
    noise,
    lengths,
    span_starts,
    w_in1,
    w_out1,
    w_qkv,
    w_attn,
    w_point1,
    w_point2,
    w_in2,
    w_out2,
    norm_params,
    kernel,
    slopes,
    cotangent,
):
    utterances, frames, model_width = frames_in.shape
    head_count = slopes.shape[0]
    head_dim = model_width // head_count
    row_count = utterances * frames
    tap_count = kernel.shape[0]
    half_taps = tap_count // 2
    factor = head_dim ** (-0.5)
    seq_length = frames * lax.axis_size("seq")
    first_frame = lax.axis_index("seq") * frames
    frame_pos = first_frame + jnp.arange(frames, dtype=jnp.int32)
    live_mask = frame_pos[None, :] < lengths[:, None]
    live_rows = live_mask.astype(jnp.float32).reshape(row_count, 1)
    span_begin = span_starts[:, :, None]
    masked = jnp.any(
        (span_begin <= frame_pos[None, None, :]) & (frame_pos[None, None, :] < span_begin + SPAN),
        axis=1,
    )
    start_in = (
        jnp.where(masked[..., None], noise, frames_in)
        .astype(jnp.float32)
        .reshape(row_count, model_width)
    )
    norm_gain = norm_params[:, 0]
    norm_shift = norm_params[:, 1]
    shards = (w_in1, w_out1, w_qkv, w_attn, w_point1, w_point2, w_in2, w_out2)
    gathered = (
        lax.all_gather(shards[0], "seq", axis=0, tiled=True),
        lax.all_gather(shards[1], "seq", axis=0, tiled=True),
        lax.all_gather(shards[2], "seq", axis=0, tiled=True),
        lax.all_gather(shards[3], "seq", axis=0, tiled=True),
        lax.all_gather(shards[4], "seq", axis=0, tiled=True),
        lax.all_gather(shards[5], "seq", axis=0, tiled=True),
        lax.all_gather(shards[6], "seq", axis=0, tiled=True),
        lax.all_gather(shards[7], "seq", axis=0, tiled=True),
    )
    full_in1, full_out1, full_qkv, full_attn, full_point1, full_point2, full_in2, full_out2 = (
        gathered
    )
    act_one = layer_norm(start_in, norm_gain[0], norm_shift[0]).astype(jnp.bfloat16)
    up_one = matmul(act_one, full_in1)
    hid_one = jax.nn.silu(up_one).astype(jnp.bfloat16)
    ffn_one = matmul(hid_one, full_out1)
    resid_one = start_in + 0.5 * ffn_one
    act_two = layer_norm(resid_one, norm_gain[1], norm_shift[1]).astype(jnp.bfloat16)
    packed = (
        matmul(act_two, full_qkv)
        .astype(jnp.bfloat16)
        .reshape(utterances, frames, 3, head_count, head_dim)
    )
    queries = packed[:, :, 0]
    keys = packed[:, :, 1]
    values = packed[:, :, 2]
    row_max = jnp.full((utterances, head_count, frames), NEGATIVE, jnp.float32)
    key_blk = lax.all_gather(keys, "seq", axis=1, tiled=True)
    value_blk = lax.all_gather(values, "seq", axis=1, tiled=True)
    amount = key_blk.shape[1]
    key_pos = jnp.arange(amount, dtype=jnp.int32)
    key_live = key_pos[None, :] < lengths[:, None]
    scores, distance = block_scores(
        queries, key_blk, frame_pos, key_pos, key_live, slopes, seq_length
    )
    new_max = jnp.maximum(row_max, jnp.max(scores, axis=-1))
    expd = jnp.exp(scores - new_max[..., None])
    row_sum = jnp.sum(expd, axis=-1)
    update = jnp.einsum(
        "uhqk,ukhd->uqhd", expd.astype(jnp.bfloat16), value_blk, preferred_element_type=jnp.float32
    )
    partial_value = update
    row_max, row_sum, partial_value = (new_max, row_sum, partial_value)
    attn_out = partial_value / jnp.transpose(row_sum, (0, 2, 1))[..., None]
    log_total = jnp.transpose(row_max + jnp.log(row_sum), (0, 2, 1))
    attn_low = attn_out.astype(jnp.bfloat16).reshape(row_count, model_width)
    attended = matmul(attn_low, full_attn)
    resid_two = resid_one + attended
    act_three = layer_norm(resid_two, norm_gain[2], norm_shift[2]).astype(jnp.bfloat16)
    joined = matmul(act_three, full_point1)
    gated = (
        glu_gate(joined, live_rows).astype(jnp.bfloat16).reshape(utterances, frames, model_width)
    )
    padded = padded_2(gated, (("seq", 1),), half_taps)
    depth = kernel[0] * padded[:, 0:frames].astype(jnp.float32)
    for position in range(1, tap_count):
        depth = depth + kernel[position] * padded[:, position : position + frames].astype(
            jnp.float32
        )
    depth = depth.reshape(row_count, model_width)
    act_four = swish_norm(depth, norm_gain[3], norm_shift[3]).astype(jnp.bfloat16)
    convolved = matmul(act_four, full_point2)
    resid_three = resid_two + convolved
    act_five = layer_norm(resid_three, norm_gain[4], norm_shift[4]).astype(jnp.bfloat16)
    up_two = matmul(act_five, full_in2)
    hid_two = jax.nn.silu(up_two).astype(jnp.bfloat16)
    ffn_two = matmul(hid_two, full_out2)
    resid_four = resid_three + 0.5 * ffn_two
    result = layer_norm(resid_four, norm_gain[5], norm_shift[5])
    gathered = (
        lax.all_gather(shards[0], "seq", axis=0, tiled=True),
        lax.all_gather(shards[1], "seq", axis=0, tiled=True),
        lax.all_gather(shards[2], "seq", axis=0, tiled=True),
        lax.all_gather(shards[3], "seq", axis=0, tiled=True),
        lax.all_gather(shards[4], "seq", axis=0, tiled=True),
        lax.all_gather(shards[5], "seq", axis=0, tiled=True),
        lax.all_gather(shards[6], "seq", axis=0, tiled=True),
        lax.all_gather(shards[7], "seq", axis=0, tiled=True),
    )
    full_in1, full_out1, full_qkv, full_attn, full_point1, full_point2, full_in2, full_out2 = (
        gathered
    )
    grad_result = cotangent.astype(jnp.float32).reshape(row_count, model_width)
    _, back_five = jax.vjp(layer_norm, resid_four, norm_gain[5], norm_shift[5])
    grad_four, gain_five, shift_five = back_five(grad_result)
    grad_ffn2 = (0.5 * grad_four).astype(jnp.bfloat16)
    _, back_silu2 = jax.vjp(jax.nn.silu, up_two)
    grad_up2 = back_silu2(matmul_right_t(grad_ffn2, full_out2))[0].astype(jnp.bfloat16)
    _, back_four = jax.vjp(layer_norm, resid_three, norm_gain[4], norm_shift[4])
    grad_norm4, gain_four, shift_four = back_four(matmul_right_t(grad_up2, full_in2))
    grad_three = grad_four + grad_norm4
    grad_conv = grad_three.astype(jnp.bfloat16)
    _, back_swish = jax.vjp(swish_norm, depth, norm_gain[3], norm_shift[3])
    grad_depth_f, gain_three, shift_three = back_swish(matmul_right_t(grad_conv, full_point2))
    grad_depth = grad_depth_f.astype(jnp.bfloat16).reshape(utterances, frames, model_width)
    grad_padded = padded_2(grad_depth, (("seq", 1),), half_taps)
    grad_depth_wide = grad_depth.astype(jnp.float32)
    grad_gated = jnp.zeros((utterances, frames, model_width), jnp.float32)
    kernel_rows = []
    for position in range(tap_count):
        lower = 2 * half_taps - position
        grad_gated = grad_gated + kernel[position] * grad_padded[:, lower : lower + frames].astype(
            jnp.float32
        )
        kernel_rows.append(
            jnp.sum(
                grad_depth_wide * padded[:, position : position + frames].astype(jnp.float32),
                axis=(0, 1),
            )
        )
    grad_kernel = jnp.stack(kernel_rows)
    _, back_gate = jax.vjp(lambda joined_in: glu_gate(joined_in, live_rows), joined)
    grad_joined = back_gate(grad_gated.reshape(row_count, model_width))[0].astype(jnp.bfloat16)
    _, back_three = jax.vjp(layer_norm, resid_two, norm_gain[2], norm_shift[2])
    grad_norm3, gain_two, shift_two = back_three(matmul_right_t(grad_joined, full_point1))
    grad_two = grad_three + grad_norm3
    grad_att = grad_two.astype(jnp.bfloat16)
    grad_heads = (
        matmul_right_t(grad_att, full_attn)
        .astype(jnp.bfloat16)
        .reshape(utterances, frames, head_count, head_dim)
    )
    spread = jnp.sum(grad_heads.astype(jnp.float32) * attn_out, axis=-1)
    log_total_t = jnp.transpose(log_total, (0, 2, 1))
    spread_t = jnp.transpose(spread, (0, 2, 1))
    grad_slope = jnp.zeros((head_count,), jnp.float32)
    key_blk = lax.all_gather(keys, "seq", axis=1, tiled=True)
    value_blk = lax.all_gather(values, "seq", axis=1, tiled=True)
    amount = key_blk.shape[1]
    key_pos = jnp.arange(amount, dtype=jnp.int32)
    key_live = key_pos[None, :] < lengths[:, None]
    scores, distance = block_scores(
        queries, key_blk, frame_pos, key_pos, key_live, slopes, seq_length
    )
    attn_prob = jnp.exp(scores - log_total_t[..., None])
    grad_prob = jnp.einsum(
        "uqhd,ukhd->uhqk", grad_heads, value_blk, preferred_element_type=jnp.float32
    )
    grad_exact = attn_prob * (grad_prob - spread_t[..., None])
    grad_scores = grad_exact.astype(jnp.bfloat16)
    grad_query = (
        jnp.einsum("uhqk,ukhd->uqhd", grad_scores, key_blk, preferred_element_type=jnp.float32)
        * factor
    )
    grad_slope = grad_slope - jnp.sum(grad_exact * distance[None, None], axis=(0, 2, 3))
    grad_query, grad_slope = (grad_query, grad_slope)
    query_blk = lax.all_gather(queries, "seq", axis=1, tiled=True)
    dhead_blk = lax.all_gather(grad_heads, "seq", axis=1, tiled=True)
    total_blk = lax.all_gather(log_total.astype(jnp.bfloat16), "seq", axis=1, tiled=True).astype(
        jnp.float32
    )
    spread_blk = lax.all_gather(spread.astype(jnp.bfloat16), "seq", axis=1, tiled=True).astype(
        jnp.float32
    )
    amount = query_blk.shape[1]
    query_pos = jnp.arange(amount, dtype=jnp.int32)
    scores, distance = block_scores(
        query_blk, keys, query_pos, frame_pos, live_mask, slopes, seq_length
    )
    attn_prob = jnp.exp(scores - jnp.transpose(total_blk, (0, 2, 1))[..., None])
    grad_value = jnp.einsum(
        "uhqk,uqhd->ukhd",
        attn_prob.astype(jnp.bfloat16),
        dhead_blk,
        preferred_element_type=jnp.float32,
    )
    grad_prob = jnp.einsum("uqhd,ukhd->uhqk", dhead_blk, values, preferred_element_type=jnp.float32)
    grad_scores = (
        attn_prob * (grad_prob - jnp.transpose(spread_blk, (0, 2, 1))[..., None])
    ).astype(jnp.bfloat16)
    grad_key = (
        jnp.einsum("uhqk,uqhd->ukhd", grad_scores, query_blk, preferred_element_type=jnp.float32)
        * factor
    )
    grad_key, grad_value = (grad_key, grad_value)
    grad_packed = (
        jnp.stack([grad_query, grad_key, grad_value], axis=2)
        .astype(jnp.bfloat16)
        .reshape(row_count, 3 * model_width)
    )
    _, back_two = jax.vjp(layer_norm, resid_one, norm_gain[1], norm_shift[1])
    grad_norm2, gain_one, shift_one = back_two(matmul_right_t(grad_packed, full_qkv))
    grad_one = grad_two + grad_norm2
    grad_ffn1 = (0.5 * grad_one).astype(jnp.bfloat16)
    _, back_silu1 = jax.vjp(jax.nn.silu, up_one)
    grad_up1 = back_silu1(matmul_right_t(grad_ffn1, full_out1))[0].astype(jnp.bfloat16)
    _, back_one = jax.vjp(layer_norm, start_in, norm_gain[0], norm_shift[0])
    grad_norm1, gain_zero, shift_zero = back_one(matmul_right_t(grad_up1, full_in1))
    grad_start = grad_one + grad_norm1
    grad_frames = jnp.where(
        masked[..., None], 0.0, grad_start.reshape(utterances, frames, model_width)
    )
    wide_pairs = (
        (act_one, grad_up1),
        (act_two, grad_packed),
        (attn_low, grad_att),
        (act_three, grad_joined),
        (act_four, grad_conv),
        (act_five, grad_up2),
    )
    wide = lax.psum_scatter(
        jnp.concatenate(
            [matmul_left_t(left_side, right_side) for left_side, right_side in wide_pairs], axis=1
        ).astype(jnp.bfloat16),
        "seq",
        scatter_dimension=0,
        tiled=True,
    ).astype(jnp.float32)
    tall_pairs = ((hid_one, grad_ffn1), (hid_two, grad_ffn2))
    tall = lax.psum_scatter(
        jnp.concatenate(
            [matmul_left_t(left_side, right_side) for left_side, right_side in tall_pairs], axis=1
        ).astype(jnp.bfloat16),
        "seq",
        scatter_dimension=0,
        tiled=True,
    ).astype(jnp.float32)
    hidden_width = w_in1.shape[1]
    column_cuts = [
        hidden_width,
        3 * model_width,
        model_width,
        2 * model_width,
        model_width,
        hidden_width,
    ]
    wide_parts = []
    column_start = 0
    for column_width in column_cuts:
        wide_parts.append(wide[:, column_start : column_start + column_width])
        column_start = column_start + column_width
    grad_in1, grad_qkv, grad_attn, grad_point1, grad_point2, grad_in2 = wide_parts
    grad_out1 = tall[:, :model_width]
    grad_out2 = tall[:, model_width:]
    grad_norms = jnp.stack(
        [
            jnp.stack([gain_zero, shift_zero]),
            jnp.stack([gain_one, shift_one]),
            jnp.stack([gain_two, shift_two]),
            jnp.stack([gain_three, shift_three]),
            jnp.stack([gain_four, shift_four]),
            jnp.stack([gain_five, shift_five]),
        ]
    )
    grad_norms, grad_kernel, grad_slope = (
        lax.psum(grad_norms.astype(jnp.bfloat16), "seq").astype(jnp.float32),
        lax.psum(grad_kernel.astype(jnp.bfloat16), "seq").astype(jnp.float32),
        lax.psum(grad_slope.astype(jnp.bfloat16), "seq").astype(jnp.float32),
    )
    block_out = result.astype(jnp.bfloat16).reshape(utterances, frames, model_width)
    return (
        block_out,
        grad_frames,
        grad_in1,
        grad_out1,
        grad_qkv,
        grad_attn,
        grad_point1,
        grad_point2,
        grad_in2,
        grad_out2,
        grad_norms,
        grad_kernel,
        grad_slope,
    )


def place():
    seq, dp = lax.axis_index("seq"), lax.axis_index("dp")
    return seq // 2, lax.rem(seq, 2), dp // 2, lax.rem(dp, 2)


def device(z, x, y, core):
    return (z * 2 + x, y * 2 + core)


def z_partners(z):
    return (z + 1 - 2 * lax.rem(z, 2), lax.rem(z + 2, 4), 3 - z)


def remote(source, target, send, recv, where):
    return pltpu.make_async_remote_copy(
        src_ref=source,
        dst_ref=target,
        send_sem=send,
        recv_sem=recv,
        device_id=where,
        device_id_type=MESH,
    )


def greet(partners, waits):
    barrier = pltpu.get_barrier_semaphore()
    for partner in partners:
        pl.semaphore_signal(barrier, inc=1, device_id=partner, device_id_type=MESH)
    pl.semaphore_wait(barrier, waits)


def utterance_of(z, x, core):
    return lax.rem(z, 2) * 4 + x * 2 + core


def home_of(utterance, y, group):
    return device(2 * group + utterance // 4, lax.rem(utterance // 2, 2), y, lax.rem(utterance, 2))


def bits_of(s):
    return s // 4, lax.rem(s // 2, 2), lax.rem(s, 2)


def flipped(bits, r):
    flips = (r // 4, r // 2 % 2, r % 2)
    return [1 - b if f else b for b, f in zip(bits, flips)]


def utterance_in_round(seq, r):
    b2, b1, b0 = bits_of(seq)
    out = flipped((b1, b0, b2), r)
    return out[0] * 4 + out[1] * 2 + out[2]


def seq_in_round(utterance, r):
    t2, t1, t0 = flipped(bits_of(utterance), r)
    return t0 * 4 + t2 * 2 + t1


def exchange_kernel(count, to_utterances, *refs):
    ins, outs = refs[:count], refs[count : 2 * count]
    send, recv, own = refs[2 * count :]
    z, x, y, core = place()
    seq = z * 2 + x
    group = z // 2
    utterance = utterance_of(z, x, core)
    same = group == core
    seqs = [seq_in_round(utterance, r) for r in range(8)]
    mates = [utterance_in_round(seq, r) for r in range(8)]
    sources = [device(s // 2, lax.rem(s, 2), y, group) for s in seqs]
    homes = [home_of(u, y, core) for u in mates]
    if to_utterances:
        targets, givers, mine, blocks = homes, sources, seq, mates
    else:
        targets, givers, mine, blocks = sources, homes, utterance, seqs
    barrier = pltpu.get_barrier_semaphore()
    for r in range(8):
        if r == 0:

            @pl.when(jnp.logical_not(same))
            def _():
                pl.semaphore_signal(barrier, inc=1, device_id=givers[0], device_id_type=MESH)
        else:
            pl.semaphore_signal(barrier, inc=1, device_id=givers[r], device_id_type=MESH)
    pl.semaphore_wait(barrier, jnp.where(same, 7, 8))

    def copy(i, r):
        return remote(
            ins[i].at[blocks[r]], outs[i].at[mine], send.at[i, r], recv.at[i, r], targets[r]
        )

    def local(i):
        return pltpu.make_async_copy(ins[i].at[blocks[0]], outs[i].at[mine], own.at[i])

    for i in range(count):

        @pl.when(jnp.logical_not(same))
        def _():
            copy(i, 0).start()

        @pl.when(same)
        def _():
            local(i).start()

        for r in range(1, 8):
            copy(i, r).start()
    for i in range(count):

        @pl.when(jnp.logical_not(same))
        def _():
            copy(i, 0).wait()

        @pl.when(same)
        def _():
            local(i).wait()

        for r in range(1, 8):
            copy(i, r).wait()


def exchange(arrays, to_utterances, collective_id):
    count = len(arrays)
    return pl.pallas_call(
        functools.partial(exchange_kernel, count, to_utterances),
        out_shape=[jax.ShapeDtypeStruct(a.shape, a.dtype) for a in arrays],
        in_specs=[ANY] * count,
        out_specs=[ANY] * count,
        scratch_shapes=[
            pltpu.SemaphoreType.DMA((count, 8)),
            pltpu.SemaphoreType.DMA((count, 8)),
            pltpu.SemaphoreType.DMA((count,)),
        ],
        compiler_params=pltpu.CompilerParams(collective_id=collective_id, has_side_effects=True),
    )(*arrays)


def units_of(shapes):
    units = []
    for index, (rows, columns) in enumerate(shapes):
        for row in range(0, rows, 128):
            for column in range(0, columns, 1024):
                units.append((index, row, column))
    return units


ROWS = 128
HALF = 64
COLUMNS = 1024
SPLIT = 384


def gather_kernel(units, count, *refs):
    shards, fulls = refs[:count], refs[count : 2 * count]
    send, recv, own = refs[2 * count :]
    z, x, y, core = place()
    zs = z_partners(z)
    over_z = [device(other, x, y, core) for other in zs]
    over_x = device(z, 1 - x, y, core)
    over_y = device(z, x, 1 - y, core)
    over_core = device(z, x, y, 1 - core)
    greet(over_z + [over_x, over_y, over_core], 6)

    def spot(unit):
        index, row, column = unit
        rows = pl.ds(row + pl.multiple_of(core * HALF, HALF), HALF)
        mine = pl.ds(column + pl.multiple_of(y * SPLIT, 128), COLUMNS - SPLIT)
        third = pl.ds(column + pl.multiple_of(y * (COLUMNS - SPLIT), 128), SPLIT)
        return shards[index], fulls[index], rows, mine, third, pl.ds(column, COLUMNS)

    def first(u):
        shard, full, rows, mine, _, _ = spot(units[u])
        source = shard.at[rows, mine]
        out = [pltpu.make_async_copy(source, full.at[z, x, rows, mine], own.at[u])]
        for j in range(3):
            out.append(
                remote(source, full.at[z, x, rows, mine], send.at[u, j], recv.at[u, j], over_z[j])
            )
        return out

    def second(u):
        _, full, rows, mine, _, _ = spot(units[u])
        piece = full.at[:, x, rows, mine]
        return [remote(piece, piece, send.at[u, 3], recv.at[u, 3], over_x)]

    def third(u):
        _, full, rows, _, part, _ = spot(units[u])
        piece = full.at[:, :, rows, part]
        return [remote(piece, piece, send.at[u, 4], recv.at[u, 4], over_y)]

    def fourth(u):
        _, full, rows, _, _, whole = spot(units[u])
        piece = full.at[:, :, rows, whole]
        return [remote(piece, piece, send.at[u, 5], recv.at[u, 5], over_core)]

    stages = (first, second, third, fourth)
    last = len(units)
    for step in range(last + len(stages)):
        for depth, stage in enumerate(stages):
            u = step - depth
            if depth > 0 and 0 <= u < last:
                for copy in stages[depth - 1](u):
                    copy.wait()
            if 0 <= u < last:
                for copy in stage(u):
                    copy.start()
        u = step - len(stages)
        if 0 <= u < last:
            for copy in stages[-1](u):
                copy.wait()


def gather(shards, collective_id):
    count = len(shards)
    shapes = [s.shape for s in shards]
    units = units_of(shapes)
    fulls = pl.pallas_call(
        functools.partial(gather_kernel, units, count),
        out_shape=[jax.ShapeDtypeStruct((4, 2) + s, BF16) for s in shapes],
        in_specs=[ANY] * count,
        out_specs=[ANY] * count,
        scratch_shapes=[
            pltpu.SemaphoreType.DMA((len(units), 6)),
            pltpu.SemaphoreType.DMA((len(units), 6)),
            pltpu.SemaphoreType.DMA((len(units),)),
        ],
        compiler_params=pltpu.CompilerParams(collective_id=collective_id, has_side_effects=True),
    )(*shards)
    return [f.reshape(8 * s[0], s[1]) for f, s in zip(fulls, shapes)]


def scatter_kernel(units, count, *refs):
    grads, outs = refs[:count], refs[count : 2 * count]
    (mine, core_in, x_in, z_in, load, s_core, r_core, s_x, r_x, s_z, r_z, s_far, r_far, s_near, r_near, local) = refs[
        2 * count :
    ]
    z, x, y, core = place()
    group = z // 2
    z_other = z + 1 - 2 * lax.rem(z, 2)
    over_core = device(z, x, y, 1 - core)
    over_x = device(z, 1 - x, y, core)
    over_z = device(z_other, x, y, core)
    far = device(3 - z, x, y, group)
    keeps = core == group
    barrier = pltpu.get_barrier_semaphore()
    for partner in (over_core, over_x, over_z):
        pl.semaphore_signal(barrier, inc=1, device_id=partner, device_id_type=MESH)
    far_givers = [device(3 - z, x, y, 0), device(3 - z, x, y, 1)]

    @pl.when(jnp.logical_not(keeps))
    def _():
        for giver in far_givers:
            pl.semaphore_signal(barrier, inc=1, device_id=giver, device_id_type=MESH)

    pl.semaphore_wait(barrier, 4)

    half = pl.multiple_of(core * HALF, HALF)
    other_half = pl.multiple_of((1 - core) * HALF, HALF)

    def core_copy(u):
        index, row, column = units[u]
        source = grads[index].at[:, :, pl.ds(row + other_half, HALF), pl.ds(column, COLUMNS)]
        return remote(source, core_in.at[u % 2], s_core.at[u % 2], r_core.at[u % 2], over_core)

    def load_copy(u):
        index, row, column = units[u]
        source = grads[index].at[:, :, pl.ds(row + half, HALF), pl.ds(column, COLUMNS)]
        return pltpu.make_async_copy(source, mine.at[u % 5], load.at[u % 2])

    def x_copy(u):
        return remote(
            mine.at[u % 5, :, 1 - x], x_in.at[u % 4], s_x.at[u % 4], r_x.at[u % 4], over_x
        )

    def z_copy(u, part):
        target_z = z_other if part == 0 else 3 - z_other
        return remote(
            mine.at[u % 5, target_z, x],
            z_in.at[u % 4, part],
            s_z.at[u % 4, part],
            r_z.at[u % 4, part],
            over_z,
        )

    def far_copy(u):
        index, row, column = units[u]
        target = outs[index].at[pl.ds(row + half, HALF), pl.ds(column, COLUMNS)]
        return remote(
            mine.at[u % 5, 3 - z, x], target, s_far.at[u % 2], r_far.at[u, core], far
        )

    def far_arrival(u, giver):
        index, row, column = units[u]
        target = outs[index].at[pl.ds(row + giver * HALF, HALF), pl.ds(column, COLUMNS)]
        return remote(
            mine.at[u % 5, 3 - z, x], target, s_far.at[u % 2], r_far.at[u, giver], far
        )

    def near_target(u):
        index, row, column = units[u]
        return outs[index].at[pl.ds(row + half, HALF), pl.ds(column, COLUMNS)]

    def near_copy(u):
        return remote(
            mine.at[u % 5, z, x], near_target(u), s_near.at[u % 2], r_near.at[u], over_core
        )

    def near_arrival(u):
        index, row, column = units[u]
        target = outs[index].at[pl.ds(row + other_half, HALF), pl.ds(column, COLUMNS)]
        return remote(
            mine.at[u % 5, z, x], target, s_near.at[u % 2], r_near.at[u], over_core
        )

    def near_local(u):
        return pltpu.make_async_copy(mine.at[u % 5, z, x], near_target(u), local.at[u % 2])

    def add(into, other):
        into[...] = (into[...].astype(F32) + other[...].astype(F32)).astype(BF16)

    def stage0(u):
        load_copy(u).start()
        core_copy(u).start()

    def stage1(u):
        load_copy(u).wait()
        core_copy(u).wait()

        @pl.loop(0, 4)
        def _(i):
            add(mine.at[u % 5, i, 1 - x], core_in.at[u % 2, i, 1 - x])

        x_copy(u).start()

        @pl.loop(0, 4)
        def _(i):
            add(mine.at[u % 5, i, x], core_in.at[u % 2, i, x])

    def stage2(u):
        x_copy(u).wait()
        for part, target_z in ((0, z_other), (1, 3 - z_other)):
            add(mine.at[u % 5, target_z, x], x_in.at[u % 4, target_z])
            z_copy(u, part).start()
        for target_z in (z, 3 - z):
            add(mine.at[u % 5, target_z, x], x_in.at[u % 4, target_z])

    def stage3(u):
        z_copy(u, 0).wait()
        z_copy(u, 1).wait()
        add(mine.at[u % 5, 3 - z, x], z_in.at[u % 4, 1])
        far_copy(u).start()
        add(mine.at[u % 5, z, x], z_in.at[u % 4, 0])

        @pl.when(keeps)
        def _():
            near_local(u).start()

        @pl.when(jnp.logical_not(keeps))
        def _():
            near_copy(u).start()

    def stage4(u):
        far_copy(u).wait_send()

        @pl.when(keeps)
        def _():
            near_local(u).wait()
            near_arrival(u).wait_recv()

        @pl.when(jnp.logical_not(keeps))
        def _():
            near_copy(u).wait_send()

    last = len(units)
    order = ((stage1, 1), (stage0, 0), (stage2, 2), (stage3, 3), (stage4, 4))
    for step in range(last + 4):
        for stage, depth in order:
            if 0 <= step - depth < last:
                stage(step - depth)

    @pl.when(jnp.logical_not(keeps))
    def _():
        for u in range(last):
            far_arrival(u, 0).wait_recv()
            far_arrival(u, 1).wait_recv()


def scatter(grads, collective_id):
    count = len(grads)
    shapes = [(g.shape[0] // 8, g.shape[1]) for g in grads]
    units = units_of(shapes)
    dma = pltpu.SemaphoreType.DMA
    return pl.pallas_call(
        functools.partial(scatter_kernel, units, count),
        out_shape=[jax.ShapeDtypeStruct(s, BF16) for s in shapes],
        in_specs=[ANY] * count,
        out_specs=[ANY] * count,
        scratch_shapes=[
            pltpu.VMEM((5, 4, 2, HALF, COLUMNS), BF16),
            pltpu.VMEM((2, 4, 2, HALF, COLUMNS), BF16),
            pltpu.VMEM((4, 4, HALF, COLUMNS), BF16),
            pltpu.VMEM((4, 2, HALF, COLUMNS), BF16),
            dma((2,)),
            dma((2,)),
            dma((2,)),
            dma((4,)),
            dma((4,)),
            dma((4, 2)),
            dma((4, 2)),
            dma((2,)),
            dma((len(units), 2)),
            dma((2,)),
            dma((len(units),)),
            dma((2,)),
        ],
        compiler_params=pltpu.CompilerParams(
            collective_id=collective_id, has_side_effects=True, vmem_limit_bytes=40 * 2**20
        ),
    )(*[g.reshape((4, 2) + s) for g, s in zip(grads, shapes)])


def per_device(
    frames_in,
    noise,
    lengths,
    span_starts,
    w_in1,
    w_out1,
    w_qkv,
    w_attn,
    w_point1,
    w_point2,
    w_in2,
    w_out2,
    norm_params,
    kernel,
    slopes,
    cotangent,
):
    utterances, frames, width = frames_in.shape
    heads = slopes.shape[0]
    head_dim = width // heads
    length = frames * 8
    taps = kernel.shape[0]
    half_taps = taps // 2
    factor = head_dim ** (-0.5)
    frame_pos = lax.axis_index("seq") * frames + jnp.arange(frames, dtype=jnp.int32)
    span_begin = span_starts[:, :, None]
    masked = jnp.any(
        (span_begin <= frame_pos[None, None, :]) & (frame_pos[None, None, :] < span_begin + SPAN),
        axis=1,
    )
    start = jnp.where(masked[..., None], noise, frames_in)
    lens = jnp.broadcast_to(lengths.astype(F32)[:, None, None], (utterances, 8, 128))
    start, cot, lens = exchange((start, cotangent, lens), True, 0)
    h0 = start.reshape(length, width).astype(F32)
    cot = cot.reshape(length, width).astype(F32)
    live_count = lens[0, 0, 0]
    position = jnp.arange(length, dtype=jnp.int32).astype(F32)
    live = (position < live_count).astype(F32)[:, None]
    key_live = position < live_count
    gain, shift = norm_params[:, 0], norm_params[:, 1]
    in1, out1, qkv, attn, point1, point2, in2, out2 = gather(
        (w_in1, w_out1, w_qkv, w_attn, w_point1, w_point2, w_in2, w_out2), 1
    )
    a1 = layer_norm(h0, gain[0], shift[0]).astype(BF16)
    u1 = matmul(a1, in1)
    s1 = jax.nn.silu(u1).astype(BF16)
    x1 = h0 + 0.5 * matmul(s1, out1)
    a2 = layer_norm(x1, gain[1], shift[1]).astype(BF16)
    packed = matmul(a2, qkv).astype(BF16).reshape(length, 3, heads, head_dim)
    q, k, v = packed[:, 0], packed[:, 1], packed[:, 2]
    distance = jnp.abs(position[:, None] - position[None, :]) / length
    scores = jnp.einsum("qhd,khd->hqk", q, k, preferred_element_type=F32) * factor
    scores = scores - slopes[:, None, None] * distance[None]
    scores = jnp.where(key_live[None, None, :], scores, NEGATIVE)
    top = jnp.max(scores, axis=-1, keepdims=True)
    expd = jnp.exp(scores - top)
    prob = expd / jnp.sum(expd, axis=-1, keepdims=True)
    prob_low = prob.astype(BF16)
    o = jnp.einsum("hqk,khd->qhd", prob_low, v, preferred_element_type=F32)
    ob = o.astype(BF16).reshape(length, width)
    x2 = x1 + matmul(ob, attn)
    a3 = layer_norm(x2, gain[2], shift[2]).astype(BF16)
    z = matmul(a3, point1)
    g = glu_gate(z, live).astype(BF16)
    padded = jnp.pad(g, ((half_taps, half_taps), (0, 0)))
    depth = kernel[0] * padded[0:length].astype(F32)
    for t in range(1, taps):
        depth = depth + kernel[t] * padded[t : t + length].astype(F32)
    c4 = swish_norm(depth, gain[3], shift[3]).astype(BF16)
    x3 = x2 + matmul(c4, point2)
    a5 = layer_norm(x3, gain[4], shift[4]).astype(BF16)
    u2 = matmul(a5, in2)
    s2 = jax.nn.silu(u2).astype(BF16)
    x4 = x3 + 0.5 * matmul(s2, out2)
    result = layer_norm(x4, gain[5], shift[5]).astype(BF16)
    _, back = jax.vjp(layer_norm, x4, gain[5], shift[5])
    dx4, gain5, shift5 = back(cot)
    df2 = (0.5 * dx4).astype(BF16)
    _, back = jax.vjp(jax.nn.silu, u2)
    du2 = back(matmul_right_t(df2, out2))[0].astype(BF16)
    _, back = jax.vjp(layer_norm, x3, gain[4], shift[4])
    dn, gain4, shift4 = back(matmul_right_t(du2, in2))
    dx3 = dx4 + dn
    dc = dx3.astype(BF16)
    _, back = jax.vjp(swish_norm, depth, gain[3], shift[3])
    dd, gain3, shift3 = back(matmul_right_t(dc, point2))
    dd = dd.astype(BF16)
    dd_padded = jnp.pad(dd, ((half_taps, half_taps), (0, 0)))
    dg = jnp.zeros((length, width), F32)
    kernel_rows = []
    for t in range(taps):
        lower = 2 * half_taps - t
        dg = dg + kernel[t] * dd_padded[lower : lower + length].astype(F32)
        kernel_rows.append(jnp.sum(dd.astype(F32) * padded[t : t + length].astype(F32), axis=0))
    _, back = jax.vjp(lambda joined: glu_gate(joined, live), z)
    dz = back(dg)[0].astype(BF16)
    _, back = jax.vjp(layer_norm, x2, gain[2], shift[2])
    dn, gain2, shift2 = back(matmul_right_t(dz, point1))
    dx2 = dx3 + dn
    da = dx2.astype(BF16)
    do = matmul_right_t(da, attn).astype(BF16).reshape(length, heads, head_dim)
    delta = jnp.sum(do.astype(F32) * o, axis=-1)
    dp = jnp.einsum("qhd,khd->hqk", do, v, preferred_element_type=F32)
    ds_exact = prob * (dp - delta.T[..., None])
    dslopes = -jnp.sum(ds_exact * distance[None], axis=(1, 2))
    ds = ds_exact.astype(BF16)
    dq = jnp.einsum("hqk,khd->qhd", ds, k, preferred_element_type=F32) * factor
    dk = jnp.einsum("hqk,qhd->khd", ds, q, preferred_element_type=F32) * factor
    dv = jnp.einsum("hqk,qhd->khd", prob_low, do, preferred_element_type=F32)
    dqkv = jnp.stack([dq, dk, dv], axis=1).astype(BF16).reshape(length, 3 * width)
    _, back = jax.vjp(layer_norm, x1, gain[1], shift[1])
    dn, gain1, shift1 = back(matmul_right_t(dqkv, qkv))
    dx1 = dx2 + dn
    df1 = (0.5 * dx1).astype(BF16)
    _, back = jax.vjp(jax.nn.silu, u1)
    du1 = back(matmul_right_t(df1, out1))[0].astype(BF16)
    _, back = jax.vjp(layer_norm, h0, gain[0], shift[0])
    dn, gain0, shift0 = back(matmul_right_t(du1, in1))
    dh0 = (dx1 + dn).astype(BF16)
    pairs = (
        (a1, du1),
        (s1, df1),
        (a2, dqkv),
        (ob, da),
        (a3, dz),
        (c4, dc),
        (a5, du2),
        (s2, df2),
    )
    grads = scatter([matmul_left_t(a, b).astype(BF16) for a, b in pairs], 2)
    small = jnp.concatenate(
        [
            jnp.stack([gain0, shift0, gain1, shift1, gain2, shift2, gain3, shift3, gain4, shift4, gain5, shift5]),
            jnp.stack(kernel_rows),
            jnp.pad(dslopes, (0, width - heads))[None],
            jnp.zeros((14, width), F32),
        ]
    ).astype(BF16)
    small = jnp.broadcast_to(small[None], (8,) + small.shape)
    block_out, dframes, small = exchange(
        (result.reshape(8, frames, width), dh0.reshape(8, frames, width), small), False, 3
    )
    small = jnp.sum(small.astype(F32), axis=0)
    grad_frames = jnp.where(masked[..., None], 0.0, dframes.astype(F32))
    return (
        block_out,
        grad_frames,
        *[grad.astype(F32) for grad in grads],
        small[:12].reshape(6, 2, width),
        small[12:17],
        small[17, :heads],
    )


def solution(mesh):
    in_specs = (
        P("dp", "seq", None),
        P("dp", "seq", None),
        P("dp"),
        P("dp", None),
        P("seq", None),
        P("seq", None),
        P("seq", None),
        P("seq", None),
        P("seq", None),
        P("seq", None),
        P("seq", None),
        P("seq", None),
        P(),
        P(),
        P(),
        P("dp", "seq", None),
    )
    out_specs = (
        P("dp", "seq", None),
        P("dp", "seq", None),
        P(("dp", "seq"), None),
        P(("dp", "seq"), None),
        P(("dp", "seq"), None),
        P(("dp", "seq"), None),
        P(("dp", "seq"), None),
        P(("dp", "seq"), None),
        P(("dp", "seq"), None),
        P(("dp", "seq"), None),
        P("dp", None, None),
        P("dp", None),
        P("dp"),
    )
    grouped = mesh.shape["seq"] == 8 and mesh.shape["dp"] == 4
    return jax.shard_map(
        per_device if grouped else per_device_any, mesh=mesh, in_specs=in_specs, out_specs=out_specs, check_vma=False
    )
```

```python
import functools

import jax
import jax.numpy as jnp
from jax import lax
from jax.experimental import pallas as pl
from jax.experimental.pallas import tpu as pltpu
from jax.sharding import PartitionSpec as P

MESH = pl.DeviceIdType.MESH
BF16 = jnp.bfloat16
F32 = jnp.float32
ANY = pl.BlockSpec(memory_space=pl.ANY)

SPAN = 10


EPSILON = 1e-05
NEGATIVE = -1e30


def padded_2(shard, sides, width):
    for axis, dim in sides:
        peers, length = (lax.axis_size(axis), shard.shape[dim])
        up = [(i, (i + 1) % peers) for i in range(peers - 1)]
        down = [(j, i) for i, j in up]
        last = lax.slice_in_dim(shard, length - width, length, axis=dim)
        initial = lax.slice_in_dim(shard, 0, width, axis=dim)
        before = lax.ppermute(last, axis, up)
        after = lax.ppermute(initial, axis, down)
        shard = jnp.concatenate([before, shard, after], axis=dim)
    return shard


def layer_norm(inputs, gain_vec, shift_vec):
    average = jnp.mean(inputs, axis=-1, keepdims=True)
    centred = inputs - average
    variance = jnp.mean(centred * centred, axis=-1, keepdims=True)
    return centred * lax.rsqrt(variance + EPSILON) * gain_vec + shift_vec


def swish_norm(inputs, gain_vec, shift_vec):
    return jax.nn.silu(layer_norm(inputs, gain_vec, shift_vec))


def glu_gate(joined, live_rows):
    half_width = joined.shape[-1] // 2
    return joined[..., :half_width] * jax.nn.sigmoid(joined[..., half_width:]) * live_rows


def matmul(left_side, right_side):
    return jnp.dot(left_side, right_side, preferred_element_type=jnp.float32)


def matmul_right_t(left_side, right_side):
    return lax.dot_general(
        left_side, right_side, (((1,), (1,)), ((), ())), preferred_element_type=jnp.float32
    )


def matmul_left_t(left_side, right_side):
    return lax.dot_general(
        left_side, right_side, (((0,), (0,)), ((), ())), preferred_element_type=jnp.float32
    )


def block_scores(queries, keys, query_pos, key_pos, key_live, slopes, seq_length):
    factor = queries.shape[-1] ** (-0.5)
    scores = (
        jnp.einsum("uqhd,ukhd->uhqk", queries, keys, preferred_element_type=jnp.float32) * factor
    )
    distance = jnp.abs(query_pos[:, None] - key_pos[None, :]).astype(jnp.float32) / seq_length
    scores = scores - slopes[None, :, None, None] * distance[None, None]
    return (jnp.where(key_live[:, None, None, :], scores, NEGATIVE), distance)


def per_device_any(
    frames_in,
    noise,
    lengths,
    span_starts,
    w_in1,
    w_out1,
    w_qkv,
    w_attn,
    w_point1,
    w_point2,
    w_in2,
    w_out2,
    norm_params,
    kernel,
    slopes,
    cotangent,
):
    utterances, frames, model_width = frames_in.shape
    head_count = slopes.shape[0]
    head_dim = model_width // head_count
    row_count = utterances * frames
    tap_count = kernel.shape[0]
    half_taps = tap_count // 2
    factor = head_dim ** (-0.5)
    seq_length = frames * lax.axis_size("seq")
    first_frame = lax.axis_index("seq") * frames
    frame_pos = first_frame + jnp.arange(frames, dtype=jnp.int32)
    live_mask = frame_pos[None, :] < lengths[:, None]
    live_rows = live_mask.astype(jnp.float32).reshape(row_count, 1)
    span_begin = span_starts[:, :, None]
    masked = jnp.any(
        (span_begin <= frame_pos[None, None, :]) & (frame_pos[None, None, :] < span_begin + SPAN),
        axis=1,
    )
    start_in = (
        jnp.where(masked[..., None], noise, frames_in)
        .astype(jnp.float32)
        .reshape(row_count, model_width)
    )
    norm_gain = norm_params[:, 0]
    norm_shift = norm_params[:, 1]
    shards = (w_in1, w_out1, w_qkv, w_attn, w_point1, w_point2, w_in2, w_out2)
    gathered = (
        lax.all_gather(shards[0], "seq", axis=0, tiled=True),
        lax.all_gather(shards[1], "seq", axis=0, tiled=True),
        lax.all_gather(shards[2], "seq", axis=0, tiled=True),
        lax.all_gather(shards[3], "seq", axis=0, tiled=True),
        lax.all_gather(shards[4], "seq", axis=0, tiled=True),
        lax.all_gather(shards[5], "seq", axis=0, tiled=True),
        lax.all_gather(shards[6], "seq", axis=0, tiled=True),
        lax.all_gather(shards[7], "seq", axis=0, tiled=True),
    )
    full_in1, full_out1, full_qkv, full_attn, full_point1, full_point2, full_in2, full_out2 = (
        gathered
    )
    act_one = layer_norm(start_in, norm_gain[0], norm_shift[0]).astype(jnp.bfloat16)
    up_one = matmul(act_one, full_in1)
    hid_one = jax.nn.silu(up_one).astype(jnp.bfloat16)
    ffn_one = matmul(hid_one, full_out1)
    resid_one = start_in + 0.5 * ffn_one
    act_two = layer_norm(resid_one, norm_gain[1], norm_shift[1]).astype(jnp.bfloat16)
    packed = (
        matmul(act_two, full_qkv)
        .astype(jnp.bfloat16)
        .reshape(utterances, frames, 3, head_count, head_dim)
    )
    queries = packed[:, :, 0]
    keys = packed[:, :, 1]
    values = packed[:, :, 2]
    row_max = jnp.full((utterances, head_count, frames), NEGATIVE, jnp.float32)
    key_blk = lax.all_gather(keys, "seq", axis=1, tiled=True)
    value_blk = lax.all_gather(values, "seq", axis=1, tiled=True)
    amount = key_blk.shape[1]
    key_pos = jnp.arange(amount, dtype=jnp.int32)
    key_live = key_pos[None, :] < lengths[:, None]
    scores, distance = block_scores(
        queries, key_blk, frame_pos, key_pos, key_live, slopes, seq_length
    )
    new_max = jnp.maximum(row_max, jnp.max(scores, axis=-1))
    expd = jnp.exp(scores - new_max[..., None])
    row_sum = jnp.sum(expd, axis=-1)
    update = jnp.einsum(
        "uhqk,ukhd->uqhd", expd.astype(jnp.bfloat16), value_blk, preferred_element_type=jnp.float32
    )
    partial_value = update
    row_max, row_sum, partial_value = (new_max, row_sum, partial_value)
    attn_out = partial_value / jnp.transpose(row_sum, (0, 2, 1))[..., None]
    log_total = jnp.transpose(row_max + jnp.log(row_sum), (0, 2, 1))
    attn_low = attn_out.astype(jnp.bfloat16).reshape(row_count, model_width)
    attended = matmul(attn_low, full_attn)
    resid_two = resid_one + attended
    act_three = layer_norm(resid_two, norm_gain[2], norm_shift[2]).astype(jnp.bfloat16)
    joined = matmul(act_three, full_point1)
    gated = (
        glu_gate(joined, live_rows).astype(jnp.bfloat16).reshape(utterances, frames, model_width)
    )
    padded = padded_2(gated, (("seq", 1),), half_taps)
    depth = kernel[0] * padded[:, 0:frames].astype(jnp.float32)
    for position in range(1, tap_count):
        depth = depth + kernel[position] * padded[:, position : position + frames].astype(
            jnp.float32
        )
    depth = depth.reshape(row_count, model_width)
    act_four = swish_norm(depth, norm_gain[3], norm_shift[3]).astype(jnp.bfloat16)
    convolved = matmul(act_four, full_point2)
    resid_three = resid_two + convolved
    act_five = layer_norm(resid_three, norm_gain[4], norm_shift[4]).astype(jnp.bfloat16)
    up_two = matmul(act_five, full_in2)
    hid_two = jax.nn.silu(up_two).astype(jnp.bfloat16)
    ffn_two = matmul(hid_two, full_out2)
    resid_four = resid_three + 0.5 * ffn_two
    result = layer_norm(resid_four, norm_gain[5], norm_shift[5])
    gathered = (
        lax.all_gather(shards[0], "seq", axis=0, tiled=True),
        lax.all_gather(shards[1], "seq", axis=0, tiled=True),
        lax.all_gather(shards[2], "seq", axis=0, tiled=True),
        lax.all_gather(shards[3], "seq", axis=0, tiled=True),
        lax.all_gather(shards[4], "seq", axis=0, tiled=True),
        lax.all_gather(shards[5], "seq", axis=0, tiled=True),
        lax.all_gather(shards[6], "seq", axis=0, tiled=True),
        lax.all_gather(shards[7], "seq", axis=0, tiled=True),
    )
    full_in1, full_out1, full_qkv, full_attn, full_point1, full_point2, full_in2, full_out2 = (
        gathered
    )
    grad_result = cotangent.astype(jnp.float32).reshape(row_count, model_width)
    _, back_five = jax.vjp(layer_norm, resid_four, norm_gain[5], norm_shift[5])
    grad_four, gain_five, shift_five = back_five(grad_result)
    grad_ffn2 = (0.5 * grad_four).astype(jnp.bfloat16)
    _, back_silu2 = jax.vjp(jax.nn.silu, up_two)
    grad_up2 = back_silu2(matmul_right_t(grad_ffn2, full_out2))[0].astype(jnp.bfloat16)
    _, back_four = jax.vjp(layer_norm, resid_three, norm_gain[4], norm_shift[4])
    grad_norm4, gain_four, shift_four = back_four(matmul_right_t(grad_up2, full_in2))
    grad_three = grad_four + grad_norm4
    grad_conv = grad_three.astype(jnp.bfloat16)
    _, back_swish = jax.vjp(swish_norm, depth, norm_gain[3], norm_shift[3])
    grad_depth_f, gain_three, shift_three = back_swish(matmul_right_t(grad_conv, full_point2))
    grad_depth = grad_depth_f.astype(jnp.bfloat16).reshape(utterances, frames, model_width)
    grad_padded = padded_2(grad_depth, (("seq", 1),), half_taps)
    grad_depth_wide = grad_depth.astype(jnp.float32)
    grad_gated = jnp.zeros((utterances, frames, model_width), jnp.float32)
    kernel_rows = []
    for position in range(tap_count):
        lower = 2 * half_taps - position
        grad_gated = grad_gated + kernel[position] * grad_padded[:, lower : lower + frames].astype(
            jnp.float32
        )
        kernel_rows.append(
            jnp.sum(
                grad_depth_wide * padded[:, position : position + frames].astype(jnp.float32),
                axis=(0, 1),
            )
        )
    grad_kernel = jnp.stack(kernel_rows)
    _, back_gate = jax.vjp(lambda joined_in: glu_gate(joined_in, live_rows), joined)
    grad_joined = back_gate(grad_gated.reshape(row_count, model_width))[0].astype(jnp.bfloat16)
    _, back_three = jax.vjp(layer_norm, resid_two, norm_gain[2], norm_shift[2])
    grad_norm3, gain_two, shift_two = back_three(matmul_right_t(grad_joined, full_point1))
    grad_two = grad_three + grad_norm3
    grad_att = grad_two.astype(jnp.bfloat16)
    grad_heads = (
        matmul_right_t(grad_att, full_attn)
        .astype(jnp.bfloat16)
        .reshape(utterances, frames, head_count, head_dim)
    )
    spread = jnp.sum(grad_heads.astype(jnp.float32) * attn_out, axis=-1)
    log_total_t = jnp.transpose(log_total, (0, 2, 1))
    spread_t = jnp.transpose(spread, (0, 2, 1))
    grad_slope = jnp.zeros((head_count,), jnp.float32)
    key_blk = lax.all_gather(keys, "seq", axis=1, tiled=True)
    value_blk = lax.all_gather(values, "seq", axis=1, tiled=True)
    amount = key_blk.shape[1]
    key_pos = jnp.arange(amount, dtype=jnp.int32)
    key_live = key_pos[None, :] < lengths[:, None]
    scores, distance = block_scores(
        queries, key_blk, frame_pos, key_pos, key_live, slopes, seq_length
    )
    attn_prob = jnp.exp(scores - log_total_t[..., None])
    grad_prob = jnp.einsum(
        "uqhd,ukhd->uhqk", grad_heads, value_blk, preferred_element_type=jnp.float32
    )
    grad_exact = attn_prob * (grad_prob - spread_t[..., None])
    grad_scores = grad_exact.astype(jnp.bfloat16)
    grad_query = (
        jnp.einsum("uhqk,ukhd->uqhd", grad_scores, key_blk, preferred_element_type=jnp.float32)
        * factor
    )
    grad_slope = grad_slope - jnp.sum(grad_exact * distance[None, None], axis=(0, 2, 3))
    grad_query, grad_slope = (grad_query, grad_slope)
    query_blk = lax.all_gather(queries, "seq", axis=1, tiled=True)
    dhead_blk = lax.all_gather(grad_heads, "seq", axis=1, tiled=True)
    total_blk = lax.all_gather(log_total.astype(jnp.bfloat16), "seq", axis=1, tiled=True).astype(
        jnp.float32
    )
    spread_blk = lax.all_gather(spread.astype(jnp.bfloat16), "seq", axis=1, tiled=True).astype(
        jnp.float32
    )
    amount = query_blk.shape[1]
    query_pos = jnp.arange(amount, dtype=jnp.int32)
    scores, distance = block_scores(
        query_blk, keys, query_pos, frame_pos, live_mask, slopes, seq_length
    )
    attn_prob = jnp.exp(scores - jnp.transpose(total_blk, (0, 2, 1))[..., None])
    grad_value = jnp.einsum(
        "uhqk,uqhd->ukhd",
        attn_prob.astype(jnp.bfloat16),
        dhead_blk,
        preferred_element_type=jnp.float32,
    )
    grad_prob = jnp.einsum("uqhd,ukhd->uhqk", dhead_blk, values, preferred_element_type=jnp.float32)
    grad_scores = (
        attn_prob * (grad_prob - jnp.transpose(spread_blk, (0, 2, 1))[..., None])
    ).astype(jnp.bfloat16)
    grad_key = (
        jnp.einsum("uhqk,uqhd->ukhd", grad_scores, query_blk, preferred_element_type=jnp.float32)
        * factor
    )
    grad_key, grad_value = (grad_key, grad_value)
    grad_packed = (
        jnp.stack([grad_query, grad_key, grad_value], axis=2)
        .astype(jnp.bfloat16)
        .reshape(row_count, 3 * model_width)
    )
    _, back_two = jax.vjp(layer_norm, resid_one, norm_gain[1], norm_shift[1])
    grad_norm2, gain_one, shift_one = back_two(matmul_right_t(grad_packed, full_qkv))
    grad_one = grad_two + grad_norm2
    grad_ffn1 = (0.5 * grad_one).astype(jnp.bfloat16)
    _, back_silu1 = jax.vjp(jax.nn.silu, up_one)
    grad_up1 = back_silu1(matmul_right_t(grad_ffn1, full_out1))[0].astype(jnp.bfloat16)
    _, back_one = jax.vjp(layer_norm, start_in, norm_gain[0], norm_shift[0])
    grad_norm1, gain_zero, shift_zero = back_one(matmul_right_t(grad_up1, full_in1))
    grad_start = grad_one + grad_norm1
    grad_frames = jnp.where(
        masked[..., None], 0.0, grad_start.reshape(utterances, frames, model_width)
    )
    wide_pairs = (
        (act_one, grad_up1),
        (act_two, grad_packed),
        (attn_low, grad_att),
        (act_three, grad_joined),
        (act_four, grad_conv),
        (act_five, grad_up2),
    )
    wide = lax.psum_scatter(
        jnp.concatenate(
            [matmul_left_t(left_side, right_side) for left_side, right_side in wide_pairs], axis=1
        ).astype(jnp.bfloat16),
        "seq",
        scatter_dimension=0,
        tiled=True,
    ).astype(jnp.float32)
    tall_pairs = ((hid_one, grad_ffn1), (hid_two, grad_ffn2))
    tall = lax.psum_scatter(
        jnp.concatenate(
            [matmul_left_t(left_side, right_side) for left_side, right_side in tall_pairs], axis=1
        ).astype(jnp.bfloat16),
        "seq",
        scatter_dimension=0,
        tiled=True,
    ).astype(jnp.float32)
    hidden_width = w_in1.shape[1]
    column_cuts = [
        hidden_width,
        3 * model_width,
        model_width,
        2 * model_width,
        model_width,
        hidden_width,
    ]
    wide_parts = []
    column_start = 0
    for column_width in column_cuts:
        wide_parts.append(wide[:, column_start : column_start + column_width])
        column_start = column_start + column_width
    grad_in1, grad_qkv, grad_attn, grad_point1, grad_point2, grad_in2 = wide_parts
    grad_out1 = tall[:, :model_width]
    grad_out2 = tall[:, model_width:]
    grad_norms = jnp.stack(
        [
            jnp.stack([gain_zero, shift_zero]),
            jnp.stack([gain_one, shift_one]),
            jnp.stack([gain_two, shift_two]),
            jnp.stack([gain_three, shift_three]),
            jnp.stack([gain_four, shift_four]),
            jnp.stack([gain_five, shift_five]),
        ]
    )
    grad_norms, grad_kernel, grad_slope = (
        lax.psum(grad_norms.astype(jnp.bfloat16), "seq").astype(jnp.float32),
        lax.psum(grad_kernel.astype(jnp.bfloat16), "seq").astype(jnp.float32),
        lax.psum(grad_slope.astype(jnp.bfloat16), "seq").astype(jnp.float32),
    )
    block_out = result.astype(jnp.bfloat16).reshape(utterances, frames, model_width)
    return (
        block_out,
        grad_frames,
        grad_in1,
        grad_out1,
        grad_qkv,
        grad_attn,
        grad_point1,
        grad_point2,
        grad_in2,
        grad_out2,
        grad_norms,
        grad_kernel,
        grad_slope,
    )


def place():
    seq, dp = lax.axis_index("seq"), lax.axis_index("dp")
    return seq // 2, lax.rem(seq, 2), dp // 2, lax.rem(dp, 2)


def device(z, x, y, core):
    return (z * 2 + x, y * 2 + core)


def z_partners(z):
    return (z + 1 - 2 * lax.rem(z, 2), lax.rem(z + 2, 4), 3 - z)


def remote(source, target, send, recv, where):
    return pltpu.make_async_remote_copy(
        src_ref=source,
        dst_ref=target,
        send_sem=send,
        recv_sem=recv,
        device_id=where,
        device_id_type=MESH,
    )


def greet(partners, waits):
    barrier = pltpu.get_barrier_semaphore()
    for partner in partners:
        pl.semaphore_signal(barrier, inc=1, device_id=partner, device_id_type=MESH)
    pl.semaphore_wait(barrier, waits)


def utterance_of(z, x, core):
    return lax.rem(z, 2) * 4 + x * 2 + core


def home_of(utterance, y, group):
    return device(2 * group + utterance // 4, lax.rem(utterance // 2, 2), y, lax.rem(utterance, 2))


def bits_of(s):
    return s // 4, lax.rem(s // 2, 2), lax.rem(s, 2)


def flipped(bits, r):
    flips = (r // 4, r // 2 % 2, r % 2)
    return [1 - b if f else b for b, f in zip(bits, flips)]


def utterance_in_round(seq, r):
    b2, b1, b0 = bits_of(seq)
    out = flipped((b1, b0, b2), r)
    return out[0] * 4 + out[1] * 2 + out[2]


def seq_in_round(utterance, r):
    t2, t1, t0 = flipped(bits_of(utterance), r)
    return t0 * 4 + t2 * 2 + t1


def exchange_kernel(count, to_utterances, *refs):
    ins, outs = refs[:count], refs[count : 2 * count]
    send, recv, own = refs[2 * count :]
    z, x, y, core = place()
    seq = z * 2 + x
    group = z // 2
    utterance = utterance_of(z, x, core)
    same = group == core
    seqs = [seq_in_round(utterance, r) for r in range(8)]
    mates = [utterance_in_round(seq, r) for r in range(8)]
    sources = [device(s // 2, lax.rem(s, 2), y, group) for s in seqs]
    homes = [home_of(u, y, core) for u in mates]
    if to_utterances:
        targets, givers, mine, blocks = homes, sources, seq, mates
    else:
        targets, givers, mine, blocks = sources, homes, utterance, seqs
    barrier = pltpu.get_barrier_semaphore()
    for r in range(8):
        if r == 0:

            @pl.when(jnp.logical_not(same))
            def _():
                pl.semaphore_signal(barrier, inc=1, device_id=givers[0], device_id_type=MESH)
        else:
            pl.semaphore_signal(barrier, inc=1, device_id=givers[r], device_id_type=MESH)
    pl.semaphore_wait(barrier, jnp.where(same, 7, 8))

    def copy(i, r):
        return remote(
            ins[i].at[blocks[r]], outs[i].at[mine], send.at[i, r], recv.at[i, r], targets[r]
        )

    def local(i):
        return pltpu.make_async_copy(ins[i].at[blocks[0]], outs[i].at[mine], own.at[i])

    for i in range(count):

        @pl.when(jnp.logical_not(same))
        def _():
            copy(i, 0).start()

        @pl.when(same)
        def _():
            local(i).start()

        for r in range(1, 8):
            copy(i, r).start()
    for i in range(count):

        @pl.when(jnp.logical_not(same))
        def _():
            copy(i, 0).wait()

        @pl.when(same)
        def _():
            local(i).wait()

        for r in range(1, 8):
            copy(i, r).wait()


def exchange(arrays, to_utterances, collective_id):
    count = len(arrays)
    return pl.pallas_call(
        functools.partial(exchange_kernel, count, to_utterances),
        out_shape=[jax.ShapeDtypeStruct(a.shape, a.dtype) for a in arrays],
        in_specs=[ANY] * count,
        out_specs=[ANY] * count,
        scratch_shapes=[
            pltpu.SemaphoreType.DMA((count, 8)),
            pltpu.SemaphoreType.DMA((count, 8)),
            pltpu.SemaphoreType.DMA((count,)),
        ],
        compiler_params=pltpu.CompilerParams(collective_id=collective_id, has_side_effects=True),
    )(*arrays)


def units_of(shapes):
    units = []
    for index, (rows, columns) in enumerate(shapes):
        for row in range(0, rows, 128):
            for column in range(0, columns, 1024):
                units.append((index, row, column))
    return units


ROWS = 128
HALF = 64
COLUMNS = 1024
LAGS = (0, 1, 2, 3, 5, 7, 8)
SPLIT = 384


def gather_kernel(units, count, *refs):
    shards, fulls = refs[:count], refs[count : 2 * count]
    send, recv, own = refs[2 * count :]
    z, x, y, core = place()
    zs = z_partners(z)
    over_z = [device(other, x, y, core) for other in zs]
    over_x = device(z, 1 - x, y, core)
    over_y = device(z, x, 1 - y, core)
    over_core = device(z, x, y, 1 - core)
    greet(over_z + [over_x, over_y, over_core], 6)

    def spot(unit):
        index, row, column = unit
        rows = pl.ds(row + pl.multiple_of(core * HALF, HALF), HALF)
        mine = pl.ds(column + pl.multiple_of(y * SPLIT, 128), COLUMNS - SPLIT)
        third = pl.ds(column + pl.multiple_of(y * (COLUMNS - SPLIT), 128), SPLIT)
        return shards[index], fulls[index], rows, mine, third, pl.ds(column, COLUMNS)

    def first(u):
        shard, full, rows, mine, _, _ = spot(units[u])
        source = shard.at[rows, mine]
        out = [pltpu.make_async_copy(source, full.at[z, x, rows, mine], own.at[u])]
        for j in range(3):
            out.append(
                remote(source, full.at[z, x, rows, mine], send.at[u, j], recv.at[u, j], over_z[j])
            )
        return out

    def second(u):
        _, full, rows, mine, _, _ = spot(units[u])
        piece = full.at[:, x, rows, mine]
        return [remote(piece, piece, send.at[u, 3], recv.at[u, 3], over_x)]

    def third(u):
        _, full, rows, _, part, _ = spot(units[u])
        pieces = [full.at[:, 1 - x, rows, part]] + [full.at[other, x, rows, part] for other in zs]
        out = [remote(p, p, send.at[u, 4 + j], recv.at[u, 4 + j], over_y) for j, p in enumerate(pieces)]
        return out

    def fourth(u):
        _, full, rows, _, _, whole = spot(units[u])
        piece = full.at[:, :, rows, whole]
        return [remote(piece, piece, send.at[u, 5], recv.at[u, 5], over_core)]

    stages = (first, second, third, fourth)
    last = len(units)
    for step in range(last + len(stages)):
        for depth, stage in enumerate(stages):
            u = step - depth
            if depth > 0 and 0 <= u < last:
                for copy in stages[depth - 1](u):
                    copy.wait()
            if 0 <= u < last:
                for copy in stage(u):
                    copy.start()
        u = step - len(stages)
        if 0 <= u < last:
            for copy in stages[-1](u):
                copy.wait()


def gather(shards, collective_id):
    count = len(shards)
    shapes = [s.shape for s in shards]
    units = units_of(shapes)
    fulls = pl.pallas_call(
        functools.partial(gather_kernel, units, count),
        out_shape=[jax.ShapeDtypeStruct((4, 2) + s, BF16) for s in shapes],
        in_specs=[ANY] * count,
        out_specs=[ANY] * count,
        scratch_shapes=[
            pltpu.SemaphoreType.DMA((len(units), 6)),
            pltpu.SemaphoreType.DMA((len(units), 6)),
            pltpu.SemaphoreType.DMA((len(units),)),
        ],
        compiler_params=pltpu.CompilerParams(collective_id=collective_id, has_side_effects=True),
    )(*shards)
    return [f.reshape(8 * s[0], s[1]) for f, s in zip(fulls, shapes)]


def scatter_kernel(units, count, *refs):
    grads, outs = refs[:count], refs[count : 2 * count]
    (mine, core_in, x_in, z_in, load, s_core, r_core, s_x, r_x, s_z, r_z, s_far, r_far, s_near, r_near, local) = refs[
        2 * count :
    ]
    z, x, y, core = place()
    group = z // 2
    z_other = z + 1 - 2 * lax.rem(z, 2)
    over_core = device(z, x, y, 1 - core)
    over_x = device(z, 1 - x, y, core)
    over_z = device(z_other, x, y, core)
    far = device(3 - z, x, y, group)
    keeps = core == group
    barrier = pltpu.get_barrier_semaphore()
    for partner in (over_core, over_x, over_z):
        pl.semaphore_signal(barrier, inc=1, device_id=partner, device_id_type=MESH)
    far_givers = [device(3 - z, x, y, 0), device(3 - z, x, y, 1)]

    @pl.when(jnp.logical_not(keeps))
    def _():
        for giver in far_givers:
            pl.semaphore_signal(barrier, inc=1, device_id=giver, device_id_type=MESH)

    pl.semaphore_wait(barrier, 4)

    half = pl.multiple_of(core * HALF, HALF)
    other_half = pl.multiple_of((1 - core) * HALF, HALF)

    def core_copy(u):
        index, row, column = units[u]
        source = grads[index].at[:, :, pl.ds(row + other_half, HALF), pl.ds(column, COLUMNS)]
        return remote(source, core_in.at[u % 2], s_core.at[u % 2], r_core.at[u % 2], over_core)

    def load_copy(u):
        index, row, column = units[u]
        source = grads[index].at[:, :, pl.ds(row + half, HALF), pl.ds(column, COLUMNS)]
        return pltpu.make_async_copy(source, mine.at[u % 5], load.at[u % 2])

    def x_copy(u):
        return remote(
            mine.at[u % 5, :, 1 - x], x_in.at[u % 4], s_x.at[u % 4], r_x.at[u % 4], over_x
        )

    def z_copy(u, part):
        target_z = z_other if part == 0 else 3 - z_other
        return remote(
            mine.at[u % 5, target_z, x],
            z_in.at[u % 4, part],
            s_z.at[u % 4, part],
            r_z.at[u % 4, part],
            over_z,
        )

    def far_copy(u):
        index, row, column = units[u]
        target = outs[index].at[pl.ds(row + half, HALF), pl.ds(column, COLUMNS)]
        return remote(
            mine.at[u % 5, 3 - z, x], target, s_far.at[u % 2], r_far.at[u, core], far
        )

    def far_arrival(u, giver):
        index, row, column = units[u]
        target = outs[index].at[pl.ds(row + giver * HALF, HALF), pl.ds(column, COLUMNS)]
        return remote(
            mine.at[u % 5, 3 - z, x], target, s_far.at[u % 2], r_far.at[u, giver], far
        )

    def near_target(u):
        index, row, column = units[u]
        return outs[index].at[pl.ds(row + half, HALF), pl.ds(column, COLUMNS)]

    def near_copy(u):
        return remote(
            mine.at[u % 5, z, x], near_target(u), s_near.at[u % 2], r_near.at[u], over_core
        )

    def near_arrival(u):
        index, row, column = units[u]
        target = outs[index].at[pl.ds(row + other_half, HALF), pl.ds(column, COLUMNS)]
        return remote(
            mine.at[u % 5, z, x], target, s_near.at[u % 2], r_near.at[u], over_core
        )

    def near_local(u):
        return pltpu.make_async_copy(mine.at[u % 5, z, x], near_target(u), local.at[u % 2])

    def add(into, other):
        into[...] = (into[...].astype(F32) + other[...].astype(F32)).astype(BF16)

    def stage0(u):
        load_copy(u).start()
        core_copy(u).start()

    def stage1(u):
        load_copy(u).wait()
        core_copy(u).wait()

        @pl.loop(0, 4)
        def _(i):
            add(mine.at[u % 5, i, 1 - x], core_in.at[u % 2, i, 1 - x])

        x_copy(u).start()

        @pl.loop(0, 4)
        def _(i):
            add(mine.at[u % 5, i, x], core_in.at[u % 2, i, x])

    def stage2(u):
        x_copy(u).wait()
        for part, target_z in ((0, z_other), (1, 3 - z_other)):
            add(mine.at[u % 5, target_z, x], x_in.at[u % 4, target_z])
            z_copy(u, part).start()
        for target_z in (z, 3 - z):
            add(mine.at[u % 5, target_z, x], x_in.at[u % 4, target_z])

    def stage3(u):
        z_copy(u, 0).wait()
        z_copy(u, 1).wait()
        add(mine.at[u % 5, 3 - z, x], z_in.at[u % 4, 1])
        far_copy(u).start()
        add(mine.at[u % 5, z, x], z_in.at[u % 4, 0])

        @pl.when(keeps)
        def _():
            near_local(u).start()

        @pl.when(jnp.logical_not(keeps))
        def _():
            near_copy(u).start()

    def stage4(u):
        far_copy(u).wait_send()

        @pl.when(keeps)
        def _():
            near_local(u).wait()
            near_arrival(u).wait_recv()

        @pl.when(jnp.logical_not(keeps))
        def _():
            near_copy(u).wait_send()

    last = len(units)
    order = ((stage1, 1), (stage0, 0), (stage2, 2), (stage3, 3), (stage4, 4))
    for step in range(last + 4):
        for stage, depth in order:
            if 0 <= step - depth < last:
                stage(step - depth)

    @pl.when(jnp.logical_not(keeps))
    def _():
        for u in range(last):
            far_arrival(u, 0).wait_recv()
            far_arrival(u, 1).wait_recv()


def scatter(grads, collective_id):
    count = len(grads)
    shapes = [(g.shape[0] // 8, g.shape[1]) for g in grads]
    units = units_of(shapes)
    dma = pltpu.SemaphoreType.DMA
    return pl.pallas_call(
        functools.partial(scatter_kernel, units, count),
        out_shape=[jax.ShapeDtypeStruct(s, BF16) for s in shapes],
        in_specs=[ANY] * count,
        out_specs=[ANY] * count,
        scratch_shapes=[
            pltpu.VMEM((5, 4, 2, HALF, COLUMNS), BF16),
            pltpu.VMEM((2, 4, 2, HALF, COLUMNS), BF16),
            pltpu.VMEM((4, 4, HALF, COLUMNS), BF16),
            pltpu.VMEM((4, 2, HALF, COLUMNS), BF16),
            dma((2,)),
            dma((2,)),
            dma((2,)),
            dma((4,)),
            dma((4,)),
            dma((4, 2)),
            dma((4, 2)),
            dma((2,)),
            dma((len(units), 2)),
            dma((2,)),
            dma((len(units),)),
            dma((2,)),
        ],
        compiler_params=pltpu.CompilerParams(
            collective_id=collective_id, has_side_effects=True, vmem_limit_bytes=40 * 2**20
        ),
    )(*[g.reshape((4, 2) + s) for g, s in zip(grads, shapes)])


def blocks(rows, size):
    def run(body):
        @pl.loop(0, rows // size)
        def _(i):
            body(pl.ds(pl.multiple_of(i * size, size), size))

    return run


def normalise(v, norm, i):
    average = jnp.mean(v, axis=-1, keepdims=True)
    centred = v - average
    variance = jnp.mean(centred * centred, axis=-1, keepdims=True)
    return centred * lax.rsqrt(variance + EPSILON) * norm[i, 0:1, :] + norm[i, 1:2, :]


TILE = 256


def sigmoid(v):
    return 0.5 * jnp.tanh(0.5 * v) + 0.5


def silu(v):
    return v * sigmoid(v)


def times_unit(left, weight, emit, poll):
    unit, loads = weight
    for n in range(COLUMNS // TILE):
        columns = pl.ds(n * TILE, TILE)
        loads[n].wait()
        emit(columns, jnp.dot(left[...], unit[:, :, :, columns].reshape(COLUMNS, TILE), preferred_element_type=F32))
        poll()


def score_block(q, k, slope_row, first, live_keys):
    shape = (q.shape[0], k.shape[0])
    scores = lax.dot_general(q, k, (((1,), (1,)), ((), ())), preferred_element_type=F32)
    rows = lax.broadcasted_iota(jnp.int32, shape, 0) + first
    keys = lax.broadcasted_iota(jnp.int32, shape, 1)
    distance = jnp.abs(rows - keys).astype(F32) * (1.0 / k.shape[0])
    scores = scores * (q.shape[1] ** -0.5) - slope_row * distance
    return jnp.where(keys.astype(F32) < live_keys, scores, NEGATIVE), distance


def softmax_block(scores):
    top = jnp.max(scores, axis=-1, keepdims=True)
    expd = jnp.exp(scores - top)
    return expd / jnp.sum(expd, axis=-1, keepdims=True)


QUERIES = 128
BLOCK = 32


def forward_kernel(units, names, *refs):
    r = dict(zip(names, refs))
    norm, taps, slope = r["norm"], r["taps"], r["slope"]
    length, width = r["x"].shape[1:]
    heads = slope.shape[0]
    head_dim = width // heads
    z, x, y, core = place()
    seq, group = z * 2 + x, z // 2
    utterance = utterance_of(z, x, core)
    same = group == core
    zs = z_partners(z)
    over_z = [device(other, x, y, core) for other in zs]
    over_x = device(z, 1 - x, y, core)
    over_y = device(z, x, 1 - y, core)
    over_core = device(z, x, y, 1 - core)
    mates = [utterance_in_round(seq, i) for i in range(8)]
    givers = [device(s // 2, lax.rem(s, 2), y, group) for s in [seq_in_round(utterance, i) for i in range(8)]]
    targets = [home_of(u, y, core) for u in mates]
    barrier = pltpu.get_barrier_semaphore()

    @pl.when(jnp.logical_not(same))
    def _():
        pl.semaphore_signal(barrier, inc=1, device_id=givers[0], device_id_type=MESH)

    for partner in givers[1:] + [over_z[0], over_z[2], over_x, over_y, over_core]:
        pl.semaphore_signal(barrier, inc=1, device_id=partner, device_id_type=MESH)
    pl.semaphore_wait(barrier, jnp.where(same, 12, 13))

    swaps = (("start", "h0"), ("lens", "lens_here"), ("cot", "cot_out"))

    def swap(i, j):
        source, target = r[swaps[i][0]], r[swaps[i][1]]
        return remote(source.at[mates[j]], target.at[seq], r["swap_send"].at[i, j], r["swap_recv"].at[i, j], targets[j])

    def swap_local(i):
        source, target = r[swaps[i][0]], r[swaps[i][1]]
        return pltpu.make_async_copy(source.at[mates[0]], target.at[seq], r["swap_own"].at[i])

    def swap_start(i, j):
        if j > 0:
            swap(i, j).start()
            return

        @pl.when(jnp.logical_not(same))
        def _():
            swap(i, 0).start()

        @pl.when(same)
        def _():
            swap_local(i).start()

    def swap_wait(i):
        @pl.when(jnp.logical_not(same))
        def _():
            swap(i, 0).wait()

        @pl.when(same)
        def _():
            swap_local(i).wait()

        for j in range(1, 8):
            swap(i, j).wait()

    send, recv, own = r["send"], r["recv"], r["own"]
    shards, fulls = r["shards"], r["fulls"]

    def spot(unit):
        index, row, column = unit
        rows = pl.ds(row + pl.multiple_of(core * HALF, HALF), HALF)
        mine = pl.ds(column + pl.multiple_of(y * SPLIT, 128), COLUMNS - SPLIT)
        third = pl.ds(column + pl.multiple_of(y * (COLUMNS - SPLIT), 128), SPLIT)
        return shards[index], fulls[index], rows, mine, third, pl.ds(column, COLUMNS)

    middle = (z == 1) | (z == 2)
    near_pair, far_pair = pl.ds(2 * (z // 2), 2), pl.ds(2 - 2 * (z // 2), 2)

    class Along:
        def __init__(self, copy, sends, gets):
            self.copy, self.sends, self.gets = copy, sends, gets

        def start(self):
            @pl.when(self.sends)
            def _():
                self.copy.start()

        def wait(self):
            @pl.when(self.sends)
            def _():
                self.copy.wait_send()

            @pl.when(self.gets)
            def _():
                self.copy.wait_recv()

    def first(u):
        shard, full, rows, mine, _, _ = spot(units[u])
        every = pl.ds(units[u][2], COLUMNS)
        return [
            remote(shard.at[rows, mine], full.at[z, x, rows, mine], send.at[u, 0], recv.at[u, 0], over_z[0]),
            pltpu.make_async_copy(shard.at[rows, every], full.at[z, x, rows, every], own.at[u]),
        ]

    def across(u):
        _, full, rows, mine, _, _ = spot(units[u])
        piece = full.at[near_pair, x, rows, mine]
        return [Along(remote(piece, piece, send.at[u, 1], recv.at[u, 1], over_z[2]), middle, middle)]

    def outward(u):
        _, full, rows, mine, _, _ = spot(units[u])
        piece = full.at[far_pair, x, rows, mine]
        copy = remote(piece, piece, send.at[u, 2], recv.at[u, 2], over_z[0])
        return [Along(copy, middle, jnp.logical_not(middle))]

    def second(u):
        _, full, rows, mine, _, _ = spot(units[u])
        piece = full.at[:, x, rows, mine]
        return [remote(piece, piece, send.at[u, 3], recv.at[u, 3], over_x)]

    def third(u):
        _, full, rows, _, part, _ = spot(units[u])
        pieces = [full.at[:, 1 - x, rows, part]] + [full.at[other, x, rows, part] for other in zs]
        out = [remote(p, p, send.at[u, 4 + j], recv.at[u, 4 + j], over_y) for j, p in enumerate(pieces)]
        return out

    def fourth(u):
        _, full, rows, _, _, whole = spot(units[u])
        piece = full.at[:, :, rows, whole]
        return [remote(piece, piece, send.at[u, 8], recv.at[u, 8], over_core)]

    stages = (first, across, outward, second, third, fourth)
    last = len(units)
    done = [0]

    actions = []
    ends = {}

    def move(u, depth):
        def act_on():
            if depth > 0:
                for copy in stages[depth - 1](u):
                    copy.wait()
            if depth < len(stages):
                for copy in stages[depth](u):
                    copy.start()

        return act_on

    for step in range(last + LAGS[-1]):
        for depth, lag in enumerate(LAGS):
            if 0 <= step - lag < last:
                actions.append(move(step - lag, depth))
                if depth == len(stages):
                    ends[step - lag] = len(actions)
        if 12 <= step < 20:
            actions.append(functools.partial(swap_start, 2, step - 12))

    def poll(count=1):
        for _ in range(count):
            if done[0] < len(actions):
                actions[done[0]]()
                done[0] += 1

    taken = [0]

    def weight():
        u = taken[0]
        taken[0] += 1
        while done[0] < ends[u]:
            poll()
        index, row, column = units[u]
        loads = []
        for n in range(COLUMNS // TILE):
            source = fulls[index].at[:, :, pl.ds(row, ROWS), pl.ds(column + n * TILE, TILE)]
            target = r["unit"].at[u % 2, :, :, :, pl.ds(n * TILE, TILE)]
            copy = pltpu.make_async_copy(source, target, r["load"].at[u % 2, n])
            copy.start()
            loads.append(copy)
        return r["unit"].at[u % 2], loads

    kept = []

    def keep(source, target):
        copy = pltpu.make_async_copy(source, target, r["kept"].at[len(kept)])
        copy.start()
        kept.append(copy)

    xs, act, acc = r["x"], r["act"], r["acc"]
    poll()
    for j in range(8):
        swap_start(0, j)
    for j in range(8):
        swap_start(1, j)
    poll(4)
    swap_wait(0)

    @blocks(length, BLOCK)
    def _(rows):
        xs[0, rows, :] = r["h0"][rows.start // 64, pl.ds(pl.multiple_of(lax.rem(rows.start, 64), BLOCK), BLOCK), :].astype(F32)
        act[rows, :] = normalise(xs[0, rows, :], norm, 0).astype(BF16)

    keep(r["h0"], r["h0_out"])

    def feed_forward(x_in, x_out, up, up_out):
        hidden = r["hidden"]
        for p in range(4):
            unit, loads = weight()

            for n in range(COLUMNS // TILE):
                columns = pl.ds(n * TILE, TILE)
                loads[n].wait()
                value = jnp.dot(act[...], unit[:, :, :, columns].reshape(COLUMNS, TILE), preferred_element_type=F32)
                up[p, :, columns] = value.astype(BF16)
                value = silu(value).astype(BF16)
                for t in range(2 * n, 2 * n + 2):
                    place_at = pl.ds((2 * p + t // 4) * 128, 128)
                    hidden[t % 4, :, place_at] = value[:, (t - 2 * n) * 128 : (t - 2 * n + 1) * 128]
                poll()

            keep(up.at[p], up_out.at[:, pl.ds(p * COLUMNS, COLUMNS)])
        for q in range(4):
            def emit(columns, value, q=q):
                if q == 0:
                    acc[:, columns] = value
                else:
                    acc[:, columns] = acc[:, columns] + value

            times_unit(hidden.at[q], weight(), emit, poll)

        @blocks(length, BLOCK)
        def _(rows):
            xs[x_out, rows, :] = xs[x_in, rows, :] + 0.5 * acc[rows, :]

    feed_forward(0, 1, r["up"], r["u1_out"])
    keep(xs.at[1], r["x1_out"])

    @blocks(length, BLOCK)
    def _(rows):
        act[rows, :] = normalise(xs[1, rows, :], norm, 1).astype(BF16)

    qkv = r["qkv"]
    for i in range(3):

        def emit(columns, value, i=i):
            qkv[i, :, columns] = value.astype(BF16)

        times_unit(act, weight(), emit, poll)
    keep(qkv, r["qkv_out"])
    swap_wait(1)
    live_count = r["lens_here"][0, 0:1, 0:1]
    keep(r["lens_here"], r["lens_out"])
    attended = r["attended"]
    for h in range(heads):
        columns = pl.ds(h * head_dim, head_dim)

        @blocks(length, QUERIES)
        def _(rows, h=h, columns=columns):
            scores, _ = score_block(
                qkv[0, rows, columns], qkv[1, :, columns], slope[h : h + 1, :], rows.start, live_count
            )
            prob = softmax_block(scores).astype(BF16)
            attended[rows, columns] = jnp.dot(prob, qkv[2, :, columns], preferred_element_type=F32).astype(BF16)

        poll(2)
    keep(attended, r["attended_out"])

    def add_to(x_in, x_out):
        def emit(columns, value):
            xs[x_out, :, columns] = xs[x_in, :, columns] + value

        return emit

    times_unit(attended, weight(), add_to(1, 2), poll)
    keep(xs.at[2], r["x2_out"])

    @blocks(length, BLOCK)
    def _(rows):
        act[rows, :] = normalise(xs[2, rows, :], norm, 2).astype(BF16)

    gates, gated = r["gates"], r["gated"]

    def emit(columns, value):
        acc[:, columns] = value
        gates[0, :, columns] = value.astype(BF16)

    times_unit(act, weight(), emit, poll)
    gated[0:8, :] = jnp.zeros((8, width), F32)
    gated[length + 8 : length + 16, :] = jnp.zeros((8, width), F32)

    def emit(columns, value):
        gates[1, :, columns] = value.astype(BF16)
        live = lax.broadcasted_iota(jnp.int32, value.shape, 0).astype(F32) < live_count
        passed = jnp.where(live, acc[:, columns] * sigmoid(value), 0.0)
        gated[pl.ds(8, length), columns] = passed.astype(BF16).astype(F32)

    times_unit(act, weight(), emit, poll)
    keep(gates, r["gates_out"])
    keep(gated, r["gated_out"])
    depth = r["depth"]

    @blocks(length, BLOCK)
    def _(rows):
        near = gated[pl.ds(pl.multiple_of(rows.start, BLOCK), BLOCK + 16), :]
        total = taps[0:1, :] * near[6 : 6 + BLOCK]
        for t in range(1, taps.shape[0]):
            total = total + taps[t : t + 1, :] * near[6 + t : 6 + t + BLOCK]
        depth[rows, :] = total
        value = normalise(total, norm, 3)
        act[rows, :] = (silu(value)).astype(BF16)

    keep(depth, r["depth_out"])
    times_unit(act, weight(), add_to(2, 3), poll)
    keep(xs.at[3], r["x3_out"])

    @blocks(length, BLOCK)
    def _(rows):
        act[rows, :] = normalise(xs[3, rows, :], norm, 4).astype(BF16)

    feed_forward(3, 4, r["up2"], r["u2_out"])
    keep(xs.at[4], r["x4_out"])

    @blocks(length, BLOCK)
    def _(rows):
        act[rows, :] = normalise(xs[4, rows, :], norm, 5).astype(BF16)

    keep(act, r["result_out"])
    swap_wait(2)
    for copy in kept:
        copy.wait()


def forward(start, lens, cot, norm, taps, slope, shards, collective_id):
    shapes = [s.shape for s in shards]
    units = units_of(shapes)
    width = norm.shape[-1]
    frames = start.shape[1]
    length = 8 * frames
    count = len(shards)
    dma = pltpu.SemaphoreType.DMA
    hidden = shapes[0][1]
    wide = lambda *lead: jax.ShapeDtypeStruct(lead + (length, width), F32)
    low = lambda *lead: jax.ShapeDtypeStruct(lead + (length, width), BF16)
    up = jax.ShapeDtypeStruct((length, hidden), BF16)
    outs = {
        "cot_out": jax.ShapeDtypeStruct(cot.shape, cot.dtype),
        "h0_out": jax.ShapeDtypeStruct(start.shape, start.dtype),
        "u1_out": up,
        "x1_out": wide(),
        "qkv_out": low(3),
        "attended_out": low(),
        "x2_out": wide(),
        "gates_out": low(2),
        "gated_out": jax.ShapeDtypeStruct((length + 16, width), F32),
        "depth_out": wide(),
        "x3_out": wide(),
        "u2_out": up,
        "x4_out": wide(),
        "result_out": low(),
        "lens_out": jax.ShapeDtypeStruct(lens.shape, lens.dtype),
    }
    scratch = {
        "h0": pltpu.VMEM(start.shape, BF16),
        "lens_here": pltpu.VMEM(lens.shape, F32),
        "x": pltpu.VMEM((5, length, width), F32),
        "act": pltpu.VMEM((length, width), BF16),
        "acc": pltpu.VMEM((length, width), F32),
        "hidden": pltpu.VMEM((4, length, width), BF16),
        "up": pltpu.VMEM((4, length, width), BF16),
        "up2": pltpu.VMEM((4, length, width), BF16),
        "qkv": pltpu.VMEM((3, length, width), BF16),
        "attended": pltpu.VMEM((length, width), BF16),
        "gates": pltpu.VMEM((2, length, width), BF16),
        "gated": pltpu.VMEM((length + 16, width), F32),
        "depth": pltpu.VMEM((length, width), F32),
        "unit": pltpu.VMEM((2, 4, 2, ROWS, COLUMNS), BF16),
        "load": dma((2, COLUMNS // TILE)),
        "swap_send": dma((3, 8)),
        "swap_recv": dma((3, 8)),
        "swap_own": dma((3,)),
        "send": dma((len(units), 9)),
        "recv": dma((len(units), 9)),
        "own": dma((len(units),)),
        "kept": dma((32,)),
    }
    names = ["start", "lens", "cot", "norm", "taps", "slope"]
    vmem = pl.BlockSpec(memory_space=pltpu.VMEM)

    def body(*refs):
        plain, rest = refs[:6], refs[6:]
        ours, rest = rest[:count], rest[count:]
        made, rest = rest[: len(outs)], rest[len(outs) :]
        fulls, rest = rest[:count], rest[count:]
        forward_kernel(
            units,
            names + list(outs) + list(scratch) + ["shards", "fulls"],
            *plain,
            *made,
            *rest,
            ours,
            fulls,
        )

    results = pl.pallas_call(
        body,
        out_shape=list(outs.values()) + [jax.ShapeDtypeStruct((4, 2) + s, BF16) for s in shapes],
        in_specs=[ANY, ANY, ANY, vmem, vmem, vmem] + [ANY] * count,
        out_specs=[ANY] * (len(outs) + count),
        scratch_shapes=list(scratch.values()),
        compiler_params=pltpu.CompilerParams(
            collective_id=collective_id, has_side_effects=True, vmem_limit_bytes=60 * 2**20
        ),
    )(start, lens, cot, norm, taps, slope, *shards)
    made = dict(zip(outs, results[: len(outs)]))
    fulls = [f.reshape(8 * s[0], s[1]) for f, s in zip(results[len(outs) :], shapes)]
    return made, fulls


def per_device(
    frames_in,
    noise,
    lengths,
    span_starts,
    w_in1,
    w_out1,
    w_qkv,
    w_attn,
    w_point1,
    w_point2,
    w_in2,
    w_out2,
    norm_params,
    kernel,
    slopes,
    cotangent,
):
    utterances, frames, width = frames_in.shape
    heads = slopes.shape[0]
    head_dim = width // heads
    length = frames * 8
    taps = kernel.shape[0]
    half_taps = taps // 2
    factor = head_dim ** (-0.5)
    frame_pos = lax.axis_index("seq") * frames + jnp.arange(frames, dtype=jnp.int32)
    span_begin = span_starts[:, :, None]
    masked = jnp.any(
        (span_begin <= frame_pos[None, None, :]) & (frame_pos[None, None, :] < span_begin + SPAN),
        axis=1,
    )
    start = jnp.where(masked[..., None], noise, frames_in)
    lens = jnp.broadcast_to(lengths.astype(F32)[:, None, None], (utterances, 8, 128))
    slope_rows = jnp.broadcast_to(slopes[:, None], (heads, length))
    shards = (w_in1, w_out1, w_qkv, w_attn, w_point1, w_point2, w_in2, w_out2)
    made, fulls = forward(start, lens, cotangent, norm_params, kernel, slope_rows, shards, 0)
    in1, out1, qkv, attn, point1, point2, in2, out2 = fulls
    gain, shift = norm_params[:, 0], norm_params[:, 1]
    h0 = made["h0_out"].reshape(length, width).astype(F32)
    cot = made["cot_out"].reshape(length, width).astype(F32)
    live_count = made["lens_out"][0, 0, 0]
    position = jnp.arange(length, dtype=jnp.int32).astype(F32)
    live = (position < live_count).astype(F32)[:, None]
    key_live = position < live_count
    u1, x1, x2, x3, u2, x4 = [made[n + "_out"].astype(F32) for n in ("u1", "x1", "x2", "x3", "u2", "x4")]
    depth, result = made["depth_out"], made["result_out"]
    a1 = layer_norm(h0, gain[0], shift[0]).astype(BF16)
    s1 = jax.nn.silu(u1).astype(BF16)
    a2 = layer_norm(x1, gain[1], shift[1]).astype(BF16)
    a3 = layer_norm(x2, gain[2], shift[2]).astype(BF16)
    c4 = swish_norm(depth, gain[3], shift[3]).astype(BF16)
    a5 = layer_norm(x3, gain[4], shift[4]).astype(BF16)
    s2 = jax.nn.silu(u2).astype(BF16)
    q, k, v = [p.reshape(length, heads, head_dim) for p in made["qkv_out"]]
    distance = jnp.abs(position[:, None] - position[None, :]) / length
    scores = jnp.einsum("qhd,khd->hqk", q, k, preferred_element_type=F32) * factor
    scores = scores - slopes[:, None, None] * distance[None]
    scores = jnp.where(key_live[None, None, :], scores, NEGATIVE)
    top = jnp.max(scores, axis=-1, keepdims=True)
    expd = jnp.exp(scores - top)
    prob = expd / jnp.sum(expd, axis=-1, keepdims=True)
    prob_low = prob.astype(BF16)
    ob = made["attended_out"]
    o = ob.astype(F32).reshape(length, heads, head_dim)
    z = jnp.concatenate([made["gates_out"][0], made["gates_out"][1]], axis=1).astype(F32)
    padded = made["gated_out"][8 - half_taps : length + 8 + half_taps]
    _, back = jax.vjp(layer_norm, x4, gain[5], shift[5])
    dx4, gain5, shift5 = back(cot)
    df2 = (0.5 * dx4).astype(BF16)
    _, back = jax.vjp(jax.nn.silu, u2)
    du2 = back(matmul_right_t(df2, out2))[0].astype(BF16)
    _, back = jax.vjp(layer_norm, x3, gain[4], shift[4])
    dn, gain4, shift4 = back(matmul_right_t(du2, in2))
    dx3 = dx4 + dn
    dc = dx3.astype(BF16)
    _, back = jax.vjp(swish_norm, depth, gain[3], shift[3])
    dd, gain3, shift3 = back(matmul_right_t(dc, point2))
    dd = dd.astype(BF16)
    dd_padded = jnp.pad(dd, ((half_taps, half_taps), (0, 0)))
    dg = jnp.zeros((length, width), F32)
    kernel_rows = []
    for t in range(taps):
        lower = 2 * half_taps - t
        dg = dg + kernel[t] * dd_padded[lower : lower + length].astype(F32)
        kernel_rows.append(jnp.sum(dd.astype(F32) * padded[t : t + length].astype(F32), axis=0))
    _, back = jax.vjp(lambda joined: glu_gate(joined, live), z)
    dz = back(dg)[0].astype(BF16)
    _, back = jax.vjp(layer_norm, x2, gain[2], shift[2])
    dn, gain2, shift2 = back(matmul_right_t(dz, point1))
    dx2 = dx3 + dn
    da = dx2.astype(BF16)
    do = matmul_right_t(da, attn).astype(BF16).reshape(length, heads, head_dim)
    delta = jnp.sum(do.astype(F32) * o, axis=-1)
    dp = jnp.einsum("qhd,khd->hqk", do, v, preferred_element_type=F32)
    ds_exact = prob * (dp - delta.T[..., None])
    dslopes = -jnp.sum(ds_exact * distance[None], axis=(1, 2))
    ds = ds_exact.astype(BF16)
    dq = jnp.einsum("hqk,khd->qhd", ds, k, preferred_element_type=F32) * factor
    dk = jnp.einsum("hqk,qhd->khd", ds, q, preferred_element_type=F32) * factor
    dv = jnp.einsum("hqk,qhd->khd", prob_low, do, preferred_element_type=F32)
    dqkv = jnp.stack([dq, dk, dv], axis=1).astype(BF16).reshape(length, 3 * width)
    _, back = jax.vjp(layer_norm, x1, gain[1], shift[1])
    dn, gain1, shift1 = back(matmul_right_t(dqkv, qkv))
    dx1 = dx2 + dn
    df1 = (0.5 * dx1).astype(BF16)
    _, back = jax.vjp(jax.nn.silu, u1)
    du1 = back(matmul_right_t(df1, out1))[0].astype(BF16)
    _, back = jax.vjp(layer_norm, h0, gain[0], shift[0])
    dn, gain0, shift0 = back(matmul_right_t(du1, in1))
    dh0 = (dx1 + dn).astype(BF16)
    pairs = (
        (a1, du1),
        (s1, df1),
        (a2, dqkv),
        (ob, da),
        (a3, dz),
        (c4, dc),
        (a5, du2),
        (s2, df2),
    )
    grads = scatter([matmul_left_t(a, b).astype(BF16) for a, b in pairs], 2)
    small = jnp.concatenate(
        [
            jnp.stack([gain0, shift0, gain1, shift1, gain2, shift2, gain3, shift3, gain4, shift4, gain5, shift5]),
            jnp.stack(kernel_rows),
            jnp.pad(dslopes, (0, width - heads))[None],
            jnp.zeros((14, width), F32),
        ]
    ).astype(BF16)
    small = jnp.broadcast_to(small[None], (8,) + small.shape)
    block_out, dframes, small = exchange(
        (result.reshape(8, frames, width), dh0.reshape(8, frames, width), small), False, 3
    )
    small = jnp.sum(small.astype(F32), axis=0)
    grad_frames = jnp.where(masked[..., None], 0.0, dframes.astype(F32))
    return (
        block_out,
        grad_frames,
        *[grad.astype(F32) for grad in grads],
        small[:12].reshape(6, 2, width),
        small[12:17],
        small[17, :heads],
    )


def solution(mesh):
    in_specs = (
        P("dp", "seq", None),
        P("dp", "seq", None),
        P("dp"),
        P("dp", None),
        P("seq", None),
        P("seq", None),
        P("seq", None),
        P("seq", None),
        P("seq", None),
        P("seq", None),
        P("seq", None),
        P("seq", None),
        P(),
        P(),
        P(),
        P("dp", "seq", None),
    )
    out_specs = (
        P("dp", "seq", None),
        P("dp", "seq", None),
        P(("dp", "seq"), None),
        P(("dp", "seq"), None),
        P(("dp", "seq"), None),
        P(("dp", "seq"), None),
        P(("dp", "seq"), None),
        P(("dp", "seq"), None),
        P(("dp", "seq"), None),
        P(("dp", "seq"), None),
        P("dp", None, None),
        P("dp", None),
        P("dp"),
    )
    grouped = mesh.shape["seq"] == 8 and mesh.shape["dp"] == 4
    return jax.shard_map(
        per_device if grouped else per_device_any, mesh=mesh, in_specs=in_specs, out_specs=out_specs, check_vma=False
    )
```

```python
import functools
import types

import jax
import jax.numpy as jnp
from jax import lax
from jax.experimental import pallas as pl
from jax.experimental.pallas import tpu as pltpu
from jax.sharding import PartitionSpec as P

MESH = pl.DeviceIdType.MESH
BF16 = jnp.bfloat16
F32 = jnp.float32
ANY = pl.BlockSpec(memory_space=pl.ANY)

SPAN = 10


EPSILON = 1e-05
NEGATIVE = -1e30


def padded_2(shard, sides, width):
    for axis, dim in sides:
        peers, length = (lax.axis_size(axis), shard.shape[dim])
        up = [(i, (i + 1) % peers) for i in range(peers - 1)]
        down = [(j, i) for i, j in up]
        last = lax.slice_in_dim(shard, length - width, length, axis=dim)
        initial = lax.slice_in_dim(shard, 0, width, axis=dim)
        before = lax.ppermute(last, axis, up)
        after = lax.ppermute(initial, axis, down)
        shard = jnp.concatenate([before, shard, after], axis=dim)
    return shard


def layer_norm(inputs, gain_vec, shift_vec):
    average = jnp.mean(inputs, axis=-1, keepdims=True)
    centred = inputs - average
    variance = jnp.mean(centred * centred, axis=-1, keepdims=True)
    return centred * lax.rsqrt(variance + EPSILON) * gain_vec + shift_vec


def swish_norm(inputs, gain_vec, shift_vec):
    return jax.nn.silu(layer_norm(inputs, gain_vec, shift_vec))


def glu_gate(joined, live_rows):
    half_width = joined.shape[-1] // 2
    return joined[..., :half_width] * jax.nn.sigmoid(joined[..., half_width:]) * live_rows


def matmul(left_side, right_side):
    return jnp.dot(left_side, right_side, preferred_element_type=jnp.float32)


def matmul_right_t(left_side, right_side):
    return lax.dot_general(
        left_side, right_side, (((1,), (1,)), ((), ())), preferred_element_type=jnp.float32
    )


def matmul_left_t(left_side, right_side):
    return lax.dot_general(
        left_side, right_side, (((0,), (0,)), ((), ())), preferred_element_type=jnp.float32
    )


def block_scores(queries, keys, query_pos, key_pos, key_live, slopes, seq_length):
    factor = queries.shape[-1] ** (-0.5)
    scores = (
        jnp.einsum("uqhd,ukhd->uhqk", queries, keys, preferred_element_type=jnp.float32) * factor
    )
    distance = jnp.abs(query_pos[:, None] - key_pos[None, :]).astype(jnp.float32) / seq_length
    scores = scores - slopes[None, :, None, None] * distance[None, None]
    return (jnp.where(key_live[:, None, None, :], scores, NEGATIVE), distance)


def per_device_any(
    frames_in,
    noise,
    lengths,
    span_starts,
    w_in1,
    w_out1,
    w_qkv,
    w_attn,
    w_point1,
    w_point2,
    w_in2,
    w_out2,
    norm_params,
    kernel,
    slopes,
    cotangent,
):
    utterances, frames, model_width = frames_in.shape
    head_count = slopes.shape[0]
    head_dim = model_width // head_count
    row_count = utterances * frames
    tap_count = kernel.shape[0]
    half_taps = tap_count // 2
    factor = head_dim ** (-0.5)
    seq_length = frames * lax.axis_size("seq")
    first_frame = lax.axis_index("seq") * frames
    frame_pos = first_frame + jnp.arange(frames, dtype=jnp.int32)
    live_mask = frame_pos[None, :] < lengths[:, None]
    live_rows = live_mask.astype(jnp.float32).reshape(row_count, 1)
    span_begin = span_starts[:, :, None]
    masked = jnp.any(
        (span_begin <= frame_pos[None, None, :]) & (frame_pos[None, None, :] < span_begin + SPAN),
        axis=1,
    )
    start_in = (
        jnp.where(masked[..., None], noise, frames_in)
        .astype(jnp.float32)
        .reshape(row_count, model_width)
    )
    norm_gain = norm_params[:, 0]
    norm_shift = norm_params[:, 1]
    shards = (w_in1, w_out1, w_qkv, w_attn, w_point1, w_point2, w_in2, w_out2)
    gathered = (
        lax.all_gather(shards[0], "seq", axis=0, tiled=True),
        lax.all_gather(shards[1], "seq", axis=0, tiled=True),
        lax.all_gather(shards[2], "seq", axis=0, tiled=True),
        lax.all_gather(shards[3], "seq", axis=0, tiled=True),
        lax.all_gather(shards[4], "seq", axis=0, tiled=True),
        lax.all_gather(shards[5], "seq", axis=0, tiled=True),
        lax.all_gather(shards[6], "seq", axis=0, tiled=True),
        lax.all_gather(shards[7], "seq", axis=0, tiled=True),
    )
    full_in1, full_out1, full_qkv, full_attn, full_point1, full_point2, full_in2, full_out2 = (
        gathered
    )
    act_one = layer_norm(start_in, norm_gain[0], norm_shift[0]).astype(jnp.bfloat16)
    up_one = matmul(act_one, full_in1)
    hid_one = jax.nn.silu(up_one).astype(jnp.bfloat16)
    ffn_one = matmul(hid_one, full_out1)
    resid_one = start_in + 0.5 * ffn_one
    act_two = layer_norm(resid_one, norm_gain[1], norm_shift[1]).astype(jnp.bfloat16)
    packed = (
        matmul(act_two, full_qkv)
        .astype(jnp.bfloat16)
        .reshape(utterances, frames, 3, head_count, head_dim)
    )
    queries = packed[:, :, 0]
    keys = packed[:, :, 1]
    values = packed[:, :, 2]
    row_max = jnp.full((utterances, head_count, frames), NEGATIVE, jnp.float32)
    key_blk = lax.all_gather(keys, "seq", axis=1, tiled=True)
    value_blk = lax.all_gather(values, "seq", axis=1, tiled=True)
    amount = key_blk.shape[1]
    key_pos = jnp.arange(amount, dtype=jnp.int32)
    key_live = key_pos[None, :] < lengths[:, None]
    scores, distance = block_scores(
        queries, key_blk, frame_pos, key_pos, key_live, slopes, seq_length
    )
    new_max = jnp.maximum(row_max, jnp.max(scores, axis=-1))
    expd = jnp.exp(scores - new_max[..., None])
    row_sum = jnp.sum(expd, axis=-1)
    update = jnp.einsum(
        "uhqk,ukhd->uqhd", expd.astype(jnp.bfloat16), value_blk, preferred_element_type=jnp.float32
    )
    partial_value = update
    row_max, row_sum, partial_value = (new_max, row_sum, partial_value)
    attn_out = partial_value / jnp.transpose(row_sum, (0, 2, 1))[..., None]
    log_total = jnp.transpose(row_max + jnp.log(row_sum), (0, 2, 1))
    attn_low = attn_out.astype(jnp.bfloat16).reshape(row_count, model_width)
    attended = matmul(attn_low, full_attn)
    resid_two = resid_one + attended
    act_three = layer_norm(resid_two, norm_gain[2], norm_shift[2]).astype(jnp.bfloat16)
    joined = matmul(act_three, full_point1)
    gated = (
        glu_gate(joined, live_rows).astype(jnp.bfloat16).reshape(utterances, frames, model_width)
    )
    padded = padded_2(gated, (("seq", 1),), half_taps)
    depth = kernel[0] * padded[:, 0:frames].astype(jnp.float32)
    for position in range(1, tap_count):
        depth = depth + kernel[position] * padded[:, position : position + frames].astype(
            jnp.float32
        )
    depth = depth.reshape(row_count, model_width)
    act_four = swish_norm(depth, norm_gain[3], norm_shift[3]).astype(jnp.bfloat16)
    convolved = matmul(act_four, full_point2)
    resid_three = resid_two + convolved
    act_five = layer_norm(resid_three, norm_gain[4], norm_shift[4]).astype(jnp.bfloat16)
    up_two = matmul(act_five, full_in2)
    hid_two = jax.nn.silu(up_two).astype(jnp.bfloat16)
    ffn_two = matmul(hid_two, full_out2)
    resid_four = resid_three + 0.5 * ffn_two
    result = layer_norm(resid_four, norm_gain[5], norm_shift[5])
    gathered = (
        lax.all_gather(shards[0], "seq", axis=0, tiled=True),
        lax.all_gather(shards[1], "seq", axis=0, tiled=True),
        lax.all_gather(shards[2], "seq", axis=0, tiled=True),
        lax.all_gather(shards[3], "seq", axis=0, tiled=True),
        lax.all_gather(shards[4], "seq", axis=0, tiled=True),
        lax.all_gather(shards[5], "seq", axis=0, tiled=True),
        lax.all_gather(shards[6], "seq", axis=0, tiled=True),
        lax.all_gather(shards[7], "seq", axis=0, tiled=True),
    )
    full_in1, full_out1, full_qkv, full_attn, full_point1, full_point2, full_in2, full_out2 = (
        gathered
    )
    grad_result = cotangent.astype(jnp.float32).reshape(row_count, model_width)
    _, back_five = jax.vjp(layer_norm, resid_four, norm_gain[5], norm_shift[5])
    grad_four, gain_five, shift_five = back_five(grad_result)
    grad_ffn2 = (0.5 * grad_four).astype(jnp.bfloat16)
    _, back_silu2 = jax.vjp(jax.nn.silu, up_two)
    grad_up2 = back_silu2(matmul_right_t(grad_ffn2, full_out2))[0].astype(jnp.bfloat16)
    _, back_four = jax.vjp(layer_norm, resid_three, norm_gain[4], norm_shift[4])
    grad_norm4, gain_four, shift_four = back_four(matmul_right_t(grad_up2, full_in2))
    grad_three = grad_four + grad_norm4
    grad_conv = grad_three.astype(jnp.bfloat16)
    _, back_swish = jax.vjp(swish_norm, depth, norm_gain[3], norm_shift[3])
    grad_depth_f, gain_three, shift_three = back_swish(matmul_right_t(grad_conv, full_point2))
    grad_depth = grad_depth_f.astype(jnp.bfloat16).reshape(utterances, frames, model_width)
    grad_padded = padded_2(grad_depth, (("seq", 1),), half_taps)
    grad_depth_wide = grad_depth.astype(jnp.float32)
    grad_gated = jnp.zeros((utterances, frames, model_width), jnp.float32)
    kernel_rows = []
    for position in range(tap_count):
        lower = 2 * half_taps - position
        grad_gated = grad_gated + kernel[position] * grad_padded[:, lower : lower + frames].astype(
            jnp.float32
        )
        kernel_rows.append(
            jnp.sum(
                grad_depth_wide * padded[:, position : position + frames].astype(jnp.float32),
                axis=(0, 1),
            )
        )
    grad_kernel = jnp.stack(kernel_rows)
    _, back_gate = jax.vjp(lambda joined_in: glu_gate(joined_in, live_rows), joined)
    grad_joined = back_gate(grad_gated.reshape(row_count, model_width))[0].astype(jnp.bfloat16)
    _, back_three = jax.vjp(layer_norm, resid_two, norm_gain[2], norm_shift[2])
    grad_norm3, gain_two, shift_two = back_three(matmul_right_t(grad_joined, full_point1))
    grad_two = grad_three + grad_norm3
    grad_att = grad_two.astype(jnp.bfloat16)
    grad_heads = (
        matmul_right_t(grad_att, full_attn)
        .astype(jnp.bfloat16)
        .reshape(utterances, frames, head_count, head_dim)
    )
    spread = jnp.sum(grad_heads.astype(jnp.float32) * attn_out, axis=-1)
    log_total_t = jnp.transpose(log_total, (0, 2, 1))
    spread_t = jnp.transpose(spread, (0, 2, 1))
    grad_slope = jnp.zeros((head_count,), jnp.float32)
    key_blk = lax.all_gather(keys, "seq", axis=1, tiled=True)
    value_blk = lax.all_gather(values, "seq", axis=1, tiled=True)
    amount = key_blk.shape[1]
    key_pos = jnp.arange(amount, dtype=jnp.int32)
    key_live = key_pos[None, :] < lengths[:, None]
    scores, distance = block_scores(
        queries, key_blk, frame_pos, key_pos, key_live, slopes, seq_length
    )
    attn_prob = jnp.exp(scores - log_total_t[..., None])
    grad_prob = jnp.einsum(
        "uqhd,ukhd->uhqk", grad_heads, value_blk, preferred_element_type=jnp.float32
    )
    grad_exact = attn_prob * (grad_prob - spread_t[..., None])
    grad_scores = grad_exact.astype(jnp.bfloat16)
    grad_query = (
        jnp.einsum("uhqk,ukhd->uqhd", grad_scores, key_blk, preferred_element_type=jnp.float32)
        * factor
    )
    grad_slope = grad_slope - jnp.sum(grad_exact * distance[None, None], axis=(0, 2, 3))
    grad_query, grad_slope = (grad_query, grad_slope)
    query_blk = lax.all_gather(queries, "seq", axis=1, tiled=True)
    dhead_blk = lax.all_gather(grad_heads, "seq", axis=1, tiled=True)
    total_blk = lax.all_gather(log_total.astype(jnp.bfloat16), "seq", axis=1, tiled=True).astype(
        jnp.float32
    )
    spread_blk = lax.all_gather(spread.astype(jnp.bfloat16), "seq", axis=1, tiled=True).astype(
        jnp.float32
    )
    amount = query_blk.shape[1]
    query_pos = jnp.arange(amount, dtype=jnp.int32)
    scores, distance = block_scores(
        query_blk, keys, query_pos, frame_pos, live_mask, slopes, seq_length
    )
    attn_prob = jnp.exp(scores - jnp.transpose(total_blk, (0, 2, 1))[..., None])
    grad_value = jnp.einsum(
        "uhqk,uqhd->ukhd",
        attn_prob.astype(jnp.bfloat16),
        dhead_blk,
        preferred_element_type=jnp.float32,
    )
    grad_prob = jnp.einsum("uqhd,ukhd->uhqk", dhead_blk, values, preferred_element_type=jnp.float32)
    grad_scores = (
        attn_prob * (grad_prob - jnp.transpose(spread_blk, (0, 2, 1))[..., None])
    ).astype(jnp.bfloat16)
    grad_key = (
        jnp.einsum("uhqk,uqhd->ukhd", grad_scores, query_blk, preferred_element_type=jnp.float32)
        * factor
    )
    grad_key, grad_value = (grad_key, grad_value)
    grad_packed = (
        jnp.stack([grad_query, grad_key, grad_value], axis=2)
        .astype(jnp.bfloat16)
        .reshape(row_count, 3 * model_width)
    )
    _, back_two = jax.vjp(layer_norm, resid_one, norm_gain[1], norm_shift[1])
    grad_norm2, gain_one, shift_one = back_two(matmul_right_t(grad_packed, full_qkv))
    grad_one = grad_two + grad_norm2
    grad_ffn1 = (0.5 * grad_one).astype(jnp.bfloat16)
    _, back_silu1 = jax.vjp(jax.nn.silu, up_one)
    grad_up1 = back_silu1(matmul_right_t(grad_ffn1, full_out1))[0].astype(jnp.bfloat16)
    _, back_one = jax.vjp(layer_norm, start_in, norm_gain[0], norm_shift[0])
    grad_norm1, gain_zero, shift_zero = back_one(matmul_right_t(grad_up1, full_in1))
    grad_start = grad_one + grad_norm1
    grad_frames = jnp.where(
        masked[..., None], 0.0, grad_start.reshape(utterances, frames, model_width)
    )
    wide_pairs = (
        (act_one, grad_up1),
        (act_two, grad_packed),
        (attn_low, grad_att),
        (act_three, grad_joined),
        (act_four, grad_conv),
        (act_five, grad_up2),
    )
    wide = lax.psum_scatter(
        jnp.concatenate(
            [matmul_left_t(left_side, right_side) for left_side, right_side in wide_pairs], axis=1
        ).astype(jnp.bfloat16),
        "seq",
        scatter_dimension=0,
        tiled=True,
    ).astype(jnp.float32)
    tall_pairs = ((hid_one, grad_ffn1), (hid_two, grad_ffn2))
    tall = lax.psum_scatter(
        jnp.concatenate(
            [matmul_left_t(left_side, right_side) for left_side, right_side in tall_pairs], axis=1
        ).astype(jnp.bfloat16),
        "seq",
        scatter_dimension=0,
        tiled=True,
    ).astype(jnp.float32)
    hidden_width = w_in1.shape[1]
    column_cuts = [
        hidden_width,
        3 * model_width,
        model_width,
        2 * model_width,
        model_width,
        hidden_width,
    ]
    wide_parts = []
    column_start = 0
    for column_width in column_cuts:
        wide_parts.append(wide[:, column_start : column_start + column_width])
        column_start = column_start + column_width
    grad_in1, grad_qkv, grad_attn, grad_point1, grad_point2, grad_in2 = wide_parts
    grad_out1 = tall[:, :model_width]
    grad_out2 = tall[:, model_width:]
    grad_norms = jnp.stack(
        [
            jnp.stack([gain_zero, shift_zero]),
            jnp.stack([gain_one, shift_one]),
            jnp.stack([gain_two, shift_two]),
            jnp.stack([gain_three, shift_three]),
            jnp.stack([gain_four, shift_four]),
            jnp.stack([gain_five, shift_five]),
        ]
    )
    grad_norms, grad_kernel, grad_slope = (
        lax.psum(grad_norms.astype(jnp.bfloat16), "seq").astype(jnp.float32),
        lax.psum(grad_kernel.astype(jnp.bfloat16), "seq").astype(jnp.float32),
        lax.psum(grad_slope.astype(jnp.bfloat16), "seq").astype(jnp.float32),
    )
    block_out = result.astype(jnp.bfloat16).reshape(utterances, frames, model_width)
    return (
        block_out,
        grad_frames,
        grad_in1,
        grad_out1,
        grad_qkv,
        grad_attn,
        grad_point1,
        grad_point2,
        grad_in2,
        grad_out2,
        grad_norms,
        grad_kernel,
        grad_slope,
    )


def place():
    seq, dp = lax.axis_index("seq"), lax.axis_index("dp")
    return seq // 2, lax.rem(seq, 2), dp // 2, lax.rem(dp, 2)


def device(z, x, y, core):
    return (z * 2 + x, y * 2 + core)


def z_partners(z):
    return (z + 1 - 2 * lax.rem(z, 2), lax.rem(z + 2, 4), 3 - z)


def remote(source, target, send, recv, where):
    return pltpu.make_async_remote_copy(
        src_ref=source,
        dst_ref=target,
        send_sem=send,
        recv_sem=recv,
        device_id=where,
        device_id_type=MESH,
    )


def greet(partners, waits):
    barrier = pltpu.get_barrier_semaphore()
    for partner in partners:
        pl.semaphore_signal(barrier, inc=1, device_id=partner, device_id_type=MESH)
    pl.semaphore_wait(barrier, waits)


def utterance_of(z, x, core):
    return lax.rem(z, 2) * 4 + x * 2 + core


def home_of(utterance, y, group):
    return device(2 * group + utterance // 4, lax.rem(utterance // 2, 2), y, lax.rem(utterance, 2))


def bits_of(s):
    return s // 4, lax.rem(s // 2, 2), lax.rem(s, 2)


def flipped(bits, r):
    flips = (r // 4, r // 2 % 2, r % 2)
    return [1 - b if f else b for b, f in zip(bits, flips)]


def utterance_in_round(seq, r):
    b2, b1, b0 = bits_of(seq)
    out = flipped((b1, b0, b2), r)
    return out[0] * 4 + out[1] * 2 + out[2]


def seq_in_round(utterance, r):
    t2, t1, t0 = flipped(bits_of(utterance), r)
    return t0 * 4 + t2 * 2 + t1


def units_of(shapes):
    units = []
    for index, (rows, columns) in enumerate(shapes):
        for row in range(0, rows, 128):
            for column in range(0, columns, 1024):
                units.append((index, row, column))
    return units


ROWS = 128
HALF = 64
COLUMNS = 1024
LAGS = (0, 1, 2, 3, 5, 7, 8)
SPLIT = 384


def blocks(rows, size):
    def run(body):
        @pl.loop(0, rows // size, unroll=2)
        def _(i):
            body(pl.ds(pl.multiple_of(i * size, size), size))

    return run


def normalise(v, norm, i):
    average = jnp.mean(v, axis=-1, keepdims=True)
    centred = v - average
    variance = jnp.mean(centred * centred, axis=-1, keepdims=True)
    return centred * lax.rsqrt(variance + EPSILON) * norm[i, 0:1, :] + norm[i, 1:2, :]


TILE = 256


def sigmoid(v):
    return 0.5 * jnp.tanh(0.5 * v) + 0.5


def silu(v):
    return v * sigmoid(v)


def times_unit(left, weight, emit, poll):
    unit, loads = weight
    for n in range(COLUMNS // TILE):
        columns = pl.ds(n * TILE, TILE)
        loads[n].wait()
        emit(columns, jnp.dot(left[...], unit[:, :, :, columns].reshape(COLUMNS, TILE), preferred_element_type=F32))
        poll()


def score_block(q, k, slope_row, first, live_keys):
    shape = (q.shape[0], k.shape[0])
    scores = lax.dot_general(q, k, (((1,), (1,)), ((), ())), preferred_element_type=F32)
    rows = lax.broadcasted_iota(jnp.int32, shape, 0) + first
    keys = lax.broadcasted_iota(jnp.int32, shape, 1)
    distance = jnp.abs(rows - keys).astype(F32) * (1.0 / k.shape[0])
    scores = scores * (q.shape[1] ** -0.5) - slope_row * distance
    return jnp.where(keys.astype(F32) < live_keys, scores, NEGATIVE), distance


def softmax_block(scores):
    top = jnp.max(scores, axis=-1, keepdims=True)
    expd = jnp.exp(scores - top)
    return expd / jnp.sum(expd, axis=-1, keepdims=True)


QUERIES = 128
BLOCK = 32


def forward_kernel(units, names, *refs):
    r = types.SimpleNamespace(**dict(zip(names, refs)))
    norm, taps, slope = r.norm, r.taps, r.slope
    length, width = r.x.shape[1:]
    heads = slope.shape[0]
    head_dim = width // heads
    z, x, y, core = place()
    seq, group = z * 2 + x, z // 2
    utterance = utterance_of(z, x, core)
    same = group == core
    zs = z_partners(z)
    over_z = [device(other, x, y, core) for other in zs]
    over_x = device(z, 1 - x, y, core)
    over_y = device(z, x, 1 - y, core)
    over_core = device(z, x, y, 1 - core)
    mates = [utterance_in_round(seq, i) for i in range(8)]
    givers = [device(s // 2, lax.rem(s, 2), y, group) for s in [seq_in_round(utterance, i) for i in range(8)]]
    targets = [home_of(u, y, core) for u in mates]
    barrier = pltpu.get_barrier_semaphore()

    @pl.when(jnp.logical_not(same))
    def _():
        pl.semaphore_signal(barrier, inc=1, device_id=givers[0], device_id_type=MESH)

    for partner in givers[1:] + [over_z[0], over_z[2], over_x, over_y, over_core]:
        pl.semaphore_signal(barrier, inc=1, device_id=partner, device_id_type=MESH)
    pl.semaphore_wait(barrier, jnp.where(same, 12, 13))

    swaps = ((r.start, r.h0), (r.lens, r.lens_here), (r.cot, r.cot_out))

    def swap(i, j):
        source, target = swaps[i]
        return remote(source.at[mates[j]], target.at[seq], r.swap_send.at[i, j], r.swap_recv.at[i, j], targets[j])

    def swap_local(i):
        source, target = swaps[i]
        return pltpu.make_async_copy(source.at[mates[0]], target.at[seq], r.swap_own.at[i])

    def swap_start(i, j):
        if j > 0:
            swap(i, j).start()
            return

        @pl.when(jnp.logical_not(same))
        def _():
            swap(i, 0).start()

        @pl.when(same)
        def _():
            swap_local(i).start()

    def swap_wait(i):
        @pl.when(jnp.logical_not(same))
        def _():
            swap(i, 0).wait()

        @pl.when(same)
        def _():
            swap_local(i).wait()

        for j in range(1, 8):
            swap(i, j).wait()

    send, recv, own = r.send, r.recv, r.own
    shards, fulls = r.shards, r.fulls

    def spot(unit):
        index, row, column = unit
        rows = pl.ds(row + pl.multiple_of(core * HALF, HALF), HALF)
        mine = pl.ds(column + pl.multiple_of(y * SPLIT, 128), COLUMNS - SPLIT)
        third = pl.ds(column + pl.multiple_of(y * (COLUMNS - SPLIT), 128), SPLIT)
        return shards[index], fulls[index], rows, mine, third, pl.ds(column, COLUMNS)

    middle = (z == 1) | (z == 2)
    near_pair, far_pair = pl.ds(2 * (z // 2), 2), pl.ds(2 - 2 * (z // 2), 2)

    class Along:
        def __init__(self, copy, sends, gets):
            self.copy, self.sends, self.gets = copy, sends, gets

        def start(self):
            @pl.when(self.sends)
            def _():
                self.copy.start()

        def wait(self):
            @pl.when(self.sends)
            def _():
                self.copy.wait_send()

            @pl.when(self.gets)
            def _():
                self.copy.wait_recv()

    def first(u):
        shard, full, rows, mine, _, _ = spot(units[u])
        every = pl.ds(units[u][2], COLUMNS)
        return [
            remote(shard.at[rows, mine], full.at[z, x, rows, mine], send.at[u, 0], recv.at[u, 0], over_z[0]),
            pltpu.make_async_copy(shard.at[rows, every], full.at[z, x, rows, every], own.at[u]),
        ]

    def across(u):
        _, full, rows, mine, _, _ = spot(units[u])
        piece = full.at[near_pair, x, rows, mine]
        return [Along(remote(piece, piece, send.at[u, 1], recv.at[u, 1], over_z[2]), middle, middle)]

    def outward(u):
        _, full, rows, mine, _, _ = spot(units[u])
        piece = full.at[far_pair, x, rows, mine]
        copy = remote(piece, piece, send.at[u, 2], recv.at[u, 2], over_z[0])
        return [Along(copy, middle, jnp.logical_not(middle))]

    def second(u):
        _, full, rows, mine, _, _ = spot(units[u])
        piece = full.at[:, x, rows, mine]
        return [remote(piece, piece, send.at[u, 3], recv.at[u, 3], over_x)]

    def third(u):
        _, full, rows, _, part, _ = spot(units[u])
        pieces = [full.at[:, 1 - x, rows, part]] + [full.at[other, x, rows, part] for other in zs]
        out = [remote(p, p, send.at[u, 4 + j], recv.at[u, 4 + j], over_y) for j, p in enumerate(pieces)]
        return out

    def fourth(u):
        _, full, rows, _, _, whole = spot(units[u])
        piece = full.at[:, :, rows, whole]
        return [remote(piece, piece, send.at[u, 8], recv.at[u, 8], over_core)]

    stages = (first, across, outward, second, third, fourth)
    last = len(units)
    done = [0]

    actions = []
    ends = {}

    def move(u, depth):
        def act_on():
            if depth > 0:
                for copy in stages[depth - 1](u):
                    copy.wait()
            if depth < len(stages):
                for copy in stages[depth](u):
                    copy.start()

        return act_on

    for step in range(last + LAGS[-1]):
        for depth, lag in enumerate(LAGS):
            if 0 <= step - lag < last:
                actions.append(move(step - lag, depth))
                if depth == len(stages):
                    ends[step - lag] = len(actions)
        if 12 <= step < 20:
            actions.append(functools.partial(swap_start, 2, step - 12))

    def poll(count=1):
        for _ in range(count):
            if done[0] < len(actions):
                actions[done[0]]()
                done[0] += 1

    taken = [0]

    def weight():
        u = taken[0]
        taken[0] += 1
        while done[0] < ends[u]:
            poll()
        index, row, column = units[u]
        loads = []
        for n in range(COLUMNS // TILE):
            source = fulls[index].at[:, :, pl.ds(row, ROWS), pl.ds(column + n * TILE, TILE)]
            target = r.unit.at[u % 2, :, :, :, pl.ds(n * TILE, TILE)]
            copy = pltpu.make_async_copy(source, target, r.load.at[u % 2, n])
            copy.start()
            loads.append(copy)
        return r.unit.at[u % 2], loads

    kept = []

    def keep(source, target):
        copy = pltpu.make_async_copy(source, target, r.kept.at[len(kept)])
        copy.start()
        kept.append(copy)

    xs, act, acc = r.x, r.act, r.acc
    poll()
    for j in range(8):
        swap_start(0, j)
    for j in range(8):
        swap_start(1, j)
    poll(4)
    swap_wait(0)

    @blocks(length, BLOCK)
    def _(rows):
        xs[0, rows, :] = r.h0[rows.start // 64, pl.ds(pl.multiple_of(lax.rem(rows.start, 64), BLOCK), BLOCK), :].astype(F32)
        act[rows, :] = normalise(xs[0, rows, :], norm, 0).astype(BF16)

    keep(r.h0, r.h0_out)

    def feed_forward(x_in, x_out, up, up_out):
        hidden = r.hidden
        for p in range(4):
            unit, loads = weight()

            for n in range(COLUMNS // TILE):
                columns = pl.ds(n * TILE, TILE)
                loads[n].wait()
                value = jnp.dot(act[...], unit[:, :, :, columns].reshape(COLUMNS, TILE), preferred_element_type=F32)
                up[p, :, columns] = value.astype(BF16)
                value = silu(value).astype(BF16)
                for t in range(2 * n, 2 * n + 2):
                    place_at = pl.ds((2 * p + t // 4) * 128, 128)
                    hidden[t % 4, :, place_at] = value[:, (t - 2 * n) * 128 : (t - 2 * n + 1) * 128]
                poll()

            keep(up.at[p], up_out.at[:, pl.ds(p * COLUMNS, COLUMNS)])
        for q in range(4):
            def emit(columns, value, q=q):
                if q == 0:
                    acc[:, columns] = value
                else:
                    acc[:, columns] = acc[:, columns] + value

            times_unit(hidden.at[q], weight(), emit, poll)

        @blocks(length, BLOCK)
        def _(rows):
            xs[x_out, rows, :] = xs[x_in, rows, :] + 0.5 * acc[rows, :]

    feed_forward(0, 1, r.up, r.u1_out)
    keep(xs.at[1], r.x1_out)

    @blocks(length, BLOCK)
    def _(rows):
        act[rows, :] = normalise(xs[1, rows, :], norm, 1).astype(BF16)

    qkv = r.qkv
    for i in range(3):

        def emit(columns, value, i=i):
            qkv[i, :, columns] = value.astype(BF16)

        times_unit(act, weight(), emit, poll)
    keep(qkv, r.qkv_out)
    swap_wait(1)
    live_count = r.lens_here[0, 0:1, 0:1]
    keep(r.lens_here, r.lens_out)
    attended = r.attended
    for h in range(heads):
        columns = pl.ds(h * head_dim, head_dim)

        @blocks(length, QUERIES)
        def _(rows, h=h, columns=columns):
            scores, _ = score_block(
                qkv[0, rows, columns], qkv[1, :, columns], slope[h : h + 1, :], rows.start, live_count
            )
            prob = softmax_block(scores).astype(BF16)
            attended[rows, columns] = jnp.dot(prob, qkv[2, :, columns], preferred_element_type=F32).astype(BF16)

        poll(2)
    keep(attended, r.attended_out)

    def add_to(x_in, x_out):
        def emit(columns, value):
            xs[x_out, :, columns] = xs[x_in, :, columns] + value

        return emit

    times_unit(attended, weight(), add_to(1, 2), poll)
    keep(xs.at[2], r.x2_out)

    @blocks(length, BLOCK)
    def _(rows):
        act[rows, :] = normalise(xs[2, rows, :], norm, 2).astype(BF16)

    gates, gated = r.gates, r.gated

    def emit(columns, value):
        acc[:, columns] = value
        gates[0, :, columns] = value.astype(BF16)

    times_unit(act, weight(), emit, poll)
    gated[0:8, :] = jnp.zeros((8, width), F32)
    gated[length + 8 : length + 16, :] = jnp.zeros((8, width), F32)

    def emit(columns, value):
        gates[1, :, columns] = value.astype(BF16)
        live = lax.broadcasted_iota(jnp.int32, value.shape, 0).astype(F32) < live_count
        passed = jnp.where(live, acc[:, columns] * sigmoid(value), 0.0)
        gated[pl.ds(8, length), columns] = passed.astype(BF16).astype(F32)

    times_unit(act, weight(), emit, poll)
    keep(gates, r.gates_out)
    keep(gated, r.gated_out)
    depth = r.depth

    @blocks(length, BLOCK)
    def _(rows):
        near = gated[pl.ds(pl.multiple_of(rows.start, BLOCK), BLOCK + 16), :]
        total = taps[0:1, :] * near[6 : 6 + BLOCK]
        for t in range(1, taps.shape[0]):
            total = total + taps[t : t + 1, :] * near[6 + t : 6 + t + BLOCK]
        depth[rows, :] = total
        value = normalise(total, norm, 3)
        act[rows, :] = (silu(value)).astype(BF16)

    keep(depth, r.depth_out)
    times_unit(act, weight(), add_to(2, 3), poll)
    keep(xs.at[3], r.x3_out)

    @blocks(length, BLOCK)
    def _(rows):
        act[rows, :] = normalise(xs[3, rows, :], norm, 4).astype(BF16)

    feed_forward(3, 4, r.up2, r.u2_out)
    keep(xs.at[4], r.x4_out)

    @blocks(length, BLOCK)
    def _(rows):
        act[rows, :] = normalise(xs[4, rows, :], norm, 5).astype(BF16)

    keep(act, r.result_out)
    swap_wait(2)
    for copy in kept:
        copy.wait()


def forward(start, lens, cot, norm, taps, slope, shards, collective_id):
    shapes = [s.shape for s in shards]
    units = units_of(shapes)
    width = norm.shape[-1]
    frames = start.shape[1]
    length = 8 * frames
    count = len(shards)
    dma = pltpu.SemaphoreType.DMA
    hidden = shapes[0][1]
    wide = lambda *lead: jax.ShapeDtypeStruct(lead + (length, width), F32)
    low = lambda *lead: jax.ShapeDtypeStruct(lead + (length, width), BF16)
    up = jax.ShapeDtypeStruct((length, hidden), BF16)
    outs = dict(
        cot_out=jax.ShapeDtypeStruct(cot.shape, cot.dtype),
        h0_out=jax.ShapeDtypeStruct(start.shape, start.dtype),
        u1_out=up,
        x1_out=wide(),
        qkv_out=low(3),
        attended_out=low(),
        x2_out=wide(),
        gates_out=low(2),
        gated_out=jax.ShapeDtypeStruct((length + 16, width), F32),
        depth_out=wide(),
        x3_out=wide(),
        u2_out=up,
        x4_out=wide(),
        result_out=low(),
        lens_out=jax.ShapeDtypeStruct(lens.shape, lens.dtype),
    )
    scratch = dict(
        h0=pltpu.VMEM(start.shape, BF16),
        lens_here=pltpu.VMEM(lens.shape, F32),
        x=pltpu.VMEM((5, length, width), F32),
        act=pltpu.VMEM((length, width), BF16),
        acc=pltpu.VMEM((length, width), F32),
        hidden=pltpu.VMEM((4, length, width), BF16),
        up=pltpu.VMEM((4, length, width), BF16),
        up2=pltpu.VMEM((4, length, width), BF16),
        qkv=pltpu.VMEM((3, length, width), BF16),
        attended=pltpu.VMEM((length, width), BF16),
        gates=pltpu.VMEM((2, length, width), BF16),
        gated=pltpu.VMEM((length + 16, width), F32),
        depth=pltpu.VMEM((length, width), F32),
        unit=pltpu.VMEM((2, 4, 2, ROWS, COLUMNS), BF16),
        load=dma((2, COLUMNS // TILE)),
        swap_send=dma((3, 8)),
        swap_recv=dma((3, 8)),
        swap_own=dma((3,)),
        send=dma((len(units), 9)),
        recv=dma((len(units), 9)),
        own=dma((len(units),)),
        kept=dma((32,)),
    )
    names = ["start", "lens", "cot", "norm", "taps", "slope"]
    vmem = pl.BlockSpec(memory_space=pltpu.VMEM)

    def body(*refs):
        plain, rest = refs[:6], refs[6:]
        ours, rest = rest[:count], rest[count:]
        made, rest = rest[: len(outs)], rest[len(outs) :]
        fulls, rest = rest[:count], rest[count:]
        forward_kernel(
            units,
            names + list(outs) + list(scratch) + ["shards", "fulls"],
            *plain,
            *made,
            *rest,
            ours,
            fulls,
        )

    results = pl.pallas_call(
        body,
        out_shape=list(outs.values()) + [jax.ShapeDtypeStruct((4, 2) + s, BF16) for s in shapes],
        in_specs=[ANY, ANY, ANY, vmem, vmem, vmem] + [ANY] * count,
        out_specs=[ANY] * (len(outs) + count),
        scratch_shapes=list(scratch.values()),
        compiler_params=pltpu.CompilerParams(
            collective_id=collective_id, has_side_effects=True, vmem_limit_bytes=60 * 2**20
        ),
    )(start, lens, cot, norm, taps, slope, *shards)
    made = types.SimpleNamespace(**dict(zip(outs, results[: len(outs)])))
    fulls = [f.reshape(8 * s[0], s[1]) for f, s in zip(results[len(outs) :], shapes)]
    return made, fulls


CADENCE = 12.0
SLOTS = 5


def norm_back(v, dy, norm, i, sums):
    average = jnp.mean(v, axis=-1, keepdims=True)
    centred = v - average
    scale = lax.rsqrt(jnp.mean(centred * centred, axis=-1, keepdims=True) + EPSILON)
    unit = centred * scale
    sums[2 * i] += jnp.sum((dy * unit).reshape(-1, 8, dy.shape[-1]), axis=0)
    sums[2 * i + 1] += jnp.sum(dy.reshape(-1, 8, dy.shape[-1]), axis=0)
    inner = dy * norm[i, 0:1, :]
    return scale * (
        inner
        - jnp.mean(inner, axis=-1, keepdims=True)
        - unit * jnp.mean(inner * unit, axis=-1, keepdims=True)
    )


def silu_back(v):
    s = sigmoid(v)
    return s * (1.0 + v * (1.0 - s))


def times_t(left, right):
    return lax.dot_general(left, right, (((1,), (1,)), ((), ())), preferred_element_type=F32)


def t_times(left, right):
    return lax.dot_general(left, right, (((0,), (0,)), ((), ())), preferred_element_type=F32)


BACK_ORDER = (7, 6, 5, 4, 3, 2, 1, 0)


def backward_kernel(units, names, *refs):
    r = types.SimpleNamespace(**dict(zip(names, refs)))
    norm, taps, slope, sums = r.norm, r.taps, r.slope, r.sums
    length, width = r.dx.shape
    heads = slope.shape[0]
    head_dim = width // heads
    z, x, y, core = place()
    seq, group = z * 2 + x, z // 2
    utterance = utterance_of(z, x, core)
    keeps = group == core
    other = jnp.logical_not(keeps)
    z_other = z + 1 - 2 * lax.rem(z, 2)
    over_core = device(z, x, y, 1 - core)
    over_x = device(z, 1 - x, y, core)
    over_z = device(z_other, x, y, core)
    far = device(3 - z, x, y, group)
    seqs = [seq_in_round(utterance, i) for i in range(8)]
    targets = [device(s // 2, lax.rem(s, 2), y, group) for s in seqs]
    givers = [home_of(utterance_in_round(seq, i), y, core) for i in range(8)]
    barrier = pltpu.get_barrier_semaphore()
    for partner in [over_core, over_x, over_z] + givers[1:]:
        pl.semaphore_signal(barrier, inc=1, device_id=partner, device_id_type=MESH)

    @pl.when(other)
    def _():
        for giver in [device(3 - z, x, y, 0), device(3 - z, x, y, 1), givers[0]]:
            pl.semaphore_signal(barrier, inc=1, device_id=giver, device_id_type=MESH)

    pl.semaphore_wait(barrier, jnp.where(keeps, 11, 12))

    swaps = ((r.result, r.result_home), (r.dframes, r.dframes_home), (r.small, r.small_home))

    def swap(i, j):
        source, target = swaps[i][0], swaps[i][1].at[utterance]
        block = source if i == 2 else source.at[seqs[j]]
        return remote(block, target, r.swap_send.at[i, j], r.swap_recv.at[i, j], targets[j])

    def swap_local(i):
        source, target = swaps[i][0], swaps[i][1].at[utterance]
        return pltpu.make_async_copy(source if i == 2 else source.at[seqs[0]], target, r.swap_own.at[i])

    def swap_start(i, j):
        if j > 0:
            swap(i, j).start()
            return

        @pl.when(other)
        def _():
            swap(i, 0).start()

        @pl.when(keeps)
        def _():
            swap_local(i).start()

    def swap_wait(i):
        @pl.when(other)
        def _():
            swap(i, 0).wait()

        @pl.when(keeps)
        def _():
            swap_local(i).wait()

        for j in range(1, 8):
            swap(i, j).wait()

    grads, outs, mine, core_in, first_in, second_in = (
        r.grads, r.outs, r.mine, r.core_in, r.first_in, r.second_in
    )
    half = pl.multiple_of(core * HALF, HALF)
    other_half = pl.multiple_of((1 - core) * HALF, HALF)
    last = len(units)

    def columns_of(u):
        return pl.ds(units[u][2], COLUMNS)

    def core_copy(u):
        source = grads[units[u][0]].at[:, :, pl.ds(units[u][1] + other_half, HALF), columns_of(u)]
        return remote(source, core_in.at[u % 2], r.s_core.at[u % 2], r.r_core.at[u % 2], over_core)

    def load_copy(u):
        source = grads[units[u][0]].at[:, :, pl.ds(units[u][1] + half, HALF), columns_of(u)]
        return pltpu.make_async_copy(source, mine.at[u % SLOTS], r.s_load.at[u % 2])

    def swapped(u):
        return u % 8 == 2

    def first_copies(u):
        slot = u % SLOTS
        held, arriving, send, recv = mine.at[slot], first_in.at[slot], r.s_first.at[slot], r.r_first.at[slot]
        if swapped(u):
            return [
                remote(held.at[t], arriving.at[pl.ds(2 * i, 2)], send.at[i], recv.at[i], over_z)
                for i, t in enumerate((z_other, 3 - z_other))
            ]
        return [remote(held.at[:, 1 - x], arriving, send.at[0], recv.at[0], over_x)]

    def second_copies(u):
        slot = u % SLOTS
        held, arriving, send, recv = mine.at[slot], second_in.at[slot], r.s_second.at[slot], r.r_second.at[slot]
        if swapped(u):
            pairs, partner = ((z, 1 - x), (3 - z, 1 - x)), over_x
        else:
            pairs, partner = ((z_other, x), (3 - z_other, x)), over_z
        return [
            remote(held.at[t, t_x], arriving.at[i], send.at[i], recv.at[i], partner)
            for i, (t, t_x) in enumerate(pairs)
        ]

    def far_copy(u, giver=None):
        start = half if giver is None else giver * HALF
        target = outs[units[u][0]].at[pl.ds(units[u][1] + start, HALF), columns_of(u)]
        recv = r.r_far.at[u, core if giver is None else giver]
        return remote(mine.at[u % SLOTS, 3 - z, x], target, r.s_far.at[u % 2], recv, far)

    def near_target(u, start):
        return outs[units[u][0]].at[pl.ds(units[u][1] + start, HALF), columns_of(u)]

    def near_copy(u, start):
        return remote(
            mine.at[u % SLOTS, z, x], near_target(u, start), r.s_near.at[u % 2], r.r_near.at[u], over_core
        )

    def near_local(u):
        return pltpu.make_async_copy(mine.at[u % SLOTS, z, x], near_target(u, half), r.s_own.at[u % 2])

    def add(into, more):
        into[...] = (into[...].astype(F32) + more[...].astype(F32)).astype(BF16)

    def stage0(u):
        load_copy(u).start()
        core_copy(u).start()

    def stage1(u):
        load_copy(u).wait()
        core_copy(u).wait()
        held, arrived = mine.at[u % SLOTS], core_in.at[u % 2]
        if swapped(u):
            sent = [(t, t_x) for t in (z_other, 3 - z_other) for t_x in (0, 1)]
            rest = [(t, t_x) for t in (z, 3 - z) for t_x in (0, 1)]
        else:
            sent, rest = [(t, 1 - x) for t in range(4)], [(t, x) for t in range(4)]
        for t in sent:
            add(held.at[t], arrived.at[t])
        for copy in first_copies(u):
            copy.start()
        for t in rest:
            add(held.at[t], arrived.at[t])

    def stage2(u):
        for copy in first_copies(u):
            copy.wait()
        held, arrived = mine.at[u % SLOTS], first_in.at[u % SLOTS]
        if swapped(u):
            sent = [((t, 1 - x), 2 * i + 1 - x) for i, t in enumerate((z, 3 - z))]
            rest = [((t, x), 2 * i + x) for i, t in enumerate((z, 3 - z))]
        else:
            sent = [((t, x), t) for t in (z_other, 3 - z_other)]
            rest = [((t, x), t) for t in (z, 3 - z)]
        for (t, i), copy in zip(sent, second_copies(u)):
            add(held.at[t], arrived.at[i])
            copy.start()
        for t, i in rest:
            add(held.at[t], arrived.at[i])

    def stage3(u):
        for copy in second_copies(u):
            copy.wait()
        held, arrived = mine.at[u % SLOTS], second_in.at[u % SLOTS]
        add(held.at[3 - z, x], arrived.at[1])
        far_copy(u).start()
        add(held.at[z, x], arrived.at[0])

        @pl.when(keeps)
        def _():
            near_local(u).start()

        @pl.when(other)
        def _():
            near_copy(u, half).start()

    def stage4(u):
        far_copy(u).wait_send()

        @pl.when(keeps)
        def _():
            near_local(u).wait()
            near_copy(u, other_half).wait_recv()

        @pl.when(other)
        def _():
            near_copy(u, half).wait_send()

    order = ((stage1, 1), (stage0, 0), (stage2, 2), (stage3, 3), (stage4, 4))
    ticks, emitted, clock = [0], [0], [0.0]

    def tick():
        step = ticks[0]
        ticks[0] += 1
        settle(min(step + 1, last))
        for stage, depth in order:
            if 0 <= step - depth < last:
                stage(step - depth)

    def spent(us):
        if emitted[0] == 0:
            return
        clock[0] += us
        while clock[0] >= CADENCE:
            clock[0] -= CADENCE
            if ticks[0] < emitted[0]:
                tick()

    stored = [0]

    def stage_copy(u):
        target = grads[units[u][0]].at[:, :, pl.ds(units[u][1], ROWS), columns_of(u)]
        return pltpu.make_async_copy(r.stage.at[u % 2], target, r.s_stage.at[u % 2])

    def settle(count):
        while stored[0] < count:
            stage_copy(stored[0]).wait()
            stored[0] += 1

    def emit(left, right):
        u = emitted[0]
        stage = r.stage.at[u % 2]
        settle(u - 1)
        for t in range(4):
            value = t_times(left[:, pl.ds(t * 256, 256)], right[...])
            stage[t] = value.astype(BF16).reshape(2, ROWS, COLUMNS)
        stage_copy(u).start()
        emitted[0] += 1
        if u == 0:
            tick()
        spent(3.0)

    wanted = []
    for index in BACK_ORDER:
        rows, columns = r.fulls[index].shape
        for row in range(0, rows, 1024):
            for column in range(0, columns, 1024):
                wanted.append((index, row, column))

    def weight_copies(i):
        index, row, column = wanted[i]
        return [
            pltpu.make_async_copy(
                r.fulls[index].at[pl.ds(row + 256 * t, 256), pl.ds(column, 1024)],
                r.unit.at[i % 2, t],
                r.s_unit.at[i % 2, t],
            )
            for t in range(4)
        ]

    taken = [0]

    def weight():
        i = taken[0]
        taken[0] += 1
        if i + 1 < len(wanted):
            for copy in weight_copies(i + 1):
                copy.start()
        return r.unit.at[i % 2], weight_copies(i)

    def times_matrix(left, take):
        unit, copies = weight()
        for t in range(4):
            copies[t].wait()
            take(pl.ds(t * 256, 256), times_t(left[...], unit[t]))
        spent(2.5)

    def into_total(q):
        def take(columns, value):
            if q == 0:
                r.total[:, columns] = value
            else:
                r.total[:, columns] = r.total[:, columns] + value

        return take

    fetched = {}

    def fetch(name, source, target):
        fetched[name] = pltpu.make_async_copy(source, target, r.s_fetch.at[len(fetched)])
        fetched[name].start()

    def arrived(*wanted_names):
        for name in wanted_names:
            fetched[name].wait()

    xs, dx, total, low, act, up, du, hidden = (
        r.xs, r.dx, r.total, r.low, r.act, r.up, r.du, r.hidden
    )
    fetch("x4", r.x4, xs.at[0])
    fetch("cot", r.cot, r.cot_here)
    for p in range(4):
        fetch(("u2", p), r.u2.at[:, pl.ds(p * COLUMNS, COLUMNS)], up.at[p])
    for copy in weight_copies(0):
        copy.start()
    fetch("x3", r.x3, xs.at[1])
    fetch("depth", r.depth, r.depth_here)
    fetch("gates", r.gates, r.gates_here)
    fetch("gated", r.gated, r.gated_here)
    fetch("qkv", r.qkv, r.qkv_here)
    fetch("attended", r.attended, r.attended_here)
    fetch("lens", r.lens, r.lens_here)
    fetch("h0", r.h0, r.h0_here)
    for j in range(8):
        swap_start(0, j)
    sums[...] = jnp.zeros(sums.shape, F32)
    arrived("x4", "cot")

    def frame_block(ref, rows):
        return ref[rows.start // 64, pl.ds(pl.multiple_of(lax.rem(rows.start, 64), BLOCK), BLOCK), :]

    @blocks(length, BLOCK)
    def _(rows):
        grad = norm_back(xs[0, rows, :], frame_block(r.cot_here, rows).astype(F32), norm, 5, sums)
        dx[rows, :] = grad
        low[rows, :] = (0.5 * grad).astype(BF16)

    fetch("x2", r.x2, xs.at[0])

    def feed_forward_back(kind, x_slot, norm_index, write):
        arrived(*[(kind, p) for p in range(4)])
        for p in range(4):

            @pl.loop(0, 8)
            def _(t):
                value = up[p, :, pl.ds(pl.multiple_of(t * 128, 128), 128)].astype(F32)
                place_at = pl.ds(pl.multiple_of((2 * p + t // 4) * 128, 128), 128)
                hidden[lax.rem(t, 4), :, place_at] = silu(value).astype(BF16)

        for q in range(4):
            emit(hidden.at[q], low)
        for p in range(4):

            def take(columns, value, p=p):
                du[p, :, columns] = (value * silu_back(up[p, :, columns].astype(F32))).astype(BF16)

            times_matrix(low, take)
            spent(1.0)
        for p in range(4):
            times_matrix(du.at[p], into_total(p))
        write()
        for p in range(4):
            emit(act, du.at[p])

    def block_norm(x_slot, norm_index):
        @blocks(length, BLOCK)
        def _(rows):
            act[rows, :] = normalise(xs[x_slot, rows, :], norm, norm_index).astype(BF16)

        spent(3.0)

    def block_norm_back(x_slot, norm_index, factor):
        @blocks(length, BLOCK)
        def _(rows):
            grad = dx[rows, :] + norm_back(xs[x_slot, rows, :], total[rows, :], norm, norm_index, sums)
            dx[rows, :] = grad
            low[rows, :] = (factor * grad).astype(BF16)

        spent(5.0)

    def after_two():
        arrived("x3")
        block_norm(1, 4)

    feed_forward_back("u2", 1, 4, after_two)
    for p in range(4):
        fetch(("u1", p), r.u1.at[:, pl.ds(p * COLUMNS, COLUMNS)], up.at[p])
    block_norm_back(1, 4, 1.0)
    fetch("x1", r.x1, xs.at[1])

    depth, gates, gated, spread = r.depth_here, r.gates_here, r.gated_here, r.spread
    arrived("depth", "gated", "gates", "lens")
    live_count = r.lens_here[0, 0:1, 0:1]

    @blocks(length, BLOCK)
    def _(rows):
        act[rows, :] = silu(normalise(depth[rows, :], norm, 3)).astype(BF16)

    emit(act, low)
    times_matrix(low, into_total(0))
    spread[0:8, :] = jnp.zeros((8, width), F32)
    spread[length + 8 : length + 16, :] = jnp.zeros((8, width), F32)

    @blocks(length, BLOCK)
    def _(rows):
        inner = depth[rows, :]
        dy = total[rows, :] * silu_back(normalise(inner, norm, 3))
        grad = norm_back(inner, dy, norm, 3, sums).astype(BF16).astype(F32)
        spread[pl.ds(pl.multiple_of(rows.start, BLOCK) + 8, BLOCK), :] = grad

    spent(6.0)

    @blocks(length, BLOCK)
    def _(rows):
        around = pl.ds(pl.multiple_of(rows.start, BLOCK), BLOCK + 16)
        near = spread[around, :]
        passed = gated[around, :]
        here = near[8 : 8 + BLOCK]
        grad = jnp.zeros((BLOCK, width), F32)
        for t in range(taps.shape[0]):
            grad = grad + taps[t : t + 1, :] * near[10 - t : 10 - t + BLOCK]
            product = here * passed[6 + t : 6 + t + BLOCK]
            sums[12 + t] += jnp.sum(product.reshape(-1, 8, width), axis=0)
        live = lax.broadcasted_iota(jnp.int32, (BLOCK, width), 0) + rows.start
        grad = jnp.where(live.astype(F32) < live_count, grad, 0.0)
        opened = sigmoid(gates[1, rows, :].astype(F32))
        du[0, rows, :] = (grad * opened).astype(BF16)
        du[1, rows, :] = (grad * gates[0, rows, :].astype(F32) * opened * (1.0 - opened)).astype(BF16)

    arrived("x2")
    spent(8.0)
    block_norm(0, 2)
    for p in range(2):
        emit(act, du.at[p])
        times_matrix(du.at[p], into_total(p))
    block_norm_back(0, 2, 1.0)

    qkv, heads_grad, sides = r.qkv_here, r.heads_grad, r.sides
    arrived("attended", "qkv")
    emit(r.attended_here, low)

    def take(columns, value):
        heads_grad[:, columns] = value.astype(BF16)

    times_matrix(low, take)
    for h in range(heads):
        columns = pl.ds(h * head_dim, head_dim)
        sides[...] = jnp.zeros(sides.shape, F32)

        @blocks(length, QUERIES)
        def _(rows, h=h, columns=columns):
            q, k, v = qkv[0, rows, columns], qkv[1, :, columns], qkv[2, :, columns]
            do = heads_grad[rows, columns]
            scores, distance = score_block(q, k, slope[h : h + 1, :], rows.start, live_count)
            prob = softmax_block(scores)
            dp = times_t(do, v)
            exact = prob * (dp - jnp.sum(prob * dp, axis=-1, keepdims=True))
            sums[17 + h, :, 0:length] -= jnp.sum((exact * distance).reshape(-1, 8, length), axis=0)
            ds = exact.astype(BF16)
            scale = head_dim**-0.5
            du[0, rows, columns] = (jnp.dot(ds, k, preferred_element_type=F32) * scale).astype(BF16)
            sides[0] += t_times(ds, q) * scale
            sides[1] += t_times(prob.astype(BF16), do)

        du[1, :, columns] = sides[0].astype(BF16)
        du[2, :, columns] = sides[1].astype(BF16)
        spent(6.0)
    arrived("x1")
    block_norm(1, 1)
    for p in range(3):
        emit(act, du.at[p])
        times_matrix(du.at[p], into_total(p))
    block_norm_back(1, 1, 0.5)
    arrived("h0")

    def after_one():
        @blocks(length, BLOCK)
        def _(rows):
            value = frame_block(r.h0_here, rows).astype(F32)
            act[rows, :] = normalise(value, norm, 0).astype(BF16)
            grad = dx[rows, :] + norm_back(value, total[rows, :], norm, 0, sums)
            spot = pl.ds(pl.multiple_of(lax.rem(rows.start, 64), BLOCK), BLOCK)
            r.dframes[rows.start // 64, spot, :] = grad.astype(BF16)

        for i in range(17):
            r.wide[i : i + 1, :] = jnp.sum(sums[i], axis=0, keepdims=True)
        for h in range(heads):
            whole = jnp.sum(jnp.sum(sums[17 + h], axis=0, keepdims=True), axis=1, keepdims=True)
            r.wide[17 + h : 18 + h, :] = jnp.broadcast_to(whole, (1, width))
        r.wide[17 + heads : 32, :] = jnp.zeros((15 - heads, width), F32)
        r.small[...] = r.wide[...].astype(BF16)
        for j in range(8):
            swap_start(1, j)
            swap_start(2, j)

    feed_forward_back("u1", 0, 0, after_one)
    while ticks[0] < last + 4:
        tick()
    for i in range(3):
        swap_wait(i)

    @pl.when(other)
    def _():
        for u in range(last):
            far_copy(u, 0).wait_recv()
            far_copy(u, 1).wait_recv()


def backward(made, fulls, norm, taps, slope, collective_id):
    width = norm.shape[-1]
    length = made.x4_out.shape[0]
    blocked = (8, length // 8, width)
    shapes = [(f.shape[0] // 8, f.shape[1]) for f in fulls]
    count = len(fulls)
    units = [
        (index, row, column)
        for index in BACK_ORDER
        for row in range(0, shapes[index][0], ROWS)
        for column in range(0, shapes[index][1], COLUMNS)
    ]
    number = len(units)
    dma = pltpu.SemaphoreType.DMA
    given = dict(
        cot=made.cot_out,
        h0=made.h0_out,
        u1=made.u1_out,
        x1=made.x1_out,
        qkv=made.qkv_out,
        attended=made.attended_out,
        x2=made.x2_out,
        gates=made.gates_out,
        gated=made.gated_out,
        depth=made.depth_out,
        x3=made.x3_out,
        u2=made.u2_out,
        x4=made.x4_out,
        result=made.result_out.reshape(blocked),
        lens=made.lens_out,
    )
    outs = dict(
        result_home=jax.ShapeDtypeStruct(blocked, BF16),
        dframes_home=jax.ShapeDtypeStruct(blocked, BF16),
        small_home=jax.ShapeDtypeStruct((8, 32, width), BF16),
    )
    scratch = dict(
        xs=pltpu.VMEM((2, length, width), F32),
        dx=pltpu.VMEM((length, width), F32),
        total=pltpu.VMEM((length, width), F32),
        low=pltpu.VMEM((length, width), BF16),
        act=pltpu.VMEM((length, width), BF16),
        up=pltpu.VMEM((4, length, width), BF16),
        du=pltpu.VMEM((4, length, width), BF16),
        hidden=pltpu.VMEM((4, length, width), BF16),
        cot_here=pltpu.VMEM(blocked, BF16),
        h0_here=pltpu.VMEM(blocked, BF16),
        dframes=pltpu.VMEM(blocked, BF16),
        depth_here=pltpu.VMEM((length, width), F32),
        gates_here=pltpu.VMEM((2, length, width), BF16),
        gated_here=pltpu.VMEM((length + 16, width), F32),
        spread=pltpu.VMEM((length + 16, width), F32),
        qkv_here=pltpu.VMEM((3, length, width), BF16),
        attended_here=pltpu.VMEM((length, width), BF16),
        heads_grad=pltpu.VMEM((length, width), BF16),
        sides=pltpu.VMEM((2, length, width // slope.shape[0]), F32),
        lens_here=pltpu.VMEM(made.lens_out.shape, F32),
        sums=pltpu.VMEM((17 + slope.shape[0], 8, width), F32),
        wide=pltpu.VMEM((32, width), F32),
        small=pltpu.VMEM((32, width), BF16),
        unit=pltpu.VMEM((2, 4, 256, 1024), BF16),
        stage=pltpu.VMEM((2, 4, 2, ROWS, COLUMNS), BF16),
        mine=pltpu.VMEM((SLOTS, 4, 2, HALF, COLUMNS), BF16),
        core_in=pltpu.VMEM((2, 4, 2, HALF, COLUMNS), BF16),
        first_in=pltpu.VMEM((SLOTS, 4, HALF, COLUMNS), BF16),
        second_in=pltpu.VMEM((SLOTS, 2, HALF, COLUMNS), BF16),
        s_unit=dma((2, 4)),
        s_stage=dma((2,)),
        s_fetch=dma((32,)),
        swap_send=dma((3, 8)),
        swap_recv=dma((3, 8)),
        swap_own=dma((3,)),
        s_load=dma((2,)),
        s_core=dma((2,)),
        r_core=dma((2,)),
        s_first=dma((SLOTS, 2)),
        r_first=dma((SLOTS, 2)),
        s_second=dma((SLOTS, 2)),
        r_second=dma((SLOTS, 2)),
        s_far=dma((2,)),
        r_far=dma((number, 2)),
        s_near=dma((2,)),
        r_near=dma((number,)),
        s_own=dma((2,)),
    )
    vmem = pl.BlockSpec(memory_space=pltpu.VMEM)
    operands = dict(given, norm=norm, taps=taps, slope=slope)

    def body(*refs):
        refs = list(refs)
        cut = lambda n: [refs.pop(0) for _ in range(n)]
        plain, full_refs, made_refs = cut(len(operands)), cut(count), cut(len(outs))
        out_refs, grad_refs = cut(count), cut(count)
        backward_kernel(
            units,
            list(operands) + list(outs) + list(scratch) + ["fulls", "outs", "grads"],
            *plain,
            *made_refs,
            *refs,
            full_refs,
            out_refs,
            grad_refs,
        )

    results = pl.pallas_call(
        body,
        out_shape=list(outs.values())
        + [jax.ShapeDtypeStruct(s, BF16) for s in shapes]
        + [jax.ShapeDtypeStruct((4, 2) + s, BF16) for s in shapes],
        in_specs=[ANY] * len(given) + [vmem] * 3 + [ANY] * count,
        out_specs=[ANY] * (len(outs) + 2 * count),
        scratch_shapes=list(scratch.values()),
        compiler_params=pltpu.CompilerParams(
            collective_id=collective_id, has_side_effects=True, vmem_limit_bytes=62 * 2**20
        ),
    )(*operands.values(), *fulls)
    return results[: len(outs)], results[len(outs) : len(outs) + count]


def per_device(
    frames_in,
    noise,
    lengths,
    span_starts,
    w_in1,
    w_out1,
    w_qkv,
    w_attn,
    w_point1,
    w_point2,
    w_in2,
    w_out2,
    norm_params,
    kernel,
    slopes,
    cotangent,
):
    utterances, frames, width = frames_in.shape
    heads = slopes.shape[0]
    length = frames * 8
    frame_pos = lax.axis_index("seq") * frames + jnp.arange(frames, dtype=jnp.int32)
    span_begin = span_starts[:, :, None]
    masked = jnp.any(
        (span_begin <= frame_pos[None, None, :]) & (frame_pos[None, None, :] < span_begin + SPAN),
        axis=1,
    )
    start = jnp.where(masked[..., None], noise, frames_in)
    lens = jnp.broadcast_to(lengths.astype(F32)[:, None, None], (utterances, 8, 128))
    slope_rows = jnp.broadcast_to(slopes[:, None], (heads, length))
    shards = (w_in1, w_out1, w_qkv, w_attn, w_point1, w_point2, w_in2, w_out2)
    made, fulls = forward(start, lens, cotangent, norm_params, kernel, slope_rows, shards, 0)
    (block_out, dframes, small), grads = backward(made, fulls, norm_params, kernel, slope_rows, 1)
    small = jnp.sum(small.astype(F32), axis=0)
    grad_frames = jnp.where(masked[..., None], 0.0, dframes.astype(F32))
    return (
        block_out,
        grad_frames,
        *[grad.astype(F32) for grad in grads],
        small[:12].reshape(6, 2, width),
        small[12:17],
        small[17 : 17 + heads, 0],
    )


def solution(mesh):
    in_specs = (
        P("dp", "seq", None),
        P("dp", "seq", None),
        P("dp"),
        P("dp", None),
        P("seq", None),
        P("seq", None),
        P("seq", None),
        P("seq", None),
        P("seq", None),
        P("seq", None),
        P("seq", None),
        P("seq", None),
        P(),
        P(),
        P(),
        P("dp", "seq", None),
    )
    out_specs = (
        P("dp", "seq", None),
        P("dp", "seq", None),
        P(("dp", "seq"), None),
        P(("dp", "seq"), None),
        P(("dp", "seq"), None),
        P(("dp", "seq"), None),
        P(("dp", "seq"), None),
        P(("dp", "seq"), None),
        P(("dp", "seq"), None),
        P(("dp", "seq"), None),
        P("dp", None, None),
        P("dp", None),
        P("dp"),
    )
    grouped = mesh.shape["seq"] == 8 and mesh.shape["dp"] == 4
    return jax.shard_map(
        per_device if grouped else per_device_any, mesh=mesh, in_specs=in_specs, out_specs=out_specs, check_vma=False
    )
```

```python
import functools
import types

import jax
import jax.numpy as jnp
from jax import lax
from jax.experimental import pallas as pl
from jax.experimental.pallas import tpu as pltpu
from jax.sharding import PartitionSpec as P

MESH = pl.DeviceIdType.MESH
BF16 = jnp.bfloat16
F32 = jnp.float32
ANY = pl.BlockSpec(memory_space=pl.ANY)

SPAN = 10


EPSILON = 1e-05
NEGATIVE = -1e30


def padded_2(shard, sides, width):
    for axis, dim in sides:
        peers, length = (lax.axis_size(axis), shard.shape[dim])
        up = [(i, (i + 1) % peers) for i in range(peers - 1)]
        down = [(j, i) for i, j in up]
        last = lax.slice_in_dim(shard, length - width, length, axis=dim)
        initial = lax.slice_in_dim(shard, 0, width, axis=dim)
        before = lax.ppermute(last, axis, up)
        after = lax.ppermute(initial, axis, down)
        shard = jnp.concatenate([before, shard, after], axis=dim)
    return shard


def layer_norm(inputs, gain_vec, shift_vec):
    average = jnp.mean(inputs, axis=-1, keepdims=True)
    centred = inputs - average
    variance = jnp.mean(centred * centred, axis=-1, keepdims=True)
    return centred * lax.rsqrt(variance + EPSILON) * gain_vec + shift_vec


def swish_norm(inputs, gain_vec, shift_vec):
    return jax.nn.silu(layer_norm(inputs, gain_vec, shift_vec))


def glu_gate(joined, live_rows):
    half_width = joined.shape[-1] // 2
    return joined[..., :half_width] * jax.nn.sigmoid(joined[..., half_width:]) * live_rows


def matmul(left_side, right_side):
    return jnp.dot(left_side, right_side, preferred_element_type=jnp.float32)


def matmul_right_t(left_side, right_side):
    return lax.dot_general(
        left_side, right_side, (((1,), (1,)), ((), ())), preferred_element_type=jnp.float32
    )


def matmul_left_t(left_side, right_side):
    return lax.dot_general(
        left_side, right_side, (((0,), (0,)), ((), ())), preferred_element_type=jnp.float32
    )


def block_scores(queries, keys, query_pos, key_pos, key_live, slopes, seq_length):
    factor = queries.shape[-1] ** (-0.5)
    scores = (
        jnp.einsum("uqhd,ukhd->uhqk", queries, keys, preferred_element_type=jnp.float32) * factor
    )
    distance = jnp.abs(query_pos[:, None] - key_pos[None, :]).astype(jnp.float32) / seq_length
    scores = scores - slopes[None, :, None, None] * distance[None, None]
    return (jnp.where(key_live[:, None, None, :], scores, NEGATIVE), distance)


def per_device_any(
    frames_in,
    noise,
    lengths,
    span_starts,
    w_in1,
    w_out1,
    w_qkv,
    w_attn,
    w_point1,
    w_point2,
    w_in2,
    w_out2,
    norm_params,
    kernel,
    slopes,
    cotangent,
):
    utterances, frames, model_width = frames_in.shape
    head_count = slopes.shape[0]
    head_dim = model_width // head_count
    row_count = utterances * frames
    tap_count = kernel.shape[0]
    half_taps = tap_count // 2
    factor = head_dim ** (-0.5)
    seq_length = frames * lax.axis_size("seq")
    first_frame = lax.axis_index("seq") * frames
    frame_pos = first_frame + jnp.arange(frames, dtype=jnp.int32)
    live_mask = frame_pos[None, :] < lengths[:, None]
    live_rows = live_mask.astype(jnp.float32).reshape(row_count, 1)
    span_begin = span_starts[:, :, None]
    masked = jnp.any(
        (span_begin <= frame_pos[None, None, :]) & (frame_pos[None, None, :] < span_begin + SPAN),
        axis=1,
    )
    start_in = (
        jnp.where(masked[..., None], noise, frames_in)
        .astype(jnp.float32)
        .reshape(row_count, model_width)
    )
    norm_gain = norm_params[:, 0]
    norm_shift = norm_params[:, 1]
    shards = (w_in1, w_out1, w_qkv, w_attn, w_point1, w_point2, w_in2, w_out2)
    gathered = (
        lax.all_gather(shards[0], "seq", axis=0, tiled=True),
        lax.all_gather(shards[1], "seq", axis=0, tiled=True),
        lax.all_gather(shards[2], "seq", axis=0, tiled=True),
        lax.all_gather(shards[3], "seq", axis=0, tiled=True),
        lax.all_gather(shards[4], "seq", axis=0, tiled=True),
        lax.all_gather(shards[5], "seq", axis=0, tiled=True),
        lax.all_gather(shards[6], "seq", axis=0, tiled=True),
        lax.all_gather(shards[7], "seq", axis=0, tiled=True),
    )
    full_in1, full_out1, full_qkv, full_attn, full_point1, full_point2, full_in2, full_out2 = (
        gathered
    )
    act_one = layer_norm(start_in, norm_gain[0], norm_shift[0]).astype(jnp.bfloat16)
    up_one = matmul(act_one, full_in1)
    hid_one = jax.nn.silu(up_one).astype(jnp.bfloat16)
    ffn_one = matmul(hid_one, full_out1)
    resid_one = start_in + 0.5 * ffn_one
    act_two = layer_norm(resid_one, norm_gain[1], norm_shift[1]).astype(jnp.bfloat16)
    packed = (
        matmul(act_two, full_qkv)
        .astype(jnp.bfloat16)
        .reshape(utterances, frames, 3, head_count, head_dim)
    )
    queries = packed[:, :, 0]
    keys = packed[:, :, 1]
    values = packed[:, :, 2]
    row_max = jnp.full((utterances, head_count, frames), NEGATIVE, jnp.float32)
    key_blk = lax.all_gather(keys, "seq", axis=1, tiled=True)
    value_blk = lax.all_gather(values, "seq", axis=1, tiled=True)
    amount = key_blk.shape[1]
    key_pos = jnp.arange(amount, dtype=jnp.int32)
    key_live = key_pos[None, :] < lengths[:, None]
    scores, distance = block_scores(
        queries, key_blk, frame_pos, key_pos, key_live, slopes, seq_length
    )
    new_max = jnp.maximum(row_max, jnp.max(scores, axis=-1))
    expd = jnp.exp(scores - new_max[..., None])
    row_sum = jnp.sum(expd, axis=-1)
    update = jnp.einsum(
        "uhqk,ukhd->uqhd", expd.astype(jnp.bfloat16), value_blk, preferred_element_type=jnp.float32
    )
    partial_value = update
    row_max, row_sum, partial_value = (new_max, row_sum, partial_value)
    attn_out = partial_value / jnp.transpose(row_sum, (0, 2, 1))[..., None]
    log_total = jnp.transpose(row_max + jnp.log(row_sum), (0, 2, 1))
    attn_low = attn_out.astype(jnp.bfloat16).reshape(row_count, model_width)
    attended = matmul(attn_low, full_attn)
    resid_two = resid_one + attended
    act_three = layer_norm(resid_two, norm_gain[2], norm_shift[2]).astype(jnp.bfloat16)
    joined = matmul(act_three, full_point1)
    gated = (
        glu_gate(joined, live_rows).astype(jnp.bfloat16).reshape(utterances, frames, model_width)
    )
    padded = padded_2(gated, (("seq", 1),), half_taps)
    depth = kernel[0] * padded[:, 0:frames].astype(jnp.float32)
    for position in range(1, tap_count):
        depth = depth + kernel[position] * padded[:, position : position + frames].astype(
            jnp.float32
        )
    depth = depth.reshape(row_count, model_width)
    act_four = swish_norm(depth, norm_gain[3], norm_shift[3]).astype(jnp.bfloat16)
    convolved = matmul(act_four, full_point2)
    resid_three = resid_two + convolved
    act_five = layer_norm(resid_three, norm_gain[4], norm_shift[4]).astype(jnp.bfloat16)
    up_two = matmul(act_five, full_in2)
    hid_two = jax.nn.silu(up_two).astype(jnp.bfloat16)
    ffn_two = matmul(hid_two, full_out2)
    resid_four = resid_three + 0.5 * ffn_two
    result = layer_norm(resid_four, norm_gain[5], norm_shift[5])
    gathered = (
        lax.all_gather(shards[0], "seq", axis=0, tiled=True),
        lax.all_gather(shards[1], "seq", axis=0, tiled=True),
        lax.all_gather(shards[2], "seq", axis=0, tiled=True),
        lax.all_gather(shards[3], "seq", axis=0, tiled=True),
        lax.all_gather(shards[4], "seq", axis=0, tiled=True),
        lax.all_gather(shards[5], "seq", axis=0, tiled=True),
        lax.all_gather(shards[6], "seq", axis=0, tiled=True),
        lax.all_gather(shards[7], "seq", axis=0, tiled=True),
    )
    full_in1, full_out1, full_qkv, full_attn, full_point1, full_point2, full_in2, full_out2 = (
        gathered
    )
    grad_result = cotangent.astype(jnp.float32).reshape(row_count, model_width)
    _, back_five = jax.vjp(layer_norm, resid_four, norm_gain[5], norm_shift[5])
    grad_four, gain_five, shift_five = back_five(grad_result)
    grad_ffn2 = (0.5 * grad_four).astype(jnp.bfloat16)
    _, back_silu2 = jax.vjp(jax.nn.silu, up_two)
    grad_up2 = back_silu2(matmul_right_t(grad_ffn2, full_out2))[0].astype(jnp.bfloat16)
    _, back_four = jax.vjp(layer_norm, resid_three, norm_gain[4], norm_shift[4])
    grad_norm4, gain_four, shift_four = back_four(matmul_right_t(grad_up2, full_in2))
    grad_three = grad_four + grad_norm4
    grad_conv = grad_three.astype(jnp.bfloat16)
    _, back_swish = jax.vjp(swish_norm, depth, norm_gain[3], norm_shift[3])
    grad_depth_f, gain_three, shift_three = back_swish(matmul_right_t(grad_conv, full_point2))
    grad_depth = grad_depth_f.astype(jnp.bfloat16).reshape(utterances, frames, model_width)
    grad_padded = padded_2(grad_depth, (("seq", 1),), half_taps)
    grad_depth_wide = grad_depth.astype(jnp.float32)
    grad_gated = jnp.zeros((utterances, frames, model_width), jnp.float32)
    kernel_rows = []
    for position in range(tap_count):
        lower = 2 * half_taps - position
        grad_gated = grad_gated + kernel[position] * grad_padded[:, lower : lower + frames].astype(
            jnp.float32
        )
        kernel_rows.append(
            jnp.sum(
                grad_depth_wide * padded[:, position : position + frames].astype(jnp.float32),
                axis=(0, 1),
            )
        )
    grad_kernel = jnp.stack(kernel_rows)
    _, back_gate = jax.vjp(lambda joined_in: glu_gate(joined_in, live_rows), joined)
    grad_joined = back_gate(grad_gated.reshape(row_count, model_width))[0].astype(jnp.bfloat16)
    _, back_three = jax.vjp(layer_norm, resid_two, norm_gain[2], norm_shift[2])
    grad_norm3, gain_two, shift_two = back_three(matmul_right_t(grad_joined, full_point1))
    grad_two = grad_three + grad_norm3
    grad_att = grad_two.astype(jnp.bfloat16)
    grad_heads = (
        matmul_right_t(grad_att, full_attn)
        .astype(jnp.bfloat16)
        .reshape(utterances, frames, head_count, head_dim)
    )
    spread = jnp.sum(grad_heads.astype(jnp.float32) * attn_out, axis=-1)
    log_total_t = jnp.transpose(log_total, (0, 2, 1))
    spread_t = jnp.transpose(spread, (0, 2, 1))
    grad_slope = jnp.zeros((head_count,), jnp.float32)
    key_blk = lax.all_gather(keys, "seq", axis=1, tiled=True)
    value_blk = lax.all_gather(values, "seq", axis=1, tiled=True)
    amount = key_blk.shape[1]
    key_pos = jnp.arange(amount, dtype=jnp.int32)
    key_live = key_pos[None, :] < lengths[:, None]
    scores, distance = block_scores(
        queries, key_blk, frame_pos, key_pos, key_live, slopes, seq_length
    )
    attn_prob = jnp.exp(scores - log_total_t[..., None])
    grad_prob = jnp.einsum(
        "uqhd,ukhd->uhqk", grad_heads, value_blk, preferred_element_type=jnp.float32
    )
    grad_exact = attn_prob * (grad_prob - spread_t[..., None])
    grad_scores = grad_exact.astype(jnp.bfloat16)
    grad_query = (
        jnp.einsum("uhqk,ukhd->uqhd", grad_scores, key_blk, preferred_element_type=jnp.float32)
        * factor
    )
    grad_slope = grad_slope - jnp.sum(grad_exact * distance[None, None], axis=(0, 2, 3))
    grad_query, grad_slope = (grad_query, grad_slope)
    query_blk = lax.all_gather(queries, "seq", axis=1, tiled=True)
    dhead_blk = lax.all_gather(grad_heads, "seq", axis=1, tiled=True)
    total_blk = lax.all_gather(log_total.astype(jnp.bfloat16), "seq", axis=1, tiled=True).astype(
        jnp.float32
    )
    spread_blk = lax.all_gather(spread.astype(jnp.bfloat16), "seq", axis=1, tiled=True).astype(
        jnp.float32
    )
    amount = query_blk.shape[1]
    query_pos = jnp.arange(amount, dtype=jnp.int32)
    scores, distance = block_scores(
        query_blk, keys, query_pos, frame_pos, live_mask, slopes, seq_length
    )
    attn_prob = jnp.exp(scores - jnp.transpose(total_blk, (0, 2, 1))[..., None])
    grad_value = jnp.einsum(
        "uhqk,uqhd->ukhd",
        attn_prob.astype(jnp.bfloat16),
        dhead_blk,
        preferred_element_type=jnp.float32,
    )
    grad_prob = jnp.einsum("uqhd,ukhd->uhqk", dhead_blk, values, preferred_element_type=jnp.float32)
    grad_scores = (
        attn_prob * (grad_prob - jnp.transpose(spread_blk, (0, 2, 1))[..., None])
    ).astype(jnp.bfloat16)
    grad_key = (
        jnp.einsum("uhqk,uqhd->ukhd", grad_scores, query_blk, preferred_element_type=jnp.float32)
        * factor
    )
    grad_key, grad_value = (grad_key, grad_value)
    grad_packed = (
        jnp.stack([grad_query, grad_key, grad_value], axis=2)
        .astype(jnp.bfloat16)
        .reshape(row_count, 3 * model_width)
    )
    _, back_two = jax.vjp(layer_norm, resid_one, norm_gain[1], norm_shift[1])
    grad_norm2, gain_one, shift_one = back_two(matmul_right_t(grad_packed, full_qkv))
    grad_one = grad_two + grad_norm2
    grad_ffn1 = (0.5 * grad_one).astype(jnp.bfloat16)
    _, back_silu1 = jax.vjp(jax.nn.silu, up_one)
    grad_up1 = back_silu1(matmul_right_t(grad_ffn1, full_out1))[0].astype(jnp.bfloat16)
    _, back_one = jax.vjp(layer_norm, start_in, norm_gain[0], norm_shift[0])
    grad_norm1, gain_zero, shift_zero = back_one(matmul_right_t(grad_up1, full_in1))
    grad_start = grad_one + grad_norm1
    grad_frames = jnp.where(
        masked[..., None], 0.0, grad_start.reshape(utterances, frames, model_width)
    )
    wide_pairs = (
        (act_one, grad_up1),
        (act_two, grad_packed),
        (attn_low, grad_att),
        (act_three, grad_joined),
        (act_four, grad_conv),
        (act_five, grad_up2),
    )
    wide = lax.psum_scatter(
        jnp.concatenate(
            [matmul_left_t(left_side, right_side) for left_side, right_side in wide_pairs], axis=1
        ).astype(jnp.bfloat16),
        "seq",
        scatter_dimension=0,
        tiled=True,
    ).astype(jnp.float32)
    tall_pairs = ((hid_one, grad_ffn1), (hid_two, grad_ffn2))
    tall = lax.psum_scatter(
        jnp.concatenate(
            [matmul_left_t(left_side, right_side) for left_side, right_side in tall_pairs], axis=1
        ).astype(jnp.bfloat16),
        "seq",
        scatter_dimension=0,
        tiled=True,
    ).astype(jnp.float32)
    hidden_width = w_in1.shape[1]
    column_cuts = [
        hidden_width,
        3 * model_width,
        model_width,
        2 * model_width,
        model_width,
        hidden_width,
    ]
    wide_parts = []
    column_start = 0
    for column_width in column_cuts:
        wide_parts.append(wide[:, column_start : column_start + column_width])
        column_start = column_start + column_width
    grad_in1, grad_qkv, grad_attn, grad_point1, grad_point2, grad_in2 = wide_parts
    grad_out1 = tall[:, :model_width]
    grad_out2 = tall[:, model_width:]
    grad_norms = jnp.stack(
        [
            jnp.stack([gain_zero, shift_zero]),
            jnp.stack([gain_one, shift_one]),
            jnp.stack([gain_two, shift_two]),
            jnp.stack([gain_three, shift_three]),
            jnp.stack([gain_four, shift_four]),
            jnp.stack([gain_five, shift_five]),
        ]
    )
    grad_norms, grad_kernel, grad_slope = (
        lax.psum(grad_norms.astype(jnp.bfloat16), "seq").astype(jnp.float32),
        lax.psum(grad_kernel.astype(jnp.bfloat16), "seq").astype(jnp.float32),
        lax.psum(grad_slope.astype(jnp.bfloat16), "seq").astype(jnp.float32),
    )
    block_out = result.astype(jnp.bfloat16).reshape(utterances, frames, model_width)
    return (
        block_out,
        grad_frames,
        grad_in1,
        grad_out1,
        grad_qkv,
        grad_attn,
        grad_point1,
        grad_point2,
        grad_in2,
        grad_out2,
        grad_norms,
        grad_kernel,
        grad_slope,
    )


def place():
    seq, dp = lax.axis_index("seq"), lax.axis_index("dp")
    return seq // 2, lax.rem(seq, 2), dp // 2, lax.rem(dp, 2)


def device(z, x, y, core):
    return (z * 2 + x, y * 2 + core)


def z_partners(z):
    return (z + 1 - 2 * lax.rem(z, 2), lax.rem(z + 2, 4), 3 - z)


def remote(source, target, send, recv, where):
    return pltpu.make_async_remote_copy(
        src_ref=source,
        dst_ref=target,
        send_sem=send,
        recv_sem=recv,
        device_id=where,
        device_id_type=MESH,
    )


def greet(partners, waits):
    barrier = pltpu.get_barrier_semaphore()
    for partner in partners:
        pl.semaphore_signal(barrier, inc=1, device_id=partner, device_id_type=MESH)
    pl.semaphore_wait(barrier, waits)


def utterance_of(z, x, core):
    return lax.rem(z, 2) * 4 + x * 2 + core


def home_of(utterance, y, group):
    return device(2 * group + utterance // 4, lax.rem(utterance // 2, 2), y, lax.rem(utterance, 2))


def bits_of(s):
    return s // 4, lax.rem(s // 2, 2), lax.rem(s, 2)


def flipped(bits, r):
    flips = (r // 4, r // 2 % 2, r % 2)
    return [1 - b if f else b for b, f in zip(bits, flips)]


def utterance_in_round(seq, r):
    b2, b1, b0 = bits_of(seq)
    out = flipped((b1, b0, b2), r)
    return out[0] * 4 + out[1] * 2 + out[2]


def seq_in_round(utterance, r):
    t2, t1, t0 = flipped(bits_of(utterance), r)
    return t0 * 4 + t2 * 2 + t1


def units_of(shapes):
    units = []
    for index, (rows, columns) in enumerate(shapes):
        for row in range(0, rows, 128):
            for column in range(0, columns, 1024):
                units.append((index, row, column))
    return units


ROWS = 128
HALF = 64
COLUMNS = 1024
LAGS = (0, 1, 2, 3, 5, 7, 8)
SPLIT = 384


def blocks(rows, size):
    def run(body):
        @pl.loop(0, rows // size, unroll=2)
        def _(i):
            body(pl.ds(pl.multiple_of(i * size, size), size))

    return run


def normalise(v, norm, i):
    average = jnp.mean(v, axis=-1, keepdims=True)
    centred = v - average
    variance = jnp.mean(centred * centred, axis=-1, keepdims=True)
    return centred * lax.rsqrt(variance + EPSILON) * norm[i, 0:1, :] + norm[i, 1:2, :]


TILE = 256


def sigmoid(v):
    return 0.5 * jnp.tanh(0.5 * v) + 0.5


def silu(v):
    return v * sigmoid(v)


def times_unit(left, weight, emit, poll):
    unit, loads = weight
    for n in range(COLUMNS // TILE):
        columns = pl.ds(n * TILE, TILE)
        loads[n].wait()
        emit(columns, jnp.dot(left[...], unit[:, :, :, columns].reshape(COLUMNS, TILE), preferred_element_type=F32))
        poll()


def score_block(q, k, slope_row, first, live_keys):
    shape = (q.shape[0], k.shape[0])
    scores = lax.dot_general(q, k, (((1,), (1,)), ((), ())), preferred_element_type=F32)
    rows = lax.broadcasted_iota(jnp.int32, shape, 0) + first
    keys = lax.broadcasted_iota(jnp.int32, shape, 1)
    distance = jnp.abs(rows - keys).astype(F32) * (1.0 / k.shape[0])
    scores = scores * (q.shape[1] ** -0.5) - slope_row * distance
    return jnp.where(keys.astype(F32) < live_keys, scores, NEGATIVE), distance


def softmax_block(scores):
    top = jnp.max(scores, axis=-1, keepdims=True)
    expd = jnp.exp(scores - top)
    return expd / jnp.sum(expd, axis=-1, keepdims=True)


QUERIES = 128
BLOCK = 32


def forward_kernel(units, names, *refs):
    r = types.SimpleNamespace(**dict(zip(names, refs)))
    norm, taps, slope = r.norm, r.taps, r.slope
    length, width = r.x.shape[1:]
    heads = slope.shape[0]
    head_dim = width // heads
    z, x, y, core = place()
    seq, group = z * 2 + x, z // 2
    utterance = utterance_of(z, x, core)
    same = group == core
    zs = z_partners(z)
    over_z = [device(other, x, y, core) for other in zs]
    over_x = device(z, 1 - x, y, core)
    over_y = device(z, x, 1 - y, core)
    over_core = device(z, x, y, 1 - core)
    mates = [utterance_in_round(seq, i) for i in range(8)]
    givers = [device(s // 2, lax.rem(s, 2), y, group) for s in [seq_in_round(utterance, i) for i in range(8)]]
    targets = [home_of(u, y, core) for u in mates]
    barrier = pltpu.get_barrier_semaphore()

    @pl.when(jnp.logical_not(same))
    def _():
        pl.semaphore_signal(barrier, inc=1, device_id=givers[0], device_id_type=MESH)

    for partner in givers[1:] + [over_z[0], over_z[2], over_x, over_y, over_core]:
        pl.semaphore_signal(barrier, inc=1, device_id=partner, device_id_type=MESH)
    pl.semaphore_wait(barrier, jnp.where(same, 12, 13))

    swaps = ((r.start, r.h0), (r.lens, r.lens_here), (r.cot, r.cot_out))

    def swap(i, j):
        source, target = swaps[i]
        return remote(source.at[mates[j]], target.at[seq], r.swap_send.at[i, j], r.swap_recv.at[i, j], targets[j])

    def swap_local(i):
        source, target = swaps[i]
        return pltpu.make_async_copy(source.at[mates[0]], target.at[seq], r.swap_own.at[i])

    def swap_start(i, j):
        if j > 0:
            swap(i, j).start()
            return

        @pl.when(jnp.logical_not(same))
        def _():
            swap(i, 0).start()

        @pl.when(same)
        def _():
            swap_local(i).start()

    def swap_wait(i):
        @pl.when(jnp.logical_not(same))
        def _():
            swap(i, 0).wait()

        @pl.when(same)
        def _():
            swap_local(i).wait()

        for j in range(1, 8):
            swap(i, j).wait()

    send, recv, own = r.send, r.recv, r.own
    shards, fulls = r.shards, r.fulls

    def spot(unit):
        index, row, column = unit
        rows = pl.ds(row + pl.multiple_of(core * HALF, HALF), HALF)
        mine = pl.ds(column + pl.multiple_of(y * SPLIT, 128), COLUMNS - SPLIT)
        third = pl.ds(column + pl.multiple_of(y * (COLUMNS - SPLIT), 128), SPLIT)
        return shards[index], fulls[index], rows, mine, third, pl.ds(column, COLUMNS)

    middle = (z == 1) | (z == 2)
    near_pair, far_pair = pl.ds(2 * (z // 2), 2), pl.ds(2 - 2 * (z // 2), 2)

    class Along:
        def __init__(self, copy, sends, gets):
            self.copy, self.sends, self.gets = copy, sends, gets

        def start(self):
            @pl.when(self.sends)
            def _():
                self.copy.start()

        def wait(self):
            @pl.when(self.sends)
            def _():
                self.copy.wait_send()

            @pl.when(self.gets)
            def _():
                self.copy.wait_recv()

    def first(u):
        shard, full, rows, mine, _, _ = spot(units[u])
        every = pl.ds(units[u][2], COLUMNS)
        return [
            remote(shard.at[rows, mine], full.at[z, x, rows, mine], send.at[u, 0], recv.at[u, 0], over_z[0]),
            pltpu.make_async_copy(shard.at[rows, every], full.at[z, x, rows, every], own.at[u]),
        ]

    def across(u):
        _, full, rows, mine, _, _ = spot(units[u])
        piece = full.at[near_pair, x, rows, mine]
        return [Along(remote(piece, piece, send.at[u, 1], recv.at[u, 1], over_z[2]), middle, middle)]

    def outward(u):
        _, full, rows, mine, _, _ = spot(units[u])
        piece = full.at[far_pair, x, rows, mine]
        copy = remote(piece, piece, send.at[u, 2], recv.at[u, 2], over_z[0])
        return [Along(copy, middle, jnp.logical_not(middle))]

    def second(u):
        _, full, rows, mine, _, _ = spot(units[u])
        piece = full.at[:, x, rows, mine]
        return [remote(piece, piece, send.at[u, 3], recv.at[u, 3], over_x)]

    def third(u):
        _, full, rows, _, part, _ = spot(units[u])
        pieces = [full.at[:, 1 - x, rows, part]] + [full.at[other, x, rows, part] for other in zs]
        out = [remote(p, p, send.at[u, 4 + j], recv.at[u, 4 + j], over_y) for j, p in enumerate(pieces)]
        return out

    def fourth(u):
        _, full, rows, _, _, whole = spot(units[u])
        piece = full.at[:, :, rows, whole]
        return [remote(piece, piece, send.at[u, 8], recv.at[u, 8], over_core)]

    stages = (first, across, outward, second, third, fourth)
    last = len(units)
    done = [0]

    actions = []
    ends = {}

    def move(u, depth):
        def act_on():
            if depth > 0:
                for copy in stages[depth - 1](u):
                    copy.wait()
            if depth < len(stages):
                for copy in stages[depth](u):
                    copy.start()

        return act_on

    for step in range(last + LAGS[-1]):
        for depth, lag in reversed(list(enumerate(LAGS))):
            if 0 <= step - lag < last:
                actions.append(move(step - lag, depth))
                if depth == len(stages):
                    ends[step - lag] = len(actions)
        if 12 <= step < 20:
            actions.append(functools.partial(swap_start, 2, step - 12))

    def poll(count=1):
        for _ in range(count):
            if done[0] < len(actions):
                actions[done[0]]()
                done[0] += 1

    taken = [0]

    def weight():
        u = taken[0]
        taken[0] += 1
        while done[0] < ends[u]:
            poll()
        index, row, column = units[u]
        loads = []
        for n in range(COLUMNS // TILE):
            source = fulls[index].at[:, :, pl.ds(row, ROWS), pl.ds(column + n * TILE, TILE)]
            target = r.unit.at[u % 2, :, :, :, pl.ds(n * TILE, TILE)]
            copy = pltpu.make_async_copy(source, target, r.load.at[u % 2, n])
            copy.start()
            loads.append(copy)
        return r.unit.at[u % 2], loads

    kept = []

    def keep(source, target):
        copy = pltpu.make_async_copy(source, target, r.kept.at[len(kept)])
        copy.start()
        kept.append(copy)

    xs, act, acc = r.x, r.act, r.acc
    poll()
    for j in range(8):
        swap_start(0, j)
    for j in range(8):
        swap_start(1, j)
    poll(4)
    swap_wait(0)

    @blocks(length, BLOCK)
    def _(rows):
        xs[0, rows, :] = r.h0[rows.start // 64, pl.ds(pl.multiple_of(lax.rem(rows.start, 64), BLOCK), BLOCK), :].astype(F32)
        act[rows, :] = normalise(xs[0, rows, :], norm, 0).astype(BF16)

    keep(r.h0, r.h0_out)

    def feed_forward(x_in, x_out, up, up_out):
        hidden = r.hidden
        for p in range(4):
            unit, loads = weight()

            for n in range(COLUMNS // TILE):
                columns = pl.ds(n * TILE, TILE)
                loads[n].wait()
                value = jnp.dot(act[...], unit[:, :, :, columns].reshape(COLUMNS, TILE), preferred_element_type=F32)
                up[p, :, columns] = value.astype(BF16)
                value = silu(value).astype(BF16)
                for t in range(2 * n, 2 * n + 2):
                    place_at = pl.ds((2 * p + t // 4) * 128, 128)
                    hidden[t % 4, :, place_at] = value[:, (t - 2 * n) * 128 : (t - 2 * n + 1) * 128]
                poll()

            keep(up.at[p], up_out.at[:, pl.ds(p * COLUMNS, COLUMNS)])
        for q in range(4):
            def emit(columns, value, q=q):
                if q == 0:
                    acc[:, columns] = value
                else:
                    acc[:, columns] = acc[:, columns] + value

            times_unit(hidden.at[q], weight(), emit, poll)

        @blocks(length, BLOCK)
        def _(rows):
            xs[x_out, rows, :] = xs[x_in, rows, :] + 0.5 * acc[rows, :]

    feed_forward(0, 1, r.up, r.u1_out)
    keep(xs.at[1], r.x1_out)

    @blocks(length, BLOCK)
    def _(rows):
        act[rows, :] = normalise(xs[1, rows, :], norm, 1).astype(BF16)

    qkv = r.qkv
    for i in range(3):

        def emit(columns, value, i=i):
            qkv[i, :, columns] = value.astype(BF16)

        times_unit(act, weight(), emit, poll)
    keep(qkv, r.qkv_out)
    swap_wait(1)
    live_count = r.lens_here[0, 0:1, 0:1]
    keep(r.lens_here, r.lens_out)
    attended = r.attended
    for h in range(heads):
        columns = pl.ds(h * head_dim, head_dim)

        @blocks(length, QUERIES)
        def _(rows, h=h, columns=columns):
            scores, _ = score_block(
                qkv[0, rows, columns], qkv[1, :, columns], slope[h : h + 1, :], rows.start, live_count
            )
            prob = softmax_block(scores).astype(BF16)
            attended[rows, columns] = jnp.dot(prob, qkv[2, :, columns], preferred_element_type=F32).astype(BF16)

        poll(2)
    keep(attended, r.attended_out)

    def add_to(x_in, x_out):
        def emit(columns, value):
            xs[x_out, :, columns] = xs[x_in, :, columns] + value

        return emit

    times_unit(attended, weight(), add_to(1, 2), poll)
    keep(xs.at[2], r.x2_out)

    @blocks(length, BLOCK)
    def _(rows):
        act[rows, :] = normalise(xs[2, rows, :], norm, 2).astype(BF16)

    gates, gated = r.gates, r.gated

    def emit(columns, value):
        acc[:, columns] = value
        gates[0, :, columns] = value.astype(BF16)

    times_unit(act, weight(), emit, poll)
    gated[0:8, :] = jnp.zeros((8, width), F32)
    gated[length + 8 : length + 16, :] = jnp.zeros((8, width), F32)

    def emit(columns, value):
        gates[1, :, columns] = value.astype(BF16)
        live = lax.broadcasted_iota(jnp.int32, value.shape, 0).astype(F32) < live_count
        passed = jnp.where(live, acc[:, columns] * sigmoid(value), 0.0)
        gated[pl.ds(8, length), columns] = passed.astype(BF16).astype(F32)

    times_unit(act, weight(), emit, poll)
    keep(gates, r.gates_out)
    keep(gated, r.gated_out)
    depth = r.depth

    @blocks(length, BLOCK)
    def _(rows):
        near = gated[pl.ds(pl.multiple_of(rows.start, BLOCK), BLOCK + 16), :]
        total = taps[0:1, :] * near[6 : 6 + BLOCK]
        for t in range(1, taps.shape[0]):
            total = total + taps[t : t + 1, :] * near[6 + t : 6 + t + BLOCK]
        depth[rows, :] = total
        value = normalise(total, norm, 3)
        act[rows, :] = (silu(value)).astype(BF16)

    keep(depth, r.depth_out)
    times_unit(act, weight(), add_to(2, 3), poll)
    keep(xs.at[3], r.x3_out)

    @blocks(length, BLOCK)
    def _(rows):
        act[rows, :] = normalise(xs[3, rows, :], norm, 4).astype(BF16)

    feed_forward(3, 4, r.up2, r.u2_out)
    keep(xs.at[4], r.x4_out)

    @blocks(length, BLOCK)
    def _(rows):
        act[rows, :] = normalise(xs[4, rows, :], norm, 5).astype(BF16)

    keep(act, r.result_out)
    swap_wait(2)
    for copy in kept:
        copy.wait()


def forward(start, lens, cot, norm, taps, slope, shards, collective_id):
    shapes = [s.shape for s in shards]
    units = units_of(shapes)
    width = norm.shape[-1]
    frames = start.shape[1]
    length = 8 * frames
    count = len(shards)
    dma = pltpu.SemaphoreType.DMA
    hidden = shapes[0][1]
    wide = lambda *lead: jax.ShapeDtypeStruct(lead + (length, width), F32)
    low = lambda *lead: jax.ShapeDtypeStruct(lead + (length, width), BF16)
    up = jax.ShapeDtypeStruct((length, hidden), BF16)
    outs = dict(
        cot_out=jax.ShapeDtypeStruct(cot.shape, cot.dtype),
        h0_out=jax.ShapeDtypeStruct(start.shape, start.dtype),
        u1_out=up,
        x1_out=wide(),
        qkv_out=low(3),
        attended_out=low(),
        x2_out=wide(),
        gates_out=low(2),
        gated_out=jax.ShapeDtypeStruct((length + 16, width), F32),
        depth_out=wide(),
        x3_out=wide(),
        u2_out=up,
        x4_out=wide(),
        result_out=low(),
        lens_out=jax.ShapeDtypeStruct(lens.shape, lens.dtype),
    )
    scratch = dict(
        h0=pltpu.VMEM(start.shape, BF16),
        lens_here=pltpu.VMEM(lens.shape, F32),
        x=pltpu.VMEM((5, length, width), F32),
        act=pltpu.VMEM((length, width), BF16),
        acc=pltpu.VMEM((length, width), F32),
        hidden=pltpu.VMEM((4, length, width), BF16),
        up=pltpu.VMEM((4, length, width), BF16),
        up2=pltpu.VMEM((4, length, width), BF16),
        qkv=pltpu.VMEM((3, length, width), BF16),
        attended=pltpu.VMEM((length, width), BF16),
        gates=pltpu.VMEM((2, length, width), BF16),
        gated=pltpu.VMEM((length + 16, width), F32),
        depth=pltpu.VMEM((length, width), F32),
        unit=pltpu.VMEM((2, 4, 2, ROWS, COLUMNS), BF16),
        load=dma((2, COLUMNS // TILE)),
        swap_send=dma((3, 8)),
        swap_recv=dma((3, 8)),
        swap_own=dma((3,)),
        send=dma((len(units), 9)),
        recv=dma((len(units), 9)),
        own=dma((len(units),)),
        kept=dma((32,)),
    )
    names = ["start", "lens", "cot", "norm", "taps", "slope"]
    vmem = pl.BlockSpec(memory_space=pltpu.VMEM)

    def body(*refs):
        plain, rest = refs[:6], refs[6:]
        ours, rest = rest[:count], rest[count:]
        made, rest = rest[: len(outs)], rest[len(outs) :]
        fulls, rest = rest[:count], rest[count:]
        forward_kernel(
            units,
            names + list(outs) + list(scratch) + ["shards", "fulls"],
            *plain,
            *made,
            *rest,
            ours,
            fulls,
        )

    results = pl.pallas_call(
        body,
        out_shape=list(outs.values()) + [jax.ShapeDtypeStruct((4, 2) + s, BF16) for s in shapes],
        in_specs=[ANY, ANY, ANY, vmem, vmem, vmem] + [ANY] * count,
        out_specs=[ANY] * (len(outs) + count),
        scratch_shapes=list(scratch.values()),
        compiler_params=pltpu.CompilerParams(
            collective_id=collective_id, has_side_effects=True, vmem_limit_bytes=60 * 2**20
        ),
    )(start, lens, cot, norm, taps, slope, *shards)
    made = types.SimpleNamespace(**dict(zip(outs, results[: len(outs)])))
    fulls = [f.reshape(8 * s[0], s[1]) for f, s in zip(results[len(outs) :], shapes)]
    return made, fulls


CADENCE = 12.0
SLOTS = 7


def norm_back(v, dy, norm, i, sums):
    average = jnp.mean(v, axis=-1, keepdims=True)
    centred = v - average
    scale = lax.rsqrt(jnp.mean(centred * centred, axis=-1, keepdims=True) + EPSILON)
    unit = centred * scale
    sums[2 * i] += jnp.sum((dy * unit).reshape(-1, 8, dy.shape[-1]), axis=0)
    sums[2 * i + 1] += jnp.sum(dy.reshape(-1, 8, dy.shape[-1]), axis=0)
    inner = dy * norm[i, 0:1, :]
    return scale * (
        inner
        - jnp.mean(inner, axis=-1, keepdims=True)
        - unit * jnp.mean(inner * unit, axis=-1, keepdims=True)
    )


def silu_back(v):
    s = sigmoid(v)
    return s * (1.0 + v * (1.0 - s))


def times_t(left, right):
    return lax.dot_general(left, right, (((1,), (1,)), ((), ())), preferred_element_type=F32)


def t_times(left, right):
    return lax.dot_general(left, right, (((0,), (0,)), ((), ())), preferred_element_type=F32)


BACK_ORDER = (7, 6, 5, 4, 3, 2, 1, 0)


def backward_kernel(units, names, *refs):
    r = types.SimpleNamespace(**dict(zip(names, refs)))
    norm, taps, slope, sums = r.norm, r.taps, r.slope, r.sums
    length, width = r.dx.shape
    heads = slope.shape[0]
    head_dim = width // heads
    z, x, y, core = place()
    seq, group = z * 2 + x, z // 2
    utterance = utterance_of(z, x, core)
    keeps = group == core
    other = jnp.logical_not(keeps)
    z_other = z + 1 - 2 * lax.rem(z, 2)
    over_core = device(z, x, y, 1 - core)
    over_x = device(z, 1 - x, y, core)
    over_z = device(z_other, x, y, core)
    far = device(3 - z, x, y, group)
    seqs = [seq_in_round(utterance, i) for i in range(8)]
    targets = [device(s // 2, lax.rem(s, 2), y, group) for s in seqs]
    givers = [home_of(utterance_in_round(seq, i), y, core) for i in range(8)]
    barrier = pltpu.get_barrier_semaphore()
    for partner in [over_core, over_x, over_z] + givers[1:]:
        pl.semaphore_signal(barrier, inc=1, device_id=partner, device_id_type=MESH)

    @pl.when(other)
    def _():
        for giver in [device(3 - z, x, y, 0), device(3 - z, x, y, 1), givers[0]]:
            pl.semaphore_signal(barrier, inc=1, device_id=giver, device_id_type=MESH)

    pl.semaphore_wait(barrier, jnp.where(keeps, 11, 12))

    swaps = ((r.result, r.result_home), (r.cot_here, r.dframes_home), (r.small, r.small_home))

    def swap(i, j):
        source, target = swaps[i][0], swaps[i][1].at[utterance]
        block = source if i == 2 else source.at[seqs[j]]
        return remote(block, target, r.swap_send.at[i, j], r.swap_recv.at[i, j], targets[j])

    def swap_local(i):
        source, target = swaps[i][0], swaps[i][1].at[utterance]
        return pltpu.make_async_copy(source if i == 2 else source.at[seqs[0]], target, r.swap_own.at[i])

    def swap_start(i, j):
        if j > 0:
            swap(i, j).start()
            return

        @pl.when(other)
        def _():
            swap(i, 0).start()

        @pl.when(keeps)
        def _():
            swap_local(i).start()

    def swap_wait(i):
        @pl.when(other)
        def _():
            swap(i, 0).wait()

        @pl.when(keeps)
        def _():
            swap_local(i).wait()

        for j in range(1, 8):
            swap(i, j).wait()

    grads, outs, mine, core_in, first_in, second_in = (
        r.grads, r.outs, r.mine, r.core_in, r.first_in, r.second_in
    )
    half = pl.multiple_of(core * HALF, HALF)
    other_half = pl.multiple_of((1 - core) * HALF, HALF)
    last = len(units)

    def columns_of(u):
        return pl.ds(units[u][2], COLUMNS)

    def core_copy(u):
        source = grads[units[u][0]].at[:, :, pl.ds(units[u][1] + other_half, HALF), columns_of(u)]
        return remote(source, core_in.at[u % 2], r.s_core.at[u % 2], r.r_core.at[u % 2], over_core)

    def load_copy(u):
        source = grads[units[u][0]].at[:, :, pl.ds(units[u][1] + half, HALF), columns_of(u)]
        return pltpu.make_async_copy(source, mine.at[u % SLOTS], r.s_load.at[u % 2])

    def swapped(u):
        return u % 8 == 2

    def first_copies(u):
        slot = u % SLOTS
        held, arriving, send, recv = mine.at[slot], first_in.at[slot], r.s_first.at[slot], r.r_first.at[slot]
        if swapped(u):
            return [
                remote(held.at[t], arriving.at[pl.ds(2 * i, 2)], send.at[i], recv.at[i], over_z)
                for i, t in enumerate((z_other, 3 - z_other))
            ]
        return [remote(held.at[:, 1 - x], arriving, send.at[0], recv.at[0], over_x)]

    def second_copies(u):
        slot = u % SLOTS
        held, arriving, send, recv = mine.at[slot], second_in.at[slot], r.s_second.at[slot], r.r_second.at[slot]
        if swapped(u):
            pairs, partner = ((z, 1 - x), (3 - z, 1 - x)), over_x
        else:
            pairs, partner = ((z_other, x), (3 - z_other, x)), over_z
        return [
            remote(held.at[t, t_x], arriving.at[i], send.at[i], recv.at[i], partner)
            for i, (t, t_x) in enumerate(pairs)
        ]

    def far_copy(u, giver=None):
        start = half if giver is None else giver * HALF
        target = outs[units[u][0]].at[pl.ds(units[u][1] + start, HALF), columns_of(u)]
        recv = r.r_far.at[u, core if giver is None else giver]
        return remote(mine.at[u % SLOTS, 3 - z, x], target, r.s_far.at[u % 2], recv, far)

    def near_target(u, start):
        return outs[units[u][0]].at[pl.ds(units[u][1] + start, HALF), columns_of(u)]

    def near_copy(u, start):
        return remote(
            mine.at[u % SLOTS, z, x], near_target(u, start), r.s_near.at[u % 2], r.r_near.at[u], over_core
        )

    def near_local(u):
        return pltpu.make_async_copy(mine.at[u % SLOTS, z, x], near_target(u, half), r.s_own.at[u % 2])

    def add(into, more):
        into[...] = (into[...].astype(F32) + more[...].astype(F32)).astype(BF16)

    def stage0(u):
        load_copy(u).start()
        core_copy(u).start()

    def stage1(u):
        load_copy(u).wait()
        core_copy(u).wait()
        held, arrived = mine.at[u % SLOTS], core_in.at[u % 2]
        if swapped(u):
            sent = [(t, t_x) for t in (z_other, 3 - z_other) for t_x in (0, 1)]
            rest = [(t, t_x) for t in (z, 3 - z) for t_x in (0, 1)]
        else:
            sent, rest = [(t, 1 - x) for t in range(4)], [(t, x) for t in range(4)]
        for t in sent:
            add(held.at[t], arrived.at[t])
        for copy in first_copies(u):
            copy.start()
        for t in rest:
            add(held.at[t], arrived.at[t])

    def stage2(u):
        for copy in first_copies(u):
            copy.wait()
        held, arrived = mine.at[u % SLOTS], first_in.at[u % SLOTS]
        if swapped(u):
            sent = [((t, 1 - x), 2 * i + 1 - x) for i, t in enumerate((z, 3 - z))]
            rest = [((t, x), 2 * i + x) for i, t in enumerate((z, 3 - z))]
        else:
            sent = [((t, x), t) for t in (z_other, 3 - z_other)]
            rest = [((t, x), t) for t in (z, 3 - z)]
        for (t, i), copy in zip(sent, second_copies(u)):
            add(held.at[t], arrived.at[i])
            copy.start()
        for t, i in rest:
            add(held.at[t], arrived.at[i])

    def stage3(u):
        for copy in second_copies(u):
            copy.wait()
        held, arrived = mine.at[u % SLOTS], second_in.at[u % SLOTS]
        add(held.at[3 - z, x], arrived.at[1])
        far_copy(u).start()
        add(held.at[z, x], arrived.at[0])

        @pl.when(keeps)
        def _():
            near_local(u).start()

        @pl.when(other)
        def _():
            near_copy(u, half).start()

    def stage4(u):
        far_copy(u).wait_send()

        @pl.when(keeps)
        def _():
            near_local(u).wait()
            near_copy(u, other_half).wait_recv()

        @pl.when(other)
        def _():
            near_copy(u, half).wait_send()

    order = ((stage1, 1), (stage0, 0), (stage2, 3), (stage3, 5), (stage4, 6))
    ticks, emitted, clock = [0], [0], [0.0]

    def tick():
        step = ticks[0]
        ticks[0] += 1
        settle(min(step + 1, last))
        for stage, depth in order:
            if 0 <= step - depth < last:
                stage(step - depth)

    def spent(us):
        if emitted[0] == 0:
            return
        clock[0] += us
        while clock[0] >= CADENCE:
            clock[0] -= CADENCE
            if ticks[0] < emitted[0]:
                tick()

    stored = [0]

    def stage_copy(u):
        target = grads[units[u][0]].at[:, :, pl.ds(units[u][1], ROWS), columns_of(u)]
        return pltpu.make_async_copy(r.stage.at[u % 2], target, r.s_stage.at[u % 2])

    def settle(count):
        while stored[0] < count:
            stage_copy(stored[0]).wait()
            stored[0] += 1

    def emit(left, right):
        u = emitted[0]
        stage = r.stage.at[u % 2]
        settle(u - 1)
        for t in range(4):
            value = t_times(left[:, pl.ds(t * 256, 256)], right[...])
            stage[t] = value.astype(BF16).reshape(2, ROWS, COLUMNS)
        stage_copy(u).start()
        emitted[0] += 1
        if u == 0:
            tick()
        spent(3.0)

    wanted = []
    for index in BACK_ORDER:
        rows, columns = r.fulls[index].shape
        for row in range(0, rows, 1024):
            for column in range(0, columns, 1024):
                wanted.append((index, row, column))

    def weight_copies(i):
        index, row, column = wanted[i]
        return [
            pltpu.make_async_copy(
                r.fulls[index].at[pl.ds(row + 256 * t, 256), pl.ds(column, 1024)],
                r.unit.at[i % 2, t],
                r.s_unit.at[i % 2, t],
            )
            for t in range(4)
        ]

    taken = [0]

    def weight():
        i = taken[0]
        taken[0] += 1
        if i + 1 < len(wanted):
            for copy in weight_copies(i + 1):
                copy.start()
        return r.unit.at[i % 2], weight_copies(i)

    def times_matrix(left, take):
        unit, copies = weight()
        for t in range(4):
            copies[t].wait()
            take(pl.ds(t * 256, 256), times_t(left[...], unit[t]))
        spent(2.5)

    def into_total(q):
        def take(columns, value):
            if q == 0:
                r.total[:, columns] = value
            else:
                r.total[:, columns] = r.total[:, columns] + value

        return take

    fetched = {}

    def fetch(name, source, target):
        fetched[name] = pltpu.make_async_copy(source, target, r.s_fetch.at[len(fetched)])
        fetched[name].start()

    def arrived(*wanted_names):
        for name in wanted_names:
            fetched[name].wait()

    xs, dx, total, low, act, up, du, hidden = (
        r.xs, r.dx, r.total, r.low, r.act, r.up, r.du, r.hidden
    )
    fetch("x4", r.x4, xs.at[0])
    fetch("cot", r.cot, r.cot_here)
    for p in range(4):
        fetch(("u2", p), r.u2.at[:, pl.ds(p * COLUMNS, COLUMNS)], up.at[p])
    for copy in weight_copies(0):
        copy.start()
    fetch("x3", r.x3, xs.at[1])
    fetch("depth", r.depth, r.depth_here)
    fetch("gates", r.gates, r.gates_here)
    fetch("gated", r.gated, r.gated_here)
    fetch("qkv", r.qkv, r.qkv_here)
    fetch("attended", r.attended, r.attended_here)
    fetch("lens", r.lens, r.lens_here)
    fetch("h0", r.h0, r.h0_here)
    for j in range(8):
        swap_start(0, j)
    sums[...] = jnp.zeros(sums.shape, F32)
    arrived("x4", "cot")

    def frame_block(ref, rows):
        return ref[rows.start // 64, pl.ds(pl.multiple_of(lax.rem(rows.start, 64), BLOCK), BLOCK), :]

    @blocks(length, BLOCK)
    def _(rows):
        grad = norm_back(xs[0, rows, :], frame_block(r.cot_here, rows).astype(F32), norm, 5, sums)
        dx[rows, :] = grad
        low[rows, :] = (0.5 * grad).astype(BF16)

    fetch("x2", r.x2, xs.at[0])

    def feed_forward_back(kind, x_slot, norm_index, write):
        arrived(*[(kind, p) for p in range(4)])
        for p in range(4):

            @pl.loop(0, 8)
            def _(t):
                value = up[p, :, pl.ds(pl.multiple_of(t * 128, 128), 128)].astype(F32)
                place_at = pl.ds(pl.multiple_of((2 * p + t // 4) * 128, 128), 128)
                hidden[lax.rem(t, 4), :, place_at] = silu(value).astype(BF16)

        for q in range(4):
            emit(hidden.at[q], low)
        for p in range(4):

            def take(columns, value, p=p):
                du[p, :, columns] = (value * silu_back(up[p, :, columns].astype(F32))).astype(BF16)

            times_matrix(low, take)
            spent(1.0)
        for p in range(4):
            times_matrix(du.at[p], into_total(p))
        write()
        for p in range(4):
            emit(act, du.at[p])

    def block_norm(x_slot, norm_index):
        @blocks(length, BLOCK)
        def _(rows):
            act[rows, :] = normalise(xs[x_slot, rows, :], norm, norm_index).astype(BF16)

        spent(3.0)

    def block_norm_back(x_slot, norm_index, factor):
        @blocks(length, BLOCK)
        def _(rows):
            grad = dx[rows, :] + norm_back(xs[x_slot, rows, :], total[rows, :], norm, norm_index, sums)
            dx[rows, :] = grad
            low[rows, :] = (factor * grad).astype(BF16)

        spent(5.0)

    def after_two():
        arrived("x3")
        block_norm(1, 4)

    feed_forward_back("u2", 1, 4, after_two)
    for p in range(4):
        fetch(("u1", p), r.u1.at[:, pl.ds(p * COLUMNS, COLUMNS)], up.at[p])
    block_norm_back(1, 4, 1.0)
    fetch("x1", r.x1, xs.at[1])

    depth, gates, gated, spread = r.depth_here, r.gates_here, r.gated_here, r.spread
    arrived("depth", "gated", "gates", "lens")
    live_count = r.lens_here[0, 0:1, 0:1]

    @blocks(length, BLOCK)
    def _(rows):
        act[rows, :] = silu(normalise(depth[rows, :], norm, 3)).astype(BF16)

    emit(act, low)
    times_matrix(low, into_total(0))
    spread[0:8, :] = jnp.zeros((8, width), F32)
    spread[length + 8 : length + 16, :] = jnp.zeros((8, width), F32)

    @blocks(length, BLOCK)
    def _(rows):
        inner = depth[rows, :]
        dy = total[rows, :] * silu_back(normalise(inner, norm, 3))
        grad = norm_back(inner, dy, norm, 3, sums).astype(BF16).astype(F32)
        spread[pl.ds(pl.multiple_of(rows.start, BLOCK) + 8, BLOCK), :] = grad

    spent(6.0)

    @blocks(length, BLOCK)
    def _(rows):
        around = pl.ds(pl.multiple_of(rows.start, BLOCK), BLOCK + 16)
        near = spread[around, :]
        passed = gated[around, :]
        here = near[8 : 8 + BLOCK]
        grad = jnp.zeros((BLOCK, width), F32)
        for t in range(taps.shape[0]):
            grad = grad + taps[t : t + 1, :] * near[10 - t : 10 - t + BLOCK]
            product = here * passed[6 + t : 6 + t + BLOCK]
            sums[12 + t] += jnp.sum(product.reshape(-1, 8, width), axis=0)
        live = lax.broadcasted_iota(jnp.int32, (BLOCK, width), 0) + rows.start
        grad = jnp.where(live.astype(F32) < live_count, grad, 0.0)
        opened = sigmoid(gates[1, rows, :].astype(F32))
        du[0, rows, :] = (grad * opened).astype(BF16)
        du[1, rows, :] = (grad * gates[0, rows, :].astype(F32) * opened * (1.0 - opened)).astype(BF16)

    arrived("x2")
    spent(8.0)
    block_norm(0, 2)
    for p in range(2):
        emit(act, du.at[p])
        times_matrix(du.at[p], into_total(p))
    block_norm_back(0, 2, 1.0)

    qkv, heads_grad, sides = r.qkv_here, act, r.sides
    arrived("attended", "qkv")
    emit(r.attended_here, low)

    def take(columns, value):
        heads_grad[:, columns] = value.astype(BF16)

    times_matrix(low, take)
    for h in range(heads):
        columns = pl.ds(h * head_dim, head_dim)
        sides[...] = jnp.zeros(sides.shape, F32)

        @blocks(length, QUERIES)
        def _(rows, h=h, columns=columns):
            q, k, v = qkv[0, rows, columns], qkv[1, :, columns], qkv[2, :, columns]
            do = heads_grad[rows, columns]
            scores, distance = score_block(q, k, slope[h : h + 1, :], rows.start, live_count)
            prob = softmax_block(scores)
            dp = times_t(do, v)
            exact = prob * (dp - jnp.sum(prob * dp, axis=-1, keepdims=True))
            sums[17 + h, :, 0:length] -= jnp.sum((exact * distance).reshape(-1, 8, length), axis=0)
            ds = exact.astype(BF16)
            scale = head_dim**-0.5
            du[0, rows, columns] = (jnp.dot(ds, k, preferred_element_type=F32) * scale).astype(BF16)
            sides[0] += t_times(ds, q) * scale
            sides[1] += t_times(prob.astype(BF16), do)

        du[1, :, columns] = sides[0].astype(BF16)
        du[2, :, columns] = sides[1].astype(BF16)
        spent(6.0)
    arrived("x1")
    block_norm(1, 1)
    for p in range(3):
        emit(act, du.at[p])
        times_matrix(du.at[p], into_total(p))
    block_norm_back(1, 1, 0.5)
    arrived("h0")

    def after_one():
        @blocks(length, BLOCK)
        def _(rows):
            value = frame_block(r.h0_here, rows).astype(F32)
            act[rows, :] = normalise(value, norm, 0).astype(BF16)
            grad = dx[rows, :] + norm_back(value, total[rows, :], norm, 0, sums)
            spot = pl.ds(pl.multiple_of(lax.rem(rows.start, 64), BLOCK), BLOCK)
            r.cot_here[rows.start // 64, spot, :] = grad.astype(BF16)

        for i in range(17):
            r.wide[i : i + 1, :] = jnp.sum(sums[i], axis=0, keepdims=True)
        for h in range(heads):
            whole = jnp.sum(jnp.sum(sums[17 + h], axis=0, keepdims=True), axis=1, keepdims=True)
            r.wide[17 + h : 18 + h, :] = jnp.broadcast_to(whole, (1, width))
        r.wide[17 + heads : 32, :] = jnp.zeros((15 - heads, width), F32)
        r.small[...] = r.wide[...].astype(BF16)
        for j in range(8):
            swap_start(1, j)
            swap_start(2, j)

    feed_forward_back("u1", 0, 0, after_one)
    while ticks[0] < last + 6:
        tick()
    for i in range(3):
        swap_wait(i)

    @pl.when(other)
    def _():
        for u in range(last):
            far_copy(u, 0).wait_recv()
            far_copy(u, 1).wait_recv()


def backward(made, fulls, norm, taps, slope, collective_id):
    width = norm.shape[-1]
    length = made.x4_out.shape[0]
    blocked = (8, length // 8, width)
    shapes = [(f.shape[0] // 8, f.shape[1]) for f in fulls]
    count = len(fulls)
    units = [
        (index, row, column)
        for index in BACK_ORDER
        for row in range(0, shapes[index][0], ROWS)
        for column in range(0, shapes[index][1], COLUMNS)
    ]
    number = len(units)
    dma = pltpu.SemaphoreType.DMA
    given = dict(
        cot=made.cot_out,
        h0=made.h0_out,
        u1=made.u1_out,
        x1=made.x1_out,
        qkv=made.qkv_out,
        attended=made.attended_out,
        x2=made.x2_out,
        gates=made.gates_out,
        gated=made.gated_out,
        depth=made.depth_out,
        x3=made.x3_out,
        u2=made.u2_out,
        x4=made.x4_out,
        result=made.result_out.reshape(blocked),
        lens=made.lens_out,
    )
    outs = dict(
        result_home=jax.ShapeDtypeStruct(blocked, BF16),
        dframes_home=jax.ShapeDtypeStruct(blocked, BF16),
        small_home=jax.ShapeDtypeStruct((8, 32, width), BF16),
    )
    scratch = dict(
        xs=pltpu.VMEM((2, length, width), F32),
        dx=pltpu.VMEM((length, width), F32),
        total=pltpu.VMEM((length, width), F32),
        low=pltpu.VMEM((length, width), BF16),
        act=pltpu.VMEM((length, width), BF16),
        up=pltpu.VMEM((4, length, width), BF16),
        du=pltpu.VMEM((4, length, width), BF16),
        hidden=pltpu.VMEM((4, length, width), BF16),
        cot_here=pltpu.VMEM(blocked, BF16),
        h0_here=pltpu.VMEM(blocked, BF16),
        depth_here=pltpu.VMEM((length, width), F32),
        gates_here=pltpu.VMEM((2, length, width), BF16),
        gated_here=pltpu.VMEM((length + 16, width), F32),
        spread=pltpu.VMEM((length + 16, width), F32),
        qkv_here=pltpu.VMEM((3, length, width), BF16),
        attended_here=pltpu.VMEM((length, width), BF16),
        sides=pltpu.VMEM((2, length, width // slope.shape[0]), F32),
        lens_here=pltpu.VMEM(made.lens_out.shape, F32),
        sums=pltpu.VMEM((17 + slope.shape[0], 8, width), F32),
        wide=pltpu.VMEM((32, width), F32),
        small=pltpu.VMEM((32, width), BF16),
        unit=pltpu.VMEM((2, 4, 256, 1024), BF16),
        stage=pltpu.VMEM((2, 4, 2, ROWS, COLUMNS), BF16),
        mine=pltpu.VMEM((SLOTS, 4, 2, HALF, COLUMNS), BF16),
        core_in=pltpu.VMEM((2, 4, 2, HALF, COLUMNS), BF16),
        first_in=pltpu.VMEM((SLOTS, 4, HALF, COLUMNS), BF16),
        second_in=pltpu.VMEM((SLOTS, 2, HALF, COLUMNS), BF16),
        s_unit=dma((2, 4)),
        s_stage=dma((2,)),
        s_fetch=dma((32,)),
        swap_send=dma((3, 8)),
        swap_recv=dma((3, 8)),
        swap_own=dma((3,)),
        s_load=dma((2,)),
        s_core=dma((2,)),
        r_core=dma((2,)),
        s_first=dma((SLOTS, 2)),
        r_first=dma((SLOTS, 2)),
        s_second=dma((SLOTS, 2)),
        r_second=dma((SLOTS, 2)),
        s_far=dma((2,)),
        r_far=dma((number, 2)),
        s_near=dma((2,)),
        r_near=dma((number,)),
        s_own=dma((2,)),
    )
    vmem = pl.BlockSpec(memory_space=pltpu.VMEM)
    operands = dict(given, norm=norm, taps=taps, slope=slope)

    def body(*refs):
        refs = list(refs)
        cut = lambda n: [refs.pop(0) for _ in range(n)]
        plain, full_refs, made_refs = cut(len(operands)), cut(count), cut(len(outs))
        out_refs, grad_refs = cut(count), cut(count)
        backward_kernel(
            units,
            list(operands) + list(outs) + list(scratch) + ["fulls", "outs", "grads"],
            *plain,
            *made_refs,
            *refs,
            full_refs,
            out_refs,
            grad_refs,
        )

    results = pl.pallas_call(
        body,
        out_shape=list(outs.values())
        + [jax.ShapeDtypeStruct(s, BF16) for s in shapes]
        + [jax.ShapeDtypeStruct((4, 2) + s, BF16) for s in shapes],
        in_specs=[ANY] * len(given) + [vmem] * 3 + [ANY] * count,
        out_specs=[ANY] * (len(outs) + 2 * count),
        scratch_shapes=list(scratch.values()),
        compiler_params=pltpu.CompilerParams(
            collective_id=collective_id, has_side_effects=True, vmem_limit_bytes=62 * 2**20
        ),
    )(*operands.values(), *fulls)
    return results[: len(outs)], results[len(outs) : len(outs) + count]


def per_device(
    frames_in,
    noise,
    lengths,
    span_starts,
    w_in1,
    w_out1,
    w_qkv,
    w_attn,
    w_point1,
    w_point2,
    w_in2,
    w_out2,
    norm_params,
    kernel,
    slopes,
    cotangent,
):
    utterances, frames, width = frames_in.shape
    heads = slopes.shape[0]
    length = frames * 8
    frame_pos = lax.axis_index("seq") * frames + jnp.arange(frames, dtype=jnp.int32)
    span_begin = span_starts[:, :, None]
    masked = jnp.any(
        (span_begin <= frame_pos[None, None, :]) & (frame_pos[None, None, :] < span_begin + SPAN),
        axis=1,
    )
    start = jnp.where(masked[..., None], noise, frames_in)
    lens = jnp.broadcast_to(lengths.astype(F32)[:, None, None], (utterances, 8, 128))
    slope_rows = jnp.broadcast_to(slopes[:, None], (heads, length))
    shards = (w_in1, w_out1, w_qkv, w_attn, w_point1, w_point2, w_in2, w_out2)
    made, fulls = forward(start, lens, cotangent, norm_params, kernel, slope_rows, shards, 0)
    (block_out, dframes, small), grads = backward(made, fulls, norm_params, kernel, slope_rows, 1)
    small = jnp.sum(small.astype(F32), axis=0)
    grad_frames = jnp.where(masked[..., None], 0.0, dframes.astype(F32))
    return (
        block_out,
        grad_frames,
        *[grad.astype(F32) for grad in grads],
        small[:12].reshape(6, 2, width),
        small[12:17],
        small[17 : 17 + heads, 0],
    )


def solution(mesh):
    in_specs = (
        P("dp", "seq", None),
        P("dp", "seq", None),
        P("dp"),
        P("dp", None),
        P("seq", None),
        P("seq", None),
        P("seq", None),
        P("seq", None),
        P("seq", None),
        P("seq", None),
        P("seq", None),
        P("seq", None),
        P(),
        P(),
        P(),
        P("dp", "seq", None),
    )
    out_specs = (
        P("dp", "seq", None),
        P("dp", "seq", None),
        P(("dp", "seq"), None),
        P(("dp", "seq"), None),
        P(("dp", "seq"), None),
        P(("dp", "seq"), None),
        P(("dp", "seq"), None),
        P(("dp", "seq"), None),
        P(("dp", "seq"), None),
        P(("dp", "seq"), None),
        P("dp", None, None),
        P("dp", None),
        P("dp"),
    )
    grouped = mesh.shape["seq"] == 8 and mesh.shape["dp"] == 4
    return jax.shard_map(
        per_device if grouped else per_device_any, mesh=mesh, in_specs=in_specs, out_specs=out_specs, check_vma=False
    )
```

```python
import functools
import types

import jax
import jax.numpy as jnp
from jax import lax
from jax.experimental import pallas as pl
from jax.experimental.pallas import tpu as pltpu
from jax.sharding import PartitionSpec as P

MESH = pl.DeviceIdType.MESH
BF16 = jnp.bfloat16
F32 = jnp.float32
ANY = pl.BlockSpec(memory_space=pl.ANY)

SPAN = 10


EPSILON = 1e-05
NEGATIVE = -1e30


def padded_2(shard, sides, width):
    for axis, dim in sides:
        peers, length = (lax.axis_size(axis), shard.shape[dim])
        up = [(i, (i + 1) % peers) for i in range(peers - 1)]
        down = [(j, i) for i, j in up]
        last = lax.slice_in_dim(shard, length - width, length, axis=dim)
        initial = lax.slice_in_dim(shard, 0, width, axis=dim)
        before = lax.ppermute(last, axis, up)
        after = lax.ppermute(initial, axis, down)
        shard = jnp.concatenate([before, shard, after], axis=dim)
    return shard


def layer_norm(inputs, gain_vec, shift_vec):
    average = jnp.mean(inputs, axis=-1, keepdims=True)
    centred = inputs - average
    variance = jnp.mean(centred * centred, axis=-1, keepdims=True)
    return centred * lax.rsqrt(variance + EPSILON) * gain_vec + shift_vec


def swish_norm(inputs, gain_vec, shift_vec):
    return jax.nn.silu(layer_norm(inputs, gain_vec, shift_vec))


def glu_gate(joined, live_rows):
    half_width = joined.shape[-1] // 2
    return joined[..., :half_width] * jax.nn.sigmoid(joined[..., half_width:]) * live_rows


def matmul(left_side, right_side):
    return jnp.dot(left_side, right_side, preferred_element_type=jnp.float32)


def matmul_right_t(left_side, right_side):
    return lax.dot_general(
        left_side, right_side, (((1,), (1,)), ((), ())), preferred_element_type=jnp.float32
    )


def matmul_left_t(left_side, right_side):
    return lax.dot_general(
        left_side, right_side, (((0,), (0,)), ((), ())), preferred_element_type=jnp.float32
    )


def block_scores(queries, keys, query_pos, key_pos, key_live, slopes, seq_length):
    factor = queries.shape[-1] ** (-0.5)
    scores = (
        jnp.einsum("uqhd,ukhd->uhqk", queries, keys, preferred_element_type=jnp.float32) * factor
    )
    distance = jnp.abs(query_pos[:, None] - key_pos[None, :]).astype(jnp.float32) / seq_length
    scores = scores - slopes[None, :, None, None] * distance[None, None]
    return (jnp.where(key_live[:, None, None, :], scores, NEGATIVE), distance)


def per_device_any(
    frames_in,
    noise,
    lengths,
    span_starts,
    w_in1,
    w_out1,
    w_qkv,
    w_attn,
    w_point1,
    w_point2,
    w_in2,
    w_out2,
    norm_params,
    kernel,
    slopes,
    cotangent,
):
    utterances, frames, model_width = frames_in.shape
    head_count = slopes.shape[0]
    head_dim = model_width // head_count
    row_count = utterances * frames
    tap_count = kernel.shape[0]
    half_taps = tap_count // 2
    factor = head_dim ** (-0.5)
    seq_length = frames * lax.axis_size("seq")
    first_frame = lax.axis_index("seq") * frames
    frame_pos = first_frame + jnp.arange(frames, dtype=jnp.int32)
    live_mask = frame_pos[None, :] < lengths[:, None]
    live_rows = live_mask.astype(jnp.float32).reshape(row_count, 1)
    span_begin = span_starts[:, :, None]
    masked = jnp.any(
        (span_begin <= frame_pos[None, None, :]) & (frame_pos[None, None, :] < span_begin + SPAN),
        axis=1,
    )
    start_in = (
        jnp.where(masked[..., None], noise, frames_in)
        .astype(jnp.float32)
        .reshape(row_count, model_width)
    )
    norm_gain = norm_params[:, 0]
    norm_shift = norm_params[:, 1]
    shards = (w_in1, w_out1, w_qkv, w_attn, w_point1, w_point2, w_in2, w_out2)
    gathered = (
        lax.all_gather(shards[0], "seq", axis=0, tiled=True),
        lax.all_gather(shards[1], "seq", axis=0, tiled=True),
        lax.all_gather(shards[2], "seq", axis=0, tiled=True),
        lax.all_gather(shards[3], "seq", axis=0, tiled=True),
        lax.all_gather(shards[4], "seq", axis=0, tiled=True),
        lax.all_gather(shards[5], "seq", axis=0, tiled=True),
        lax.all_gather(shards[6], "seq", axis=0, tiled=True),
        lax.all_gather(shards[7], "seq", axis=0, tiled=True),
    )
    full_in1, full_out1, full_qkv, full_attn, full_point1, full_point2, full_in2, full_out2 = (
        gathered
    )
    act_one = layer_norm(start_in, norm_gain[0], norm_shift[0]).astype(jnp.bfloat16)
    up_one = matmul(act_one, full_in1)
    hid_one = jax.nn.silu(up_one).astype(jnp.bfloat16)
    ffn_one = matmul(hid_one, full_out1)
    resid_one = start_in + 0.5 * ffn_one
    act_two = layer_norm(resid_one, norm_gain[1], norm_shift[1]).astype(jnp.bfloat16)
    packed = (
        matmul(act_two, full_qkv)
        .astype(jnp.bfloat16)
        .reshape(utterances, frames, 3, head_count, head_dim)
    )
    queries = packed[:, :, 0]
    keys = packed[:, :, 1]
    values = packed[:, :, 2]
    row_max = jnp.full((utterances, head_count, frames), NEGATIVE, jnp.float32)
    key_blk = lax.all_gather(keys, "seq", axis=1, tiled=True)
    value_blk = lax.all_gather(values, "seq", axis=1, tiled=True)
    amount = key_blk.shape[1]
    key_pos = jnp.arange(amount, dtype=jnp.int32)
    key_live = key_pos[None, :] < lengths[:, None]
    scores, distance = block_scores(
        queries, key_blk, frame_pos, key_pos, key_live, slopes, seq_length
    )
    new_max = jnp.maximum(row_max, jnp.max(scores, axis=-1))
    expd = jnp.exp(scores - new_max[..., None])
    row_sum = jnp.sum(expd, axis=-1)
    update = jnp.einsum(
        "uhqk,ukhd->uqhd", expd.astype(jnp.bfloat16), value_blk, preferred_element_type=jnp.float32
    )
    partial_value = update
    row_max, row_sum, partial_value = (new_max, row_sum, partial_value)
    attn_out = partial_value / jnp.transpose(row_sum, (0, 2, 1))[..., None]
    log_total = jnp.transpose(row_max + jnp.log(row_sum), (0, 2, 1))
    attn_low = attn_out.astype(jnp.bfloat16).reshape(row_count, model_width)
    attended = matmul(attn_low, full_attn)
    resid_two = resid_one + attended
    act_three = layer_norm(resid_two, norm_gain[2], norm_shift[2]).astype(jnp.bfloat16)
    joined = matmul(act_three, full_point1)
    gated = (
        glu_gate(joined, live_rows).astype(jnp.bfloat16).reshape(utterances, frames, model_width)
    )
    padded = padded_2(gated, (("seq", 1),), half_taps)
    depth = kernel[0] * padded[:, 0:frames].astype(jnp.float32)
    for position in range(1, tap_count):
        depth = depth + kernel[position] * padded[:, position : position + frames].astype(
            jnp.float32
        )
    depth = depth.reshape(row_count, model_width)
    act_four = swish_norm(depth, norm_gain[3], norm_shift[3]).astype(jnp.bfloat16)
    convolved = matmul(act_four, full_point2)
    resid_three = resid_two + convolved
    act_five = layer_norm(resid_three, norm_gain[4], norm_shift[4]).astype(jnp.bfloat16)
    up_two = matmul(act_five, full_in2)
    hid_two = jax.nn.silu(up_two).astype(jnp.bfloat16)
    ffn_two = matmul(hid_two, full_out2)
    resid_four = resid_three + 0.5 * ffn_two
    result = layer_norm(resid_four, norm_gain[5], norm_shift[5])
    gathered = (
        lax.all_gather(shards[0], "seq", axis=0, tiled=True),
        lax.all_gather(shards[1], "seq", axis=0, tiled=True),
        lax.all_gather(shards[2], "seq", axis=0, tiled=True),
        lax.all_gather(shards[3], "seq", axis=0, tiled=True),
        lax.all_gather(shards[4], "seq", axis=0, tiled=True),
        lax.all_gather(shards[5], "seq", axis=0, tiled=True),
        lax.all_gather(shards[6], "seq", axis=0, tiled=True),
        lax.all_gather(shards[7], "seq", axis=0, tiled=True),
    )
    full_in1, full_out1, full_qkv, full_attn, full_point1, full_point2, full_in2, full_out2 = (
        gathered
    )
    grad_result = cotangent.astype(jnp.float32).reshape(row_count, model_width)
    _, back_five = jax.vjp(layer_norm, resid_four, norm_gain[5], norm_shift[5])
    grad_four, gain_five, shift_five = back_five(grad_result)
    grad_ffn2 = (0.5 * grad_four).astype(jnp.bfloat16)
    _, back_silu2 = jax.vjp(jax.nn.silu, up_two)
    grad_up2 = back_silu2(matmul_right_t(grad_ffn2, full_out2))[0].astype(jnp.bfloat16)
    _, back_four = jax.vjp(layer_norm, resid_three, norm_gain[4], norm_shift[4])
    grad_norm4, gain_four, shift_four = back_four(matmul_right_t(grad_up2, full_in2))
    grad_three = grad_four + grad_norm4
    grad_conv = grad_three.astype(jnp.bfloat16)
    _, back_swish = jax.vjp(swish_norm, depth, norm_gain[3], norm_shift[3])
    grad_depth_f, gain_three, shift_three = back_swish(matmul_right_t(grad_conv, full_point2))
    grad_depth = grad_depth_f.astype(jnp.bfloat16).reshape(utterances, frames, model_width)
    grad_padded = padded_2(grad_depth, (("seq", 1),), half_taps)
    grad_depth_wide = grad_depth.astype(jnp.float32)
    grad_gated = jnp.zeros((utterances, frames, model_width), jnp.float32)
    kernel_rows = []
    for position in range(tap_count):
        lower = 2 * half_taps - position
        grad_gated = grad_gated + kernel[position] * grad_padded[:, lower : lower + frames].astype(
            jnp.float32
        )
        kernel_rows.append(
            jnp.sum(
                grad_depth_wide * padded[:, position : position + frames].astype(jnp.float32),
                axis=(0, 1),
            )
        )
    grad_kernel = jnp.stack(kernel_rows)
    _, back_gate = jax.vjp(lambda joined_in: glu_gate(joined_in, live_rows), joined)
    grad_joined = back_gate(grad_gated.reshape(row_count, model_width))[0].astype(jnp.bfloat16)
    _, back_three = jax.vjp(layer_norm, resid_two, norm_gain[2], norm_shift[2])
    grad_norm3, gain_two, shift_two = back_three(matmul_right_t(grad_joined, full_point1))
    grad_two = grad_three + grad_norm3
    grad_att = grad_two.astype(jnp.bfloat16)
    grad_heads = (
        matmul_right_t(grad_att, full_attn)
        .astype(jnp.bfloat16)
        .reshape(utterances, frames, head_count, head_dim)
    )
    spread = jnp.sum(grad_heads.astype(jnp.float32) * attn_out, axis=-1)
    log_total_t = jnp.transpose(log_total, (0, 2, 1))
    spread_t = jnp.transpose(spread, (0, 2, 1))
    grad_slope = jnp.zeros((head_count,), jnp.float32)
    key_blk = lax.all_gather(keys, "seq", axis=1, tiled=True)
    value_blk = lax.all_gather(values, "seq", axis=1, tiled=True)
    amount = key_blk.shape[1]
    key_pos = jnp.arange(amount, dtype=jnp.int32)
    key_live = key_pos[None, :] < lengths[:, None]
    scores, distance = block_scores(
        queries, key_blk, frame_pos, key_pos, key_live, slopes, seq_length
    )
    attn_prob = jnp.exp(scores - log_total_t[..., None])
    grad_prob = jnp.einsum(
        "uqhd,ukhd->uhqk", grad_heads, value_blk, preferred_element_type=jnp.float32
    )
    grad_exact = attn_prob * (grad_prob - spread_t[..., None])
    grad_scores = grad_exact.astype(jnp.bfloat16)
    grad_query = (
        jnp.einsum("uhqk,ukhd->uqhd", grad_scores, key_blk, preferred_element_type=jnp.float32)
        * factor
    )
    grad_slope = grad_slope - jnp.sum(grad_exact * distance[None, None], axis=(0, 2, 3))
    grad_query, grad_slope = (grad_query, grad_slope)
    query_blk = lax.all_gather(queries, "seq", axis=1, tiled=True)
    dhead_blk = lax.all_gather(grad_heads, "seq", axis=1, tiled=True)
    total_blk = lax.all_gather(log_total.astype(jnp.bfloat16), "seq", axis=1, tiled=True).astype(
        jnp.float32
    )
    spread_blk = lax.all_gather(spread.astype(jnp.bfloat16), "seq", axis=1, tiled=True).astype(
        jnp.float32
    )
    amount = query_blk.shape[1]
    query_pos = jnp.arange(amount, dtype=jnp.int32)
    scores, distance = block_scores(
        query_blk, keys, query_pos, frame_pos, live_mask, slopes, seq_length
    )
    attn_prob = jnp.exp(scores - jnp.transpose(total_blk, (0, 2, 1))[..., None])
    grad_value = jnp.einsum(
        "uhqk,uqhd->ukhd",
        attn_prob.astype(jnp.bfloat16),
        dhead_blk,
        preferred_element_type=jnp.float32,
    )
    grad_prob = jnp.einsum("uqhd,ukhd->uhqk", dhead_blk, values, preferred_element_type=jnp.float32)
    grad_scores = (
        attn_prob * (grad_prob - jnp.transpose(spread_blk, (0, 2, 1))[..., None])
    ).astype(jnp.bfloat16)
    grad_key = (
        jnp.einsum("uhqk,uqhd->ukhd", grad_scores, query_blk, preferred_element_type=jnp.float32)
        * factor
    )
    grad_key, grad_value = (grad_key, grad_value)
    grad_packed = (
        jnp.stack([grad_query, grad_key, grad_value], axis=2)
        .astype(jnp.bfloat16)
        .reshape(row_count, 3 * model_width)
    )
    _, back_two = jax.vjp(layer_norm, resid_one, norm_gain[1], norm_shift[1])
    grad_norm2, gain_one, shift_one = back_two(matmul_right_t(grad_packed, full_qkv))
    grad_one = grad_two + grad_norm2
    grad_ffn1 = (0.5 * grad_one).astype(jnp.bfloat16)
    _, back_silu1 = jax.vjp(jax.nn.silu, up_one)
    grad_up1 = back_silu1(matmul_right_t(grad_ffn1, full_out1))[0].astype(jnp.bfloat16)
    _, back_one = jax.vjp(layer_norm, start_in, norm_gain[0], norm_shift[0])
    grad_norm1, gain_zero, shift_zero = back_one(matmul_right_t(grad_up1, full_in1))
    grad_start = grad_one + grad_norm1
    grad_frames = jnp.where(
        masked[..., None], 0.0, grad_start.reshape(utterances, frames, model_width)
    )
    wide_pairs = (
        (act_one, grad_up1),
        (act_two, grad_packed),
        (attn_low, grad_att),
        (act_three, grad_joined),
        (act_four, grad_conv),
        (act_five, grad_up2),
    )
    wide = lax.psum_scatter(
        jnp.concatenate(
            [matmul_left_t(left_side, right_side) for left_side, right_side in wide_pairs], axis=1
        ).astype(jnp.bfloat16),
        "seq",
        scatter_dimension=0,
        tiled=True,
    ).astype(jnp.float32)
    tall_pairs = ((hid_one, grad_ffn1), (hid_two, grad_ffn2))
    tall = lax.psum_scatter(
        jnp.concatenate(
            [matmul_left_t(left_side, right_side) for left_side, right_side in tall_pairs], axis=1
        ).astype(jnp.bfloat16),
        "seq",
        scatter_dimension=0,
        tiled=True,
    ).astype(jnp.float32)
    hidden_width = w_in1.shape[1]
    column_cuts = [
        hidden_width,
        3 * model_width,
        model_width,
        2 * model_width,
        model_width,
        hidden_width,
    ]
    wide_parts = []
    column_start = 0
    for column_width in column_cuts:
        wide_parts.append(wide[:, column_start : column_start + column_width])
        column_start = column_start + column_width
    grad_in1, grad_qkv, grad_attn, grad_point1, grad_point2, grad_in2 = wide_parts
    grad_out1 = tall[:, :model_width]
    grad_out2 = tall[:, model_width:]
    grad_norms = jnp.stack(
        [
            jnp.stack([gain_zero, shift_zero]),
            jnp.stack([gain_one, shift_one]),
            jnp.stack([gain_two, shift_two]),
            jnp.stack([gain_three, shift_three]),
            jnp.stack([gain_four, shift_four]),
            jnp.stack([gain_five, shift_five]),
        ]
    )
    grad_norms, grad_kernel, grad_slope = (
        lax.psum(grad_norms.astype(jnp.bfloat16), "seq").astype(jnp.float32),
        lax.psum(grad_kernel.astype(jnp.bfloat16), "seq").astype(jnp.float32),
        lax.psum(grad_slope.astype(jnp.bfloat16), "seq").astype(jnp.float32),
    )
    block_out = result.astype(jnp.bfloat16).reshape(utterances, frames, model_width)
    return (
        block_out,
        grad_frames,
        grad_in1,
        grad_out1,
        grad_qkv,
        grad_attn,
        grad_point1,
        grad_point2,
        grad_in2,
        grad_out2,
        grad_norms,
        grad_kernel,
        grad_slope,
    )


def place():
    seq, dp = lax.axis_index("seq"), lax.axis_index("dp")
    return seq // 2, lax.rem(seq, 2), dp // 2, lax.rem(dp, 2)


def device(z, x, y, core):
    return (z * 2 + x, y * 2 + core)


def z_partners(z):
    return (z + 1 - 2 * lax.rem(z, 2), lax.rem(z + 2, 4), 3 - z)


def remote(source, target, send, recv, where):
    return pltpu.make_async_remote_copy(
        src_ref=source,
        dst_ref=target,
        send_sem=send,
        recv_sem=recv,
        device_id=where,
        device_id_type=MESH,
    )


def greet(partners, waits):
    barrier = pltpu.get_barrier_semaphore()
    for partner in partners:
        pl.semaphore_signal(barrier, inc=1, device_id=partner, device_id_type=MESH)
    pl.semaphore_wait(barrier, waits)


def utterance_of(z, x, core):
    return lax.rem(z, 2) * 4 + x * 2 + core


def home_of(utterance, y, group):
    return device(2 * group + utterance // 4, lax.rem(utterance // 2, 2), y, lax.rem(utterance, 2))


def bits_of(s):
    return s // 4, lax.rem(s // 2, 2), lax.rem(s, 2)


def flipped(bits, r):
    flips = (r // 4, r // 2 % 2, r % 2)
    return [1 - b if f else b for b, f in zip(bits, flips)]


def utterance_in_round(seq, r):
    b2, b1, b0 = bits_of(seq)
    out = flipped((b1, b0, b2), r)
    return out[0] * 4 + out[1] * 2 + out[2]


def seq_in_round(utterance, r):
    t2, t1, t0 = flipped(bits_of(utterance), r)
    return t0 * 4 + t2 * 2 + t1


def units_of(shapes):
    units = []
    for index, (rows, columns) in enumerate(shapes):
        for row in range(0, rows, 128):
            for column in range(0, columns, 1024):
                units.append((index, row, column))
    return units


ROWS = 128
HALF = 64
COLUMNS = 1024
LAGS = (0, 1, 2, 3, 5, 7, 8)
SPLIT = 384


def blocks(rows, size):
    def run(body):
        @pl.loop(0, rows // size, unroll=2)
        def _(i):
            body(pl.ds(pl.multiple_of(i * size, size), size))

    return run


def normalise(v, norm, i):
    average = jnp.mean(v, axis=-1, keepdims=True)
    centred = v - average
    variance = jnp.mean(centred * centred, axis=-1, keepdims=True)
    return centred * lax.rsqrt(variance + EPSILON) * norm[i, 0:1, :] + norm[i, 1:2, :]


TILE = 256


def sigmoid(v):
    return 0.5 * jnp.tanh(0.5 * v) + 0.5


def silu(v):
    return v * sigmoid(v)


def times_unit(left, weight, emit, poll):
    unit, loads = weight
    for n in range(COLUMNS // TILE):
        columns = pl.ds(n * TILE, TILE)
        loads[n].wait()
        emit(columns, jnp.dot(left[...], unit[:, :, :, columns].reshape(COLUMNS, TILE), preferred_element_type=F32))
        poll()


def score_block(q, k, slope_row, first, live_keys):
    shape = (q.shape[0], k.shape[0])
    scores = lax.dot_general(q, k, (((1,), (1,)), ((), ())), preferred_element_type=F32)
    rows = lax.broadcasted_iota(jnp.int32, shape, 0) + first
    keys = lax.broadcasted_iota(jnp.int32, shape, 1)
    distance = jnp.abs(rows - keys).astype(F32) * (1.0 / k.shape[0])
    scores = scores * (q.shape[1] ** -0.5) - slope_row * distance
    return jnp.where(keys.astype(F32) < live_keys, scores, NEGATIVE), distance


def softmax_block(scores):
    top = jnp.max(scores, axis=-1, keepdims=True)
    expd = jnp.exp(scores - top)
    return expd / jnp.sum(expd, axis=-1, keepdims=True)


QUERIES = 128
BLOCK = 32


def forward_kernel(units, names, *refs):
    r = types.SimpleNamespace(**dict(zip(names, refs)))
    norm, taps, slope = r.norm, r.taps, r.slope
    length, width = r.x.shape[1:]
    heads = slope.shape[0]
    head_dim = width // heads
    z, x, y, core = place()
    seq, group = z * 2 + x, z // 2
    utterance = utterance_of(z, x, core)
    same = group == core
    zs = z_partners(z)
    over_z = [device(other, x, y, core) for other in zs]
    over_x = device(z, 1 - x, y, core)
    over_y = device(z, x, 1 - y, core)
    over_core = device(z, x, y, 1 - core)
    mates = [utterance_in_round(seq, i) for i in range(8)]
    givers = [device(s // 2, lax.rem(s, 2), y, group) for s in [seq_in_round(utterance, i) for i in range(8)]]
    targets = [home_of(u, y, core) for u in mates]
    barrier = pltpu.get_barrier_semaphore()

    @pl.when(jnp.logical_not(same))
    def _():
        pl.semaphore_signal(barrier, inc=1, device_id=givers[0], device_id_type=MESH)

    for partner in givers[1:] + [over_z[0], over_z[2], over_x, over_y, over_core]:
        pl.semaphore_signal(barrier, inc=1, device_id=partner, device_id_type=MESH)
    pl.semaphore_wait(barrier, jnp.where(same, 12, 13))

    swaps = ((r.start, r.h0), (r.lens, r.lens_here), (r.cot, r.cot_out))

    def swap(i, j):
        source, target = swaps[i]
        return remote(source.at[mates[j]], target.at[seq], r.swap_send.at[i, j], r.swap_recv.at[i, j], targets[j])

    def swap_local(i):
        source, target = swaps[i]
        return pltpu.make_async_copy(source.at[mates[0]], target.at[seq], r.swap_own.at[i])

    def swap_start(i, j):
        if j > 0:
            swap(i, j).start()
            return

        @pl.when(jnp.logical_not(same))
        def _():
            swap(i, 0).start()

        @pl.when(same)
        def _():
            swap_local(i).start()

    def swap_wait(i):
        @pl.when(jnp.logical_not(same))
        def _():
            swap(i, 0).wait()

        @pl.when(same)
        def _():
            swap_local(i).wait()

        for j in range(1, 8):
            swap(i, j).wait()

    send, recv, own = r.send, r.recv, r.own
    shards, fulls = r.shards, r.fulls

    def spot(unit):
        index, row, column = unit
        rows = pl.ds(row + pl.multiple_of(core * HALF, HALF), HALF)
        mine = pl.ds(column + pl.multiple_of(y * SPLIT, 128), COLUMNS - SPLIT)
        third = pl.ds(column + pl.multiple_of(y * (COLUMNS - SPLIT), 128), SPLIT)
        return shards[index], fulls[index], rows, mine, third, pl.ds(column, COLUMNS)

    middle = (z == 1) | (z == 2)
    near_pair, far_pair = pl.ds(2 * (z // 2), 2), pl.ds(2 - 2 * (z // 2), 2)

    class Along:
        def __init__(self, copy, sends, gets):
            self.copy, self.sends, self.gets = copy, sends, gets

        def start(self):
            @pl.when(self.sends)
            def _():
                self.copy.start()

        def wait(self):
            @pl.when(self.sends)
            def _():
                self.copy.wait_send()

            @pl.when(self.gets)
            def _():
                self.copy.wait_recv()

    def first(u):
        shard, full, rows, mine, _, _ = spot(units[u])
        every = pl.ds(units[u][2], COLUMNS)
        return [
            remote(shard.at[rows, mine], full.at[z, x, rows, mine], send.at[u, 0], recv.at[u, 0], over_z[0]),
            pltpu.make_async_copy(shard.at[rows, every], full.at[z, x, rows, every], own.at[u]),
        ]

    def across(u):
        _, full, rows, mine, _, _ = spot(units[u])
        piece = full.at[near_pair, x, rows, mine]
        return [Along(remote(piece, piece, send.at[u, 1], recv.at[u, 1], over_z[2]), middle, middle)]

    def outward(u):
        _, full, rows, mine, _, _ = spot(units[u])
        piece = full.at[far_pair, x, rows, mine]
        copy = remote(piece, piece, send.at[u, 2], recv.at[u, 2], over_z[0])
        return [Along(copy, middle, jnp.logical_not(middle))]

    def second(u):
        _, full, rows, mine, _, _ = spot(units[u])
        piece = full.at[:, x, rows, mine]
        return [remote(piece, piece, send.at[u, 3], recv.at[u, 3], over_x)]

    def third(u):
        _, full, rows, _, part, _ = spot(units[u])
        pieces = [full.at[:, 1 - x, rows, part]] + [full.at[other, x, rows, part] for other in zs]
        out = [remote(p, p, send.at[u, 4 + j], recv.at[u, 4 + j], over_y) for j, p in enumerate(pieces)]
        return out

    def fourth(u):
        _, full, rows, _, _, whole = spot(units[u])
        piece = full.at[:, :, rows, whole]
        return [remote(piece, piece, send.at[u, 8], recv.at[u, 8], over_core)]

    stages = (first, across, outward, second, third, fourth)
    last = len(units)
    done = [0]

    actions = []
    ends = {}

    def move(u, depth):
        def act_on():
            if depth > 0:
                for copy in stages[depth - 1](u):
                    copy.wait()
            if depth < len(stages):
                for copy in stages[depth](u):
                    copy.start()

        return act_on

    for step in range(last + LAGS[-1]):
        for depth, lag in reversed(list(enumerate(LAGS))):
            if 0 <= step - lag < last:
                actions.append(move(step - lag, depth))
                if depth == len(stages):
                    ends[step - lag] = len(actions)
        if 12 <= step < 20:
            actions.append(functools.partial(swap_start, 2, step - 12))

    def poll(count=1):
        for _ in range(count):
            if done[0] < len(actions):
                actions[done[0]]()
                done[0] += 1

    taken = [0]

    def weight():
        u = taken[0]
        taken[0] += 1
        while done[0] < ends[u]:
            poll()
        index, row, column = units[u]
        loads = []
        for n in range(COLUMNS // TILE):
            source = fulls[index].at[:, :, pl.ds(row, ROWS), pl.ds(column + n * TILE, TILE)]
            target = r.unit.at[u % 2, :, :, :, pl.ds(n * TILE, TILE)]
            copy = pltpu.make_async_copy(source, target, r.load.at[u % 2, n])
            copy.start()
            loads.append(copy)
        return r.unit.at[u % 2], loads

    kept = []

    def keep(source, target):
        copy = pltpu.make_async_copy(source, target, r.kept.at[len(kept)])
        copy.start()
        kept.append(copy)

    xs, act, acc = r.x, r.act, r.acc
    poll()
    for j in range(8):
        swap_start(0, j)
    for j in range(8):
        swap_start(1, j)
    poll(4)
    swap_wait(0)

    @blocks(length, BLOCK)
    def _(rows):
        xs[0, rows, :] = r.h0[rows.start // 64, pl.ds(pl.multiple_of(lax.rem(rows.start, 64), BLOCK), BLOCK), :].astype(F32)
        act[rows, :] = normalise(xs[0, rows, :], norm, 0).astype(BF16)

    keep(r.h0, r.h0_out)

    hidden_kept = []

    def feed_forward(x_in, x_out, up, up_out, hidden_out):
        hidden = r.hidden
        for copy in hidden_kept:
            copy.wait()
        for p in range(4):
            unit, loads = weight()

            for n in range(COLUMNS // TILE):
                columns = pl.ds(n * TILE, TILE)
                loads[n].wait()
                value = jnp.dot(act[...], unit[:, :, :, columns].reshape(COLUMNS, TILE), preferred_element_type=F32)
                up[p, :, columns] = value.astype(BF16)
                value = silu(value).astype(BF16)
                for t in range(2 * n, 2 * n + 2):
                    place_at = pl.ds((2 * p + t // 4) * 128, 128)
                    hidden[t % 4, :, place_at] = value[:, (t - 2 * n) * 128 : (t - 2 * n + 1) * 128]
                poll()

            keep(up.at[p], up_out.at[:, pl.ds(p * COLUMNS, COLUMNS)])
        hidden_kept[:] = [pltpu.make_async_copy(hidden, hidden_out, r.kept.at[31])]
        hidden_kept[0].start()
        for q in range(4):
            def emit(columns, value, q=q):
                if q == 0:
                    acc[:, columns] = value
                else:
                    acc[:, columns] = acc[:, columns] + value

            times_unit(hidden.at[q], weight(), emit, poll)

        @blocks(length, BLOCK)
        def _(rows):
            xs[x_out, rows, :] = xs[x_in, rows, :] + 0.5 * acc[rows, :]

    feed_forward(0, 1, r.up, r.u1_out, r.s1_out)
    keep(xs.at[1], r.x1_out)

    @blocks(length, BLOCK)
    def _(rows):
        act[rows, :] = normalise(xs[1, rows, :], norm, 1).astype(BF16)

    qkv = r.qkv
    for i in range(3):

        def emit(columns, value, i=i):
            qkv[i, :, columns] = value.astype(BF16)

        times_unit(act, weight(), emit, poll)
    keep(qkv, r.qkv_out)
    swap_wait(1)
    live_count = r.lens_here[0, 0:1, 0:1]
    keep(r.lens_here, r.lens_out)
    attended = r.attended
    for h in range(heads):
        columns = pl.ds(h * head_dim, head_dim)

        @blocks(length, QUERIES)
        def _(rows, h=h, columns=columns):
            scores, _ = score_block(
                qkv[0, rows, columns], qkv[1, :, columns], slope[h : h + 1, :], rows.start, live_count
            )
            prob = softmax_block(scores).astype(BF16)
            attended[rows, columns] = jnp.dot(prob, qkv[2, :, columns], preferred_element_type=F32).astype(BF16)

        poll(2)
    keep(attended, r.attended_out)

    def add_to(x_in, x_out):
        def emit(columns, value):
            xs[x_out, :, columns] = xs[x_in, :, columns] + value

        return emit

    times_unit(attended, weight(), add_to(1, 2), poll)
    keep(xs.at[2], r.x2_out)

    @blocks(length, BLOCK)
    def _(rows):
        act[rows, :] = normalise(xs[2, rows, :], norm, 2).astype(BF16)

    gates, gated = r.gates, r.gated

    def emit(columns, value):
        acc[:, columns] = value
        gates[0, :, columns] = value.astype(BF16)

    times_unit(act, weight(), emit, poll)
    gated[0:8, :] = jnp.zeros((8, width), F32)
    gated[length + 8 : length + 16, :] = jnp.zeros((8, width), F32)

    def emit(columns, value):
        gates[1, :, columns] = value.astype(BF16)
        live = lax.broadcasted_iota(jnp.int32, value.shape, 0).astype(F32) < live_count
        passed = jnp.where(live, acc[:, columns] * sigmoid(value), 0.0)
        gated[pl.ds(8, length), columns] = passed.astype(BF16).astype(F32)

    times_unit(act, weight(), emit, poll)
    keep(gates, r.gates_out)
    keep(gated, r.gated_out)
    depth = r.depth

    @blocks(length, BLOCK)
    def _(rows):
        near = gated[pl.ds(pl.multiple_of(rows.start, BLOCK), BLOCK + 16), :]
        total = taps[0:1, :] * near[6 : 6 + BLOCK]
        for t in range(1, taps.shape[0]):
            total = total + taps[t : t + 1, :] * near[6 + t : 6 + t + BLOCK]
        depth[rows, :] = total
        value = normalise(total, norm, 3)
        act[rows, :] = (silu(value)).astype(BF16)

    keep(depth, r.depth_out)
    times_unit(act, weight(), add_to(2, 3), poll)
    keep(xs.at[3], r.x3_out)

    @blocks(length, BLOCK)
    def _(rows):
        act[rows, :] = normalise(xs[3, rows, :], norm, 4).astype(BF16)

    feed_forward(3, 4, r.up2, r.u2_out, r.s2_out)
    keep(xs.at[4], r.x4_out)

    @blocks(length, BLOCK)
    def _(rows):
        act[rows, :] = normalise(xs[4, rows, :], norm, 5).astype(BF16)

    keep(act, r.result_out)
    swap_wait(2)
    for copy in hidden_kept + kept:
        copy.wait()


def forward(start, lens, cot, norm, taps, slope, shards, collective_id):
    shapes = [s.shape for s in shards]
    units = units_of(shapes)
    width = norm.shape[-1]
    frames = start.shape[1]
    length = 8 * frames
    count = len(shards)
    dma = pltpu.SemaphoreType.DMA
    hidden = shapes[0][1]
    wide = lambda *lead: jax.ShapeDtypeStruct(lead + (length, width), F32)
    low = lambda *lead: jax.ShapeDtypeStruct(lead + (length, width), BF16)
    up = jax.ShapeDtypeStruct((length, hidden), BF16)
    outs = dict(
        cot_out=jax.ShapeDtypeStruct(cot.shape, cot.dtype),
        h0_out=jax.ShapeDtypeStruct(start.shape, start.dtype),
        u1_out=up,
        x1_out=wide(),
        qkv_out=low(3),
        attended_out=low(),
        x2_out=wide(),
        gates_out=low(2),
        gated_out=jax.ShapeDtypeStruct((length + 16, width), F32),
        depth_out=wide(),
        x3_out=wide(),
        u2_out=up,
        x4_out=wide(),
        result_out=low(),
        s1_out=low(4),
        s2_out=low(4),
        lens_out=jax.ShapeDtypeStruct(lens.shape, lens.dtype),
    )
    scratch = dict(
        h0=pltpu.VMEM(start.shape, BF16),
        lens_here=pltpu.VMEM(lens.shape, F32),
        x=pltpu.VMEM((5, length, width), F32),
        act=pltpu.VMEM((length, width), BF16),
        acc=pltpu.VMEM((length, width), F32),
        hidden=pltpu.VMEM((4, length, width), BF16),
        up=pltpu.VMEM((4, length, width), BF16),
        up2=pltpu.VMEM((4, length, width), BF16),
        qkv=pltpu.VMEM((3, length, width), BF16),
        attended=pltpu.VMEM((length, width), BF16),
        gates=pltpu.VMEM((2, length, width), BF16),
        gated=pltpu.VMEM((length + 16, width), F32),
        depth=pltpu.VMEM((length, width), F32),
        unit=pltpu.VMEM((2, 4, 2, ROWS, COLUMNS), BF16),
        load=dma((2, COLUMNS // TILE)),
        swap_send=dma((3, 8)),
        swap_recv=dma((3, 8)),
        swap_own=dma((3,)),
        send=dma((len(units), 9)),
        recv=dma((len(units), 9)),
        own=dma((len(units),)),
        kept=dma((32,)),
    )
    names = ["start", "lens", "cot", "norm", "taps", "slope"]
    vmem = pl.BlockSpec(memory_space=pltpu.VMEM)

    def body(*refs):
        plain, rest = refs[:6], refs[6:]
        ours, rest = rest[:count], rest[count:]
        made, rest = rest[: len(outs)], rest[len(outs) :]
        fulls, rest = rest[:count], rest[count:]
        forward_kernel(
            units,
            names + list(outs) + list(scratch) + ["shards", "fulls"],
            *plain,
            *made,
            *rest,
            ours,
            fulls,
        )

    results = pl.pallas_call(
        body,
        out_shape=list(outs.values()) + [jax.ShapeDtypeStruct((4, 2) + s, BF16) for s in shapes],
        in_specs=[ANY, ANY, ANY, vmem, vmem, vmem] + [ANY] * count,
        out_specs=[ANY] * (len(outs) + count),
        scratch_shapes=list(scratch.values()),
        compiler_params=pltpu.CompilerParams(
            collective_id=collective_id, has_side_effects=True, vmem_limit_bytes=60 * 2**20
        ),
    )(start, lens, cot, norm, taps, slope, *shards)
    made = types.SimpleNamespace(**dict(zip(outs, results[: len(outs)])))
    fulls = [f.reshape(8 * s[0], s[1]) for f, s in zip(results[len(outs) :], shapes)]
    return made, fulls


CADENCE = 12.0
SLOTS = 7


def norm_back(v, dy, norm, i, sums):
    average = jnp.mean(v, axis=-1, keepdims=True)
    centred = v - average
    scale = lax.rsqrt(jnp.mean(centred * centred, axis=-1, keepdims=True) + EPSILON)
    unit = centred * scale
    sums[2 * i] += jnp.sum((dy * unit).reshape(-1, 8, dy.shape[-1]), axis=0)
    sums[2 * i + 1] += jnp.sum(dy.reshape(-1, 8, dy.shape[-1]), axis=0)
    inner = dy * norm[i, 0:1, :]
    return scale * (
        inner
        - jnp.mean(inner, axis=-1, keepdims=True)
        - unit * jnp.mean(inner * unit, axis=-1, keepdims=True)
    )


def silu_back(v):
    s = sigmoid(v)
    return s * (1.0 + v * (1.0 - s))


def times_t(left, right):
    return lax.dot_general(left, right, (((1,), (1,)), ((), ())), preferred_element_type=F32)


def t_times(left, right):
    return lax.dot_general(left, right, (((0,), (0,)), ((), ())), preferred_element_type=F32)


BACK_ORDER = (7, 6, 5, 4, 3, 2, 1, 0)


def backward_kernel(units, names, *refs):
    r = types.SimpleNamespace(**dict(zip(names, refs)))
    norm, taps, slope, sums = r.norm, r.taps, r.slope, r.sums
    length, width = r.dx.shape
    heads = slope.shape[0]
    head_dim = width // heads
    z, x, y, core = place()
    seq, group = z * 2 + x, z // 2
    utterance = utterance_of(z, x, core)
    keeps = group == core
    other = jnp.logical_not(keeps)
    z_other = z + 1 - 2 * lax.rem(z, 2)
    over_core = device(z, x, y, 1 - core)
    over_x = device(z, 1 - x, y, core)
    over_z = device(z_other, x, y, core)
    far = device(3 - z, x, y, group)
    seqs = [seq_in_round(utterance, i) for i in range(8)]
    targets = [device(s // 2, lax.rem(s, 2), y, group) for s in seqs]
    givers = [home_of(utterance_in_round(seq, i), y, core) for i in range(8)]
    barrier = pltpu.get_barrier_semaphore()
    for partner in [over_core, over_x, over_z] + givers[1:]:
        pl.semaphore_signal(barrier, inc=1, device_id=partner, device_id_type=MESH)

    @pl.when(other)
    def _():
        for giver in [device(3 - z, x, y, 0), device(3 - z, x, y, 1), givers[0]]:
            pl.semaphore_signal(barrier, inc=1, device_id=giver, device_id_type=MESH)

    pl.semaphore_wait(barrier, jnp.where(keeps, 11, 12))

    swaps = ((r.result, r.result_home), (r.cot_here, r.dframes_home), (r.small, r.small_home))

    def swap(i, j):
        source, target = swaps[i][0], swaps[i][1].at[utterance]
        block = source if i == 2 else source.at[seqs[j]]
        return remote(block, target, r.swap_send.at[i, j], r.swap_recv.at[i, j], targets[j])

    def swap_local(i):
        source, target = swaps[i][0], swaps[i][1].at[utterance]
        return pltpu.make_async_copy(source if i == 2 else source.at[seqs[0]], target, r.swap_own.at[i])

    def swap_start(i, j):
        if j > 0:
            swap(i, j).start()
            return

        @pl.when(other)
        def _():
            swap(i, 0).start()

        @pl.when(keeps)
        def _():
            swap_local(i).start()

    def swap_wait(i):
        @pl.when(other)
        def _():
            swap(i, 0).wait()

        @pl.when(keeps)
        def _():
            swap_local(i).wait()

        for j in range(1, 8):
            swap(i, j).wait()

    grads, outs, mine, core_in, first_in, second_in = (
        r.grads, r.outs, r.mine, r.core_in, r.first_in, r.second_in
    )
    half = pl.multiple_of(core * HALF, HALF)
    other_half = pl.multiple_of((1 - core) * HALF, HALF)
    last = len(units)

    def columns_of(u):
        return pl.ds(units[u][2], COLUMNS)

    def core_copy(u):
        source = grads[units[u][0]].at[:, :, pl.ds(units[u][1] + other_half, HALF), columns_of(u)]
        return remote(source, core_in.at[u % 2], r.s_core.at[u % 2], r.r_core.at[u % 2], over_core)

    def load_copy(u):
        source = grads[units[u][0]].at[:, :, pl.ds(units[u][1] + half, HALF), columns_of(u)]
        return pltpu.make_async_copy(source, mine.at[u % SLOTS], r.s_load.at[u % 2])

    def swapped(u):
        return u % 8 == 2

    def first_copies(u):
        slot = u % SLOTS
        held, arriving, send, recv = mine.at[slot], first_in.at[slot], r.s_first.at[slot], r.r_first.at[slot]
        if swapped(u):
            return [
                remote(held.at[t], arriving.at[pl.ds(2 * i, 2)], send.at[i], recv.at[i], over_z)
                for i, t in enumerate((z_other, 3 - z_other))
            ]
        return [remote(held.at[:, 1 - x], arriving, send.at[0], recv.at[0], over_x)]

    def second_copies(u):
        slot = u % SLOTS
        held, arriving, send, recv = mine.at[slot], second_in.at[slot], r.s_second.at[slot], r.r_second.at[slot]
        if swapped(u):
            pairs, partner = ((z, 1 - x), (3 - z, 1 - x)), over_x
        else:
            pairs, partner = ((z_other, x), (3 - z_other, x)), over_z
        return [
            remote(held.at[t, t_x], arriving.at[i], send.at[i], recv.at[i], partner)
            for i, (t, t_x) in enumerate(pairs)
        ]

    def far_copy(u, giver=None):
        start = half if giver is None else giver * HALF
        target = outs[units[u][0]].at[pl.ds(units[u][1] + start, HALF), columns_of(u)]
        recv = r.r_far.at[u, core if giver is None else giver]
        return remote(mine.at[u % SLOTS, 3 - z, x], target, r.s_far.at[u % 2], recv, far)

    def near_target(u, start):
        return outs[units[u][0]].at[pl.ds(units[u][1] + start, HALF), columns_of(u)]

    def near_copy(u, start):
        return remote(
            mine.at[u % SLOTS, z, x], near_target(u, start), r.s_near.at[u % 2], r.r_near.at[u], over_core
        )

    def near_local(u):
        return pltpu.make_async_copy(mine.at[u % SLOTS, z, x], near_target(u, half), r.s_own.at[u % 2])

    def add(into, more):
        into[...] = (into[...].astype(F32) + more[...].astype(F32)).astype(BF16)

    def stage0(u):
        load_copy(u).start()
        core_copy(u).start()

    def stage1(u):
        load_copy(u).wait()
        core_copy(u).wait()
        held, arrived = mine.at[u % SLOTS], core_in.at[u % 2]
        if swapped(u):
            sent = [(t, t_x) for t in (z_other, 3 - z_other) for t_x in (0, 1)]
            rest = [(t, t_x) for t in (z, 3 - z) for t_x in (0, 1)]
        else:
            sent, rest = [(t, 1 - x) for t in range(4)], [(t, x) for t in range(4)]
        for t in sent:
            add(held.at[t], arrived.at[t])
        for copy in first_copies(u):
            copy.start()
        for t in rest:
            add(held.at[t], arrived.at[t])

    def stage2(u):
        for copy in first_copies(u):
            copy.wait()
        held, arrived = mine.at[u % SLOTS], first_in.at[u % SLOTS]
        if swapped(u):
            sent = [((t, 1 - x), 2 * i + 1 - x) for i, t in enumerate((z, 3 - z))]
            rest = [((t, x), 2 * i + x) for i, t in enumerate((z, 3 - z))]
        else:
            sent = [((t, x), t) for t in (z_other, 3 - z_other)]
            rest = [((t, x), t) for t in (z, 3 - z)]
        for (t, i), copy in zip(sent, second_copies(u)):
            add(held.at[t], arrived.at[i])
            copy.start()
        for t, i in rest:
            add(held.at[t], arrived.at[i])

    def stage3(u):
        for copy in second_copies(u):
            copy.wait()
        held, arrived = mine.at[u % SLOTS], second_in.at[u % SLOTS]
        add(held.at[3 - z, x], arrived.at[1])
        far_copy(u).start()
        add(held.at[z, x], arrived.at[0])

        @pl.when(keeps)
        def _():
            near_local(u).start()

        @pl.when(other)
        def _():
            near_copy(u, half).start()

    def stage4(u):
        far_copy(u).wait_send()

        @pl.when(keeps)
        def _():
            near_local(u).wait()
            near_copy(u, other_half).wait_recv()

        @pl.when(other)
        def _():
            near_copy(u, half).wait_send()

    order = ((stage1, 1), (stage0, 0), (stage2, 3), (stage3, 5), (stage4, 6))
    ticks, emitted, clock = [0], [0], [0.0]

    def tick():
        step = ticks[0]
        ticks[0] += 1
        settle(min(step + 1, last))
        for stage, depth in order:
            if 0 <= step - depth < last:
                stage(step - depth)

    def spent(us):
        if emitted[0] == 0:
            return
        clock[0] += us
        while clock[0] >= CADENCE:
            clock[0] -= CADENCE
            if ticks[0] < emitted[0]:
                tick()

    stored = [0]

    def stage_copy(u):
        target = grads[units[u][0]].at[:, :, pl.ds(units[u][1], ROWS), columns_of(u)]
        return pltpu.make_async_copy(r.stage.at[u % 2], target, r.s_stage.at[u % 2])

    def settle(count):
        while stored[0] < count:
            stage_copy(stored[0]).wait()
            stored[0] += 1

    def emit(left, right):
        u = emitted[0]
        stage = r.stage.at[u % 2]
        settle(u - 1)
        for t in range(4):
            value = t_times(left[:, pl.ds(t * 256, 256)], right[...])
            stage[t] = value.astype(BF16).reshape(2, ROWS, COLUMNS)
        stage_copy(u).start()
        emitted[0] += 1
        if u == 0:
            tick()
        spent(3.0)

    wanted = []
    for index in BACK_ORDER:
        rows, columns = r.fulls[index].shape
        for row in range(0, rows, 1024):
            for column in range(0, columns, 1024):
                wanted.append((index, row, column))

    def weight_copies(i):
        index, row, column = wanted[i]
        return [
            pltpu.make_async_copy(
                r.fulls[index].at[pl.ds(row + 256 * t, 256), pl.ds(column, 1024)],
                r.unit.at[i % 2, t],
                r.s_unit.at[i % 2, t],
            )
            for t in range(4)
        ]

    taken = [0]

    def weight():
        i = taken[0]
        taken[0] += 1
        if i + 1 < len(wanted):
            for copy in weight_copies(i + 1):
                copy.start()
        return r.unit.at[i % 2], weight_copies(i)

    def times_matrix(left, take):
        unit, copies = weight()
        for t in range(4):
            copies[t].wait()
            take(pl.ds(t * 256, 256), times_t(left[...], unit[t]))
        spent(2.5)

    def into_total(q):
        def take(columns, value):
            if q == 0:
                r.total[:, columns] = value
            else:
                r.total[:, columns] = r.total[:, columns] + value

        return take

    fetched = {}

    def fetch(name, source, target):
        fetched[name] = pltpu.make_async_copy(source, target, r.s_fetch.at[len(fetched)])
        fetched[name].start()

    def arrived(*wanted_names):
        for name in wanted_names:
            fetched[name].wait()

    xs, dx, total, low, act, up, du, hidden = (
        r.xs, r.dx, r.total, r.low, r.act, r.up, r.du, r.hidden
    )
    fetch("x4", r.x4, xs.at[0])
    fetch("cot", r.cot, r.cot_here)
    fetch("s2", r.s2, hidden)
    for p in range(4):
        fetch(("u2", p), r.u2.at[:, pl.ds(p * COLUMNS, COLUMNS)], up.at[p])
    for copy in weight_copies(0):
        copy.start()
    fetch("x3", r.x3, xs.at[1])
    fetch("depth", r.depth, r.depth_here)
    fetch("gates", r.gates, r.gates_here)
    fetch("gated", r.gated, r.gated_here)
    fetch("qkv", r.qkv, r.qkv_here)
    fetch("attended", r.attended, r.attended_here)
    fetch("lens", r.lens, r.lens_here)
    fetch("h0", r.h0, r.h0_here)
    for j in range(8):
        swap_start(0, j)
    sums[...] = jnp.zeros(sums.shape, F32)
    arrived("x4", "cot")

    def frame_block(ref, rows):
        return ref[rows.start // 64, pl.ds(pl.multiple_of(lax.rem(rows.start, 64), BLOCK), BLOCK), :]

    @blocks(length, BLOCK)
    def _(rows):
        grad = norm_back(xs[0, rows, :], frame_block(r.cot_here, rows).astype(F32), norm, 5, sums)
        dx[rows, :] = grad
        low[rows, :] = (0.5 * grad).astype(BF16)

    fetch("x2", r.x2, xs.at[0])

    def feed_forward_back(kind, stored_as, write):
        arrived(stored_as)
        for q in range(4):
            emit(hidden.at[q], low)
        arrived(*[(kind, p) for p in range(4)])
        for p in range(4):

            def take(columns, value, p=p):
                du[p, :, columns] = (value * silu_back(up[p, :, columns].astype(F32))).astype(BF16)

            times_matrix(low, take)
            spent(1.0)
        for p in range(4):
            times_matrix(du.at[p], into_total(p))
        write()
        for p in range(4):
            emit(act, du.at[p])

    def block_norm(x_slot, norm_index):
        @blocks(length, BLOCK)
        def _(rows):
            act[rows, :] = normalise(xs[x_slot, rows, :], norm, norm_index).astype(BF16)

        spent(3.0)

    def block_norm_back(x_slot, norm_index, factor):
        @blocks(length, BLOCK)
        def _(rows):
            grad = dx[rows, :] + norm_back(xs[x_slot, rows, :], total[rows, :], norm, norm_index, sums)
            dx[rows, :] = grad
            low[rows, :] = (factor * grad).astype(BF16)

        spent(5.0)

    def after_two():
        arrived("x3")
        block_norm(1, 4)

    feed_forward_back("u2", "s2", after_two)
    fetch("s1", r.s1, hidden)
    for p in range(4):
        fetch(("u1", p), r.u1.at[:, pl.ds(p * COLUMNS, COLUMNS)], up.at[p])
    block_norm_back(1, 4, 1.0)
    fetch("x1", r.x1, xs.at[1])

    depth, gates, gated, spread = r.depth_here, r.gates_here, r.gated_here, r.spread
    arrived("depth", "gated", "gates", "lens")
    live_count = r.lens_here[0, 0:1, 0:1]

    @blocks(length, BLOCK)
    def _(rows):
        act[rows, :] = silu(normalise(depth[rows, :], norm, 3)).astype(BF16)

    emit(act, low)
    times_matrix(low, into_total(0))
    spread[0:8, :] = jnp.zeros((8, width), F32)
    spread[length + 8 : length + 16, :] = jnp.zeros((8, width), F32)

    @blocks(length, BLOCK)
    def _(rows):
        inner = depth[rows, :]
        dy = total[rows, :] * silu_back(normalise(inner, norm, 3))
        grad = norm_back(inner, dy, norm, 3, sums).astype(BF16).astype(F32)
        spread[pl.ds(pl.multiple_of(rows.start, BLOCK) + 8, BLOCK), :] = grad

    spent(6.0)

    @blocks(length, BLOCK)
    def _(rows):
        around = pl.ds(pl.multiple_of(rows.start, BLOCK), BLOCK + 16)
        near = spread[around, :]
        passed = gated[around, :]
        here = near[8 : 8 + BLOCK]
        grad = jnp.zeros((BLOCK, width), F32)
        for t in range(taps.shape[0]):
            grad = grad + taps[t : t + 1, :] * near[10 - t : 10 - t + BLOCK]
            product = here * passed[6 + t : 6 + t + BLOCK]
            sums[12 + t] += jnp.sum(product.reshape(-1, 8, width), axis=0)
        live = lax.broadcasted_iota(jnp.int32, (BLOCK, width), 0) + rows.start
        grad = jnp.where(live.astype(F32) < live_count, grad, 0.0)
        opened = sigmoid(gates[1, rows, :].astype(F32))
        du[0, rows, :] = (grad * opened).astype(BF16)
        du[1, rows, :] = (grad * gates[0, rows, :].astype(F32) * opened * (1.0 - opened)).astype(BF16)

    arrived("x2")
    spent(8.0)
    block_norm(0, 2)
    for p in range(2):
        emit(act, du.at[p])
        times_matrix(du.at[p], into_total(p))
    block_norm_back(0, 2, 1.0)

    qkv, heads_grad, sides = r.qkv_here, act, r.sides
    arrived("attended", "qkv")
    emit(r.attended_here, low)

    def take(columns, value):
        heads_grad[:, columns] = value.astype(BF16)

    times_matrix(low, take)
    for h in range(heads):
        columns = pl.ds(h * head_dim, head_dim)
        sides[...] = jnp.zeros(sides.shape, F32)

        @blocks(length, QUERIES)
        def _(rows, h=h, columns=columns):
            q, k, v = qkv[0, rows, columns], qkv[1, :, columns], qkv[2, :, columns]
            do = heads_grad[rows, columns]
            scores, distance = score_block(q, k, slope[h : h + 1, :], rows.start, live_count)
            prob = softmax_block(scores)
            dp = times_t(do, v)
            exact = prob * (dp - jnp.sum(prob * dp, axis=-1, keepdims=True))
            sums[17 + h, :, 0:length] -= jnp.sum((exact * distance).reshape(-1, 8, length), axis=0)
            ds = exact.astype(BF16)
            scale = head_dim**-0.5
            du[0, rows, columns] = (jnp.dot(ds, k, preferred_element_type=F32) * scale).astype(BF16)
            sides[0] += t_times(ds, q) * scale
            sides[1] += t_times(prob.astype(BF16), do)

        du[1, :, columns] = sides[0].astype(BF16)
        du[2, :, columns] = sides[1].astype(BF16)
        spent(6.0)
    arrived("x1")
    block_norm(1, 1)
    for p in range(3):
        emit(act, du.at[p])
        times_matrix(du.at[p], into_total(p))
    block_norm_back(1, 1, 0.5)
    arrived("h0")

    def after_one():
        @blocks(length, BLOCK)
        def _(rows):
            value = frame_block(r.h0_here, rows).astype(F32)
            act[rows, :] = normalise(value, norm, 0).astype(BF16)
            grad = dx[rows, :] + norm_back(value, total[rows, :], norm, 0, sums)
            spot = pl.ds(pl.multiple_of(lax.rem(rows.start, 64), BLOCK), BLOCK)
            r.cot_here[rows.start // 64, spot, :] = grad.astype(BF16)

        for i in range(17):
            r.wide[i : i + 1, :] = jnp.sum(sums[i], axis=0, keepdims=True)
        for h in range(heads):
            whole = jnp.sum(jnp.sum(sums[17 + h], axis=0, keepdims=True), axis=1, keepdims=True)
            r.wide[17 + h : 18 + h, :] = jnp.broadcast_to(whole, (1, width))
        r.wide[17 + heads : 32, :] = jnp.zeros((15 - heads, width), F32)
        r.small[...] = r.wide[...].astype(BF16)
        for j in range(8):
            swap_start(1, j)
            swap_start(2, j)

    feed_forward_back("u1", "s1", after_one)
    while ticks[0] < last + 6:
        tick()
    for i in range(3):
        swap_wait(i)

    @pl.when(other)
    def _():
        for u in range(last):
            far_copy(u, 0).wait_recv()
            far_copy(u, 1).wait_recv()


def backward(made, fulls, norm, taps, slope, collective_id):
    width = norm.shape[-1]
    length = made.x4_out.shape[0]
    blocked = (8, length // 8, width)
    shapes = [(f.shape[0] // 8, f.shape[1]) for f in fulls]
    count = len(fulls)
    units = [
        (index, row, column)
        for index in BACK_ORDER
        for row in range(0, shapes[index][0], ROWS)
        for column in range(0, shapes[index][1], COLUMNS)
    ]
    number = len(units)
    dma = pltpu.SemaphoreType.DMA
    given = dict(
        cot=made.cot_out,
        h0=made.h0_out,
        u1=made.u1_out,
        x1=made.x1_out,
        qkv=made.qkv_out,
        attended=made.attended_out,
        x2=made.x2_out,
        gates=made.gates_out,
        gated=made.gated_out,
        depth=made.depth_out,
        x3=made.x3_out,
        u2=made.u2_out,
        s1=made.s1_out,
        s2=made.s2_out,
        x4=made.x4_out,
        result=made.result_out.reshape(blocked),
        lens=made.lens_out,
    )
    outs = dict(
        result_home=jax.ShapeDtypeStruct(blocked, BF16),
        dframes_home=jax.ShapeDtypeStruct(blocked, BF16),
        small_home=jax.ShapeDtypeStruct((8, 32, width), BF16),
    )
    scratch = dict(
        xs=pltpu.VMEM((2, length, width), F32),
        dx=pltpu.VMEM((length, width), F32),
        total=pltpu.VMEM((length, width), F32),
        low=pltpu.VMEM((length, width), BF16),
        act=pltpu.VMEM((length, width), BF16),
        up=pltpu.VMEM((4, length, width), BF16),
        du=pltpu.VMEM((4, length, width), BF16),
        hidden=pltpu.VMEM((4, length, width), BF16),
        cot_here=pltpu.VMEM(blocked, BF16),
        h0_here=pltpu.VMEM(blocked, BF16),
        depth_here=pltpu.VMEM((length, width), F32),
        gates_here=pltpu.VMEM((2, length, width), BF16),
        gated_here=pltpu.VMEM((length + 16, width), F32),
        spread=pltpu.VMEM((length + 16, width), F32),
        qkv_here=pltpu.VMEM((3, length, width), BF16),
        attended_here=pltpu.VMEM((length, width), BF16),
        sides=pltpu.VMEM((2, length, width // slope.shape[0]), F32),
        lens_here=pltpu.VMEM(made.lens_out.shape, F32),
        sums=pltpu.VMEM((17 + slope.shape[0], 8, width), F32),
        wide=pltpu.VMEM((32, width), F32),
        small=pltpu.VMEM((32, width), BF16),
        unit=pltpu.VMEM((2, 4, 256, 1024), BF16),
        stage=pltpu.VMEM((2, 4, 2, ROWS, COLUMNS), BF16),
        mine=pltpu.VMEM((SLOTS, 4, 2, HALF, COLUMNS), BF16),
        core_in=pltpu.VMEM((2, 4, 2, HALF, COLUMNS), BF16),
        first_in=pltpu.VMEM((SLOTS, 4, HALF, COLUMNS), BF16),
        second_in=pltpu.VMEM((SLOTS, 2, HALF, COLUMNS), BF16),
        s_unit=dma((2, 4)),
        s_stage=dma((2,)),
        s_fetch=dma((32,)),
        swap_send=dma((3, 8)),
        swap_recv=dma((3, 8)),
        swap_own=dma((3,)),
        s_load=dma((2,)),
        s_core=dma((2,)),
        r_core=dma((2,)),
        s_first=dma((SLOTS, 2)),
        r_first=dma((SLOTS, 2)),
        s_second=dma((SLOTS, 2)),
        r_second=dma((SLOTS, 2)),
        s_far=dma((2,)),
        r_far=dma((number, 2)),
        s_near=dma((2,)),
        r_near=dma((number,)),
        s_own=dma((2,)),
    )
    vmem = pl.BlockSpec(memory_space=pltpu.VMEM)
    operands = dict(given, norm=norm, taps=taps, slope=slope)

    def body(*refs):
        refs = list(refs)
        cut = lambda n: [refs.pop(0) for _ in range(n)]
        plain, full_refs, made_refs = cut(len(operands)), cut(count), cut(len(outs))
        out_refs, grad_refs = cut(count), cut(count)
        backward_kernel(
            units,
            list(operands) + list(outs) + list(scratch) + ["fulls", "outs", "grads"],
            *plain,
            *made_refs,
            *refs,
            full_refs,
            out_refs,
            grad_refs,
        )

    results = pl.pallas_call(
        body,
        out_shape=list(outs.values())
        + [jax.ShapeDtypeStruct(s, BF16) for s in shapes]
        + [jax.ShapeDtypeStruct((4, 2) + s, BF16) for s in shapes],
        in_specs=[ANY] * len(given) + [vmem] * 3 + [ANY] * count,
        out_specs=[ANY] * (len(outs) + 2 * count),
        scratch_shapes=list(scratch.values()),
        compiler_params=pltpu.CompilerParams(
            collective_id=collective_id, has_side_effects=True, vmem_limit_bytes=62 * 2**20
        ),
    )(*operands.values(), *fulls)
    return results[: len(outs)], results[len(outs) : len(outs) + count]


def per_device(
    frames_in,
    noise,
    lengths,
    span_starts,
    w_in1,
    w_out1,
    w_qkv,
    w_attn,
    w_point1,
    w_point2,
    w_in2,
    w_out2,
    norm_params,
    kernel,
    slopes,
    cotangent,
):
    utterances, frames, width = frames_in.shape
    heads = slopes.shape[0]
    length = frames * 8
    frame_pos = lax.axis_index("seq") * frames + jnp.arange(frames, dtype=jnp.int32)
    span_begin = span_starts[:, :, None]
    masked = jnp.any(
        (span_begin <= frame_pos[None, None, :]) & (frame_pos[None, None, :] < span_begin + SPAN),
        axis=1,
    )
    start = jnp.where(masked[..., None], noise, frames_in)
    lens = jnp.broadcast_to(lengths.astype(F32)[:, None, None], (utterances, 8, 128))
    slope_rows = jnp.broadcast_to(slopes[:, None], (heads, length))
    shards = (w_in1, w_out1, w_qkv, w_attn, w_point1, w_point2, w_in2, w_out2)
    made, fulls = forward(start, lens, cotangent, norm_params, kernel, slope_rows, shards, 0)
    (block_out, dframes, small), grads = backward(made, fulls, norm_params, kernel, slope_rows, 1)
    small = jnp.sum(small.astype(F32), axis=0)
    grad_frames = jnp.where(masked[..., None], 0.0, dframes.astype(F32))
    return (
        block_out,
        grad_frames,
        *[grad.astype(F32) for grad in grads],
        small[:12].reshape(6, 2, width),
        small[12:17],
        small[17 : 17 + heads, 0],
    )


def solution(mesh):
    in_specs = (
        P("dp", "seq", None),
        P("dp", "seq", None),
        P("dp"),
        P("dp", None),
        P("seq", None),
        P("seq", None),
        P("seq", None),
        P("seq", None),
        P("seq", None),
        P("seq", None),
        P("seq", None),
        P("seq", None),
        P(),
        P(),
        P(),
        P("dp", "seq", None),
    )
    out_specs = (
        P("dp", "seq", None),
        P("dp", "seq", None),
        P(("dp", "seq"), None),
        P(("dp", "seq"), None),
        P(("dp", "seq"), None),
        P(("dp", "seq"), None),
        P(("dp", "seq"), None),
        P(("dp", "seq"), None),
        P(("dp", "seq"), None),
        P(("dp", "seq"), None),
        P("dp", None, None),
        P("dp", None),
        P("dp"),
    )
    grouped = mesh.shape["seq"] == 8 and mesh.shape["dp"] == 4
    return jax.shard_map(
        per_device if grouped else per_device_any, mesh=mesh, in_specs=in_specs, out_specs=out_specs, check_vma=False
    )
```
